32 devices in a mesh: shard: 32 (over z, y, x, core).
Axes of the slice: x: 2, y: 2, z: 4, core: 2. Of those that a mesh axis runs over, the one named last changes fastest.
Arguments:
- queries: bfloat16 [512, 8, 9600], P('shard'), may hold values from -6 to 6
- index_videos: bfloat16 [4096, 8, 9600], P('shard'), may hold values from -6 to 6
- candidates: int32 [512, 8], P('shard'), may hold values from 0 to 4095, as said below
- conv_one: bfloat16 [32, 1, 3, 3], replicated, may hold values from -2 to 2
- conv_two: bfloat16 [64, 32, 3, 3], replicated, may hold values from -0.375 to 0.375
- conv_three: bfloat16 [1, 64, 3, 3], replicated, may hold values from -0.25 to 0.25
Outputs:
- scores: float32 [512, 8], P('shard')
The draws below stay inside these ranges and needn't reach their ends.
Inputs may be any that keep to these rules, and one draw needn't show every extreme that they name: `candidates`: each new video's 8 ids are distinct. The videos of id v are held by device v // 128. Of one device's pairs at most 8 name videos of one holder; in every draw some holders receive exactly 8 from every device.
All inputs are finite; a program needn't handle non-finite values.
Results may differ from the reference program's by a relative error of at most 0.0041.
Values may be sent and summed in bfloat16 or wider, within the bound.
No kernel may reach another device: no remote copies, remote signals or barrier semaphores. Data moves between devices by JAX's collectives and lax.ppermute only.
A program may use at most 256 MiB of HBM per device.

```python
import math
import jax
import jax.numpy as jnp
from jax import lax

F = 8
R = 5
REGION_FEATURES = 1920
C1 = 32
C2 = 64
K = 8
Q_DEV = 16
IDX_DEV = 128
QUERIES = 512
VIDEOS = 4096


def draw_candidates(key, part):
    devices = QUERIES // Q_DEV
    pairs = Q_DEV * K
    cap = max(2, (2 * pairs + devices - 1) // devices)
    hot_count = max(1, devices // 16)
    order = jax.random.permutation(jax.random.fold_in(key, 7), devices)
    hot = order[:hot_count]
    cold = order[hot_count:]
    cold_count = devices - hot_count

    def one_device(device):
        dkey = jax.random.fold_in(key, 1000 + device)
        cold_perm = cold[jax.random.permutation(jax.random.fold_in(dkey, 1), cold_count)]
        owners = jnp.concatenate([jnp.repeat(hot, cap), jnp.tile(cold_perm, cap)])[:pairs]
        ranks = jnp.concatenate([jnp.tile(jnp.arange(cap), hot_count), jnp.repeat(jnp.arange(cap), cold_count)])[:pairs]
        base = jax.random.randint(jax.random.fold_in(dkey, 2), (devices,), 0, IDX_DEV)
        slots = (base[owners] + ranks) % IDX_DEV
        ids = owners * IDX_DEV + slots
        shuffled = ids[jax.random.permutation(jax.random.fold_in(dkey, 3), pairs)]
        return shuffled.reshape(Q_DEV, K)
    return jax.vmap(one_device)(jnp.arange(devices)).reshape(QUERIES, K).astype(jnp.int32)


def level_of(own_key, shape, pieces, least, high):
    gain = 1.0
    for position, parts in pieces:
        steps = jax.random.uniform(jax.random.fold_in(jax.random.fold_in(own_key, 6), position), (parts,), jnp.float32, least / len(pieces), high / len(pieces))
        gain = gain * jnp.repeat(jnp.exp(steps), shape[position] // parts).reshape((-1,) + (1,) * (len(shape) - 1 - position))
    return gain


def bell_draw(own_key, extent, width, limit, split=(), kind=jnp.bfloat16):
    values = jax.random.normal(own_key, extent, jnp.float32) * width
    if len(split) > 0:
        values = level_of(own_key, extent, split, -0.22, 0.18) * values
    return jnp.clip(values, min=-limit, max=limit).astype(kind)


def setup_inputs(seed: int = 0) -> dict:
    arg_keys = jax.random.split(jax.random.key(seed), 7)
    queries = bell_draw(arg_keys[0], (QUERIES, F, R * REGION_FEATURES), 1.0, 6.0, ((0, 32),))
    index_videos = bell_draw(arg_keys[1], (VIDEOS, F, R * REGION_FEATURES), 1.0, 6.0, ((0, 32),))
    candidates = draw_candidates(jax.random.fold_in(arg_keys[6], 71), 0)
    conv_one = bell_draw(arg_keys[3], (C1, 1, 3, 3), 9 ** -0.5, 2.0)
    conv_two = bell_draw(arg_keys[4], (C2, C1, 3, 3), (9 * C1) ** -0.5, 0.375)
    conv_three = bell_draw(arg_keys[5], (1, C2, 3, 3), (9 * C2) ** -0.5, 0.25)
    return dict(queries=queries, index_videos=index_videos, candidates=candidates, conv_one=conv_one, conv_two=conv_two, conv_three=conv_three)


def conv_same(x, w):
    return lax.conv_general_dilated(x.astype(jnp.float32), w.astype(jnp.float32), (1, 1), 'SAME', dimension_numbers=('NCHW', 'OIHW', 'NCHW'))

def pool_two(x):
    b, c, h, w = x.shape
    return lax.optimization_barrier(jnp.max(x.reshape(b, c, h // 2, 2, w // 2, 2), axis=(3, 5)))

def pair_scores(left, right, conv_one, conv_two, conv_three):
    count = left.shape[0]
    left_frame_features = left.astype(jnp.float32).reshape(count, F * R, REGION_FEATURES)
    right_frame_features = right.astype(jnp.float32).reshape(count, F * R, REGION_FEATURES)
    region_similarities = jnp.einsum('avs,afs->avf', left_frame_features, right_frame_features) * (1.0 / math.sqrt(REGION_FEATURES))
    region_similarities = region_similarities.reshape(count, F, R, F, R)
    frame_map = lax.optimization_barrier(jnp.mean(lax.optimization_barrier(jnp.max(region_similarities, axis=4)), axis=2)).astype(jnp.bfloat16)
    first = pool_two(jax.nn.relu(conv_same(frame_map[:, None], conv_one))).astype(jnp.bfloat16)
    second = pool_two(jax.nn.relu(conv_same(first, conv_two))).astype(jnp.bfloat16)
    final = conv_same(second, conv_three)[:, 0]
    return lax.optimization_barrier(jnp.mean(lax.optimization_barrier(jnp.max(jnp.clip(final, -1.0, 1.0), axis=2)), axis=1))

def reference(queries, index_videos, candidates, conv_one, conv_two, conv_three):
    total = QUERIES * K
    flat = candidates.reshape(total)
    owner_query = (jnp.arange(total) // K).astype(jnp.int32)
    block = 64

    def one_block(i):
        start = (i * block).astype(jnp.int32)
        ids = lax.dynamic_slice_in_dim(flat, start, block)
        rows = lax.dynamic_slice_in_dim(owner_query, start, block)
        return pair_scores(queries[rows], index_videos[ids], conv_one, conv_two, conv_three)
    result = lax.map(one_block, jnp.arange(total // block, dtype=jnp.int32))
    return result.reshape(QUERIES, K)
```

```python
import functools
import math

import jax
import jax.numpy as jnp
import numpy as np
from jax import lax
from jax.experimental import pallas as pl
from jax.experimental.pallas import tpu as pltpu
from jax.sharding import PartitionSpec as P

R = 5
GROUP = 16
NONE = 1 << 30


def shifts(size):
    k, i, y = np.meshgrid(np.arange(3), np.arange(size), np.arange(size), indexing="ij")
    return (i == y + k - 1).astype(np.float32)


def conv_matrix(w, size):
    s = jnp.asarray(shifts(size), jnp.bfloat16)
    half = jnp.einsum("ockl,kiy->oclyi", w, s, preferred_element_type=jnp.float32).astype(jnp.bfloat16)
    full = jnp.einsum("oclyi,ljx->cijoyx", half, s, preferred_element_type=jnp.float32)
    return full.astype(jnp.bfloat16)


def pooled_matrix(w, size):
    m = conv_matrix(w, size)
    c, _, _, o, _, _ = m.shape
    m = m.reshape(c, size, size, o, size // 2, 2, size // 2, 2)
    m = m.transpose(0, 1, 2, 5, 7, 3, 4, 6)
    return m.reshape(c * size * size, o * size * size)


def head_matrices(conv_one, conv_two, conv_three):
    one = pooled_matrix(conv_one, 8)
    two = pooled_matrix(conv_two, 4)
    three = conv_matrix(conv_three, 2)[:, :, :, 0]
    c = three.shape[0]
    three = jnp.swapaxes(three.reshape(c * 4, 2, 2), 1, 2)
    three = jnp.pad(three, ((0, 0), (0, 0), (0, 126))).reshape(c * 4, 256)
    return one, two, three


def dot(a, b):
    return jnp.dot(a, b, preferred_element_type=jnp.float32)


def pair_kernel(frames, senders, group, scale, rows_ref, vids_ref, count_ref, entry_ref,
                one_ref, two_ref, three_ref, q_hbm, own_hbm, other_hbm, out_ref,
                q_in, v_in, q_rows, v_rows, maps, q_sem, v_sem):
    idx_dev = own_hbm.shape[0]
    width = q_hbm.shape[2] // R
    side = group * frames
    count = count_ref[0]
    groups = (count + group - 1) // group

    def fetch(step, slot):
        def one_pair(p, _):
            row = rows_ref[step * group + p]
            vid = vids_ref[step * group + p]
            pltpu.make_async_copy(q_hbm.at[row], q_in.at[slot, p], q_sem.at[slot]).start()

            @pl.when(vid < idx_dev)
            def _():
                pltpu.make_async_copy(own_hbm.at[vid], v_in.at[slot, p], v_sem.at[slot]).start()

            @pl.when(vid >= idx_dev)
            def _():
                pltpu.make_async_copy(
                    other_hbm.at[vid - idx_dev], v_in.at[slot, p], v_sem.at[slot]
                ).start()
            return 0
        lax.fori_loop(0, group, one_pair, 0)

    row_id = lax.broadcasted_iota(jnp.int32, (side, side), 0)
    col_id = lax.broadcasted_iota(jnp.int32, (side, side), 1)
    same_pair = row_id // frames == col_id // frames
    cells = frames * frames
    lane = lax.broadcasted_iota(jnp.int32, (side, cells), 1)
    sub = lax.broadcasted_iota(jnp.int32, (side, cells), 0)
    spread = (lane % frames == sub % frames).astype(jnp.bfloat16)
    own_frame = lane // frames == sub % frames
    fold = (
        lax.broadcasted_iota(jnp.int32, (group, side), 1) // frames
        == lax.broadcasted_iota(jnp.int32, (group, side), 0)
    ).astype(jnp.bfloat16)

    maps[...] = jnp.zeros_like(maps)

    @pl.when(groups > 0)
    def _():
        fetch(0, 0)

    def step(g, _):
        slot = lax.rem(g, 2)

        @pl.when(g + 1 < groups)
        def _():
            fetch(g + 1, 1 - slot)

        pltpu.make_async_copy(q_in.at[slot], q_in.at[slot], q_sem.at[slot]).wait()
        pltpu.make_async_copy(v_in.at[slot], v_in.at[slot], v_sem.at[slot]).wait()
        for r in range(R):
            cols = pl.ds(r * width, width)
            q_rows[pl.ds(r * side, side), :] = q_in[slot, :, :, cols].reshape(side, width)
            v_rows[pl.ds(r * side, side), :] = v_in[slot, :, :, cols].reshape(side, width)
        total = jnp.zeros((side, side), jnp.float32)
        for r in range(R):
            sim = lax.dot_general(
                q_rows[pl.ds(r * side, side), :], v_rows[...], (((1,), (1,)), ((), ())),
                preferred_element_type=jnp.float32,
            )
            best = sim[:, :side]
            for s in range(1, R):
                best = jnp.maximum(best, sim[:, s * side:(s + 1) * side])
            total = total + best
        mean = jnp.where(same_pair, total * scale, 0.0).astype(jnp.bfloat16)
        wide = jnp.where(own_frame, dot(mean, spread), 0.0).astype(jnp.bfloat16)
        maps[pl.ds(pl.multiple_of(g * group, group), group), :] = dot(fold, wide)
        return 0

    lax.fori_loop(0, groups, step, 0)

    def pooled(x, parts):
        n = x.shape[1] // parts
        best = x[:, :n]
        for i in range(1, parts):
            best = jnp.maximum(best, x[:, i * n:(i + 1) * n])
        return jnp.maximum(best, 0.0).astype(jnp.bfloat16)

    first = pooled(dot(maps[...].astype(jnp.bfloat16), one_ref[...]), 4)
    second = pooled(dot(first, two_ref[...]), 4)
    final = jnp.clip(dot(second, three_ref[...]), -1.0, 1.0)
    best = jnp.maximum(final[:, :128], final[:, 128:])
    score = (best[:, 0:1] + best[:, 1:2]) * 0.5
    pairs = out_ref.shape[1]
    place = lax.broadcasted_iota(jnp.int32, (score.shape[0], pairs), 1)
    for s in range(senders):
        hit = entry_ref[...] == place + s * pairs
        out_ref[pl.ds(s, 1), :] = jnp.sum(jnp.where(hit, score, 0.0), axis=0, keepdims=True)


def pair_scores(gathered, own, other, rows, vids, count, entry, heads, senders, pairs):
    frames, width = gathered.shape[1], gathered.shape[2]
    cap = rows.shape[0]
    side = GROUP * frames
    scale = 1.0 / (math.sqrt(width // R) * R)
    smem = pl.BlockSpec(memory_space=pltpu.SMEM)
    vmem = pl.BlockSpec(memory_space=pltpu.VMEM)
    hbm = pl.BlockSpec(memory_space=pl.ANY)
    return pl.pallas_call(
        functools.partial(pair_kernel, frames, senders, GROUP, scale),
        out_shape=jax.ShapeDtypeStruct((senders, pairs), jnp.float32),
        in_specs=[smem, smem, smem, vmem, vmem, vmem, vmem, hbm, hbm, hbm],
        out_specs=vmem,
        scratch_shapes=[
            pltpu.VMEM((2, GROUP, frames, width), jnp.bfloat16),
            pltpu.VMEM((2, GROUP, frames, width), jnp.bfloat16),
            pltpu.VMEM((R * side, width // R), jnp.bfloat16),
            pltpu.VMEM((R * side, width // R), jnp.bfloat16),
            pltpu.VMEM((cap, frames * frames), jnp.float32),
            pltpu.SemaphoreType.DMA((2,)),
            pltpu.SemaphoreType.DMA((2,)),
        ],
        compiler_params=pltpu.CompilerParams(vmem_limit_bytes=48 * 1024 * 1024),
        cost_estimate=pl.CostEstimate(
            flops=2 * cap * side * R * R * frames * (width // R),
            bytes_accessed=cap * frames * width * 4, transcendentals=0,
        ),
        name="pair_scores",
    )(rows, vids, count, entry, *heads, gathered, own, other)


def body(queries, index_videos, candidates, conv_one, conv_two, conv_three):
    devices = lax.axis_size("shard")
    q_dev, frames, width = queries.shape
    k_count = candidates.shape[1]
    idx_dev = index_videos.shape[0]
    pairs = q_dev * k_count
    chips = devices // 2
    per_holder = max(2, (2 * pairs + devices - 1) // devices)
    cap = chips * 2 * per_holder
    me = lax.axis_index("shard")
    chip, core = me // 2, me % 2
    same_core = [[2 * i + c for i in range(chips)] for c in range(2)]

    ids = lax.all_gather(
        candidates.reshape(1, pairs), "shard", axis=0, tiled=True, axis_index_groups=same_core
    )
    gathered = lax.all_gather(
        queries, "shard", axis=0, tiled=True, axis_index_groups=same_core
    )
    other = lax.ppermute(index_videos, "shard", [(d, d ^ 1) for d in range(devices)])

    flat = ids.reshape(chips * pairs)
    mine = flat // (2 * idx_dev) == chip
    local = flat % (2 * idx_dev)
    local = jnp.where(local // idx_dev == core, local % idx_dev, local % idx_dev + idx_dev)
    entry = jnp.arange(chips * pairs, dtype=jnp.int32)
    code = jnp.where(mine, entry * (2 * idx_dev) + local, NONE)
    code = jnp.sort(code)[:cap]
    count = jnp.sum(mine.astype(jnp.int32)).reshape(1)
    valid = code < NONE
    entry = jnp.where(valid, code // (2 * idx_dev), NONE)
    rows = jnp.where(valid, entry // k_count, 0)
    vids = jnp.where(valid, code % (2 * idx_dev), 0)

    heads = head_matrices(conv_one, conv_two, conv_three)
    table = pair_scores(
        gathered, index_videos, other, rows, vids, count, entry.reshape(cap, 1), heads, chips, pairs
    )
    back = lax.all_to_all(
        table, "shard", split_axis=0, concat_axis=0, tiled=True, axis_index_groups=same_core
    )
    return jnp.sum(back, axis=0).reshape(q_dev, k_count)


def solution(mesh):
    placed = (P("shard", None, None), P("shard", None, None), P("shard", None), P(), P(), P())
    return jax.shard_map(
        body, mesh=mesh, in_specs=placed, out_specs=P("shard", None), check_vma=False
    )
```

```python
import functools
import math

import jax
import jax.numpy as jnp
import numpy as np
from jax import lax
from jax.experimental import pallas as pl
from jax.experimental.pallas import tpu as pltpu
from jax.sharding import PartitionSpec as P

R = 5
GROUP = 16
NONE = 1 << 30
ROUTES = (("zxy", 8), ("zyx", 8))


def dot(a, b):
    return jnp.dot(a, b, preferred_element_type=jnp.float32)


def iota(shape, dim):
    return lax.broadcasted_iota(jnp.int32, shape, dim)


def head_kernel(one_w, two_w, three_w, one_ref, two_ref, three_ref, one_acc, two_acc, three_acc):
    one_acc[...] = jnp.zeros_like(one_acc)
    two_acc[...] = jnp.zeros_like(two_acc)
    three_acc[...] = jnp.zeros_like(three_acc)
    c1, c2 = two_w.shape[1], two_w.shape[2]
    b1, b2 = c1.bit_length() - 1, c2.bit_length() - 1

    def tap(t, _):
        k = lax.div(t, 3) - 1
        l = lax.rem(t, 3) - 1

        n = one_acc.shape[1]
        row, col = iota((64, n), 0), iota((64, n), 1) >> b1
        y = ((col >> 2) & 3) * 2 + ((col >> 5) & 1)
        x = (col & 3) * 2 + ((col >> 4) & 1)
        hit = ((row >> 3) == y + k) & ((row & 7) == x + l)
        spread = ((iota((c1, n), 1) & (c1 - 1)) == iota((c1, n), 0)).astype(jnp.bfloat16)
        val = dot(jnp.broadcast_to(one_w[t], (16, c1)), spread)[:1]
        one_acc[...] = jnp.where(hit, val, one_acc[...])

        n = two_acc.shape[1]
        spread = ((iota((c2, n), 1) & (c2 - 1)) == iota((c2, n), 0)).astype(jnp.bfloat16)
        val = dot(two_w[t], spread)

        def cell(ij, _):
            col = iota((c1, n), 1) >> b2
            y = ((col >> 1) & 1) * 2 + ((col >> 3) & 1)
            x = (col & 1) * 2 + ((col >> 2) & 1)
            hit = (lax.div(ij, 4) == y + k) & (lax.rem(ij, 4) == x + l)
            rows = pl.ds(pl.multiple_of(ij * c1, c1), c1)
            two_acc[rows, :] = jnp.where(hit, val, two_acc[rows, :])
            return 0
        lax.fori_loop(0, 16, cell, 0)

        m, n = three_acc.shape
        pick = ((iota((m, c2), 0) & (c2 - 1)) == iota((m, c2), 1)).astype(jnp.bfloat16)
        val = lax.dot_general(
            pick, jnp.broadcast_to(three_w[t], (128, c2)), (((1,), (1,)), ((), ())),
            preferred_element_type=jnp.float32,
        )[:, :1]
        row, col = iota((m, n), 0) >> b2, iota((m, n), 1)
        y, x = col & 127, col >> 7
        hit = ((row >> 1) == y + k) & ((row & 1) == x + l) & (y < 2)
        three_acc[...] = jnp.where(hit, val, three_acc[...])
        return 0

    lax.fori_loop(0, 9, tap, 0)
    one_ref[...] = one_acc[...].astype(jnp.bfloat16)
    two_ref[...] = two_acc[...].astype(jnp.bfloat16)
    three_ref[...] = three_acc[...].astype(jnp.bfloat16)


def head_matrices(conv_one, conv_two, conv_three):
    c1, c2 = conv_two.shape[1], conv_two.shape[0]
    one_w = conv_one.transpose(2, 3, 1, 0).reshape(9, 1, c1)
    two_w = conv_two.transpose(2, 3, 1, 0).reshape(9, c1, c2)
    three_w = conv_three.transpose(2, 3, 0, 1).reshape(9, 1, c2)
    shapes = [(64, 64 * c1), (16 * c1, 16 * c2), (4 * c2, 256)]
    vmem = pl.BlockSpec(memory_space=pltpu.VMEM)
    return pl.pallas_call(
        head_kernel,
        out_shape=[jax.ShapeDtypeStruct(s, jnp.bfloat16) for s in shapes],
        in_specs=[vmem] * 3,
        out_specs=[vmem] * 3,
        scratch_shapes=[pltpu.VMEM(s, jnp.float32) for s in shapes],
        compiler_params=pltpu.CompilerParams(vmem_limit_bytes=24 * 1024 * 1024),
        cost_estimate=pl.CostEstimate(flops=10**9, bytes_accessed=3 * 10**6, transcendentals=0),
        name="head_matrices",
    )(one_w, two_w, three_w)


def pair_kernel(frames, buffers, q_dev, scale, rows_ref, vids_ref, count_ref, entry_ref, one_ref,
                two_ref, three_ref, before_ref, own_hbm, other_hbm, *rest):
    q_hbm, rest = rest[:buffers], rest[buffers:]
    out_ref, q_in, v_in, q_rows, v_rows, maps, q_sem, v_sem = rest
    idx_dev = own_hbm.shape[0]
    width = own_hbm.shape[2] // R
    side = GROUP * frames
    count = count_ref[0]
    groups = (count + GROUP - 1) // GROUP

    def fetch(step, slot):
        def one_pair(p, _):
            row = rows_ref[step * GROUP + p]
            vid = vids_ref[step * GROUP + p]
            buf, row = lax.div(row, q_dev), lax.rem(row, q_dev)
            for b in range(buffers):
                @pl.when(buf == b)
                def _():
                    pltpu.make_async_copy(
                        q_hbm[b].at[row], q_in.at[slot, p], q_sem.at[slot]
                    ).start()

            @pl.when(vid < idx_dev)
            def _():
                pltpu.make_async_copy(own_hbm.at[vid], v_in.at[slot, p], v_sem.at[slot]).start()

            @pl.when(vid >= idx_dev)
            def _():
                pltpu.make_async_copy(
                    other_hbm.at[vid - idx_dev], v_in.at[slot, p], v_sem.at[slot]
                ).start()
            return 0
        lax.fori_loop(0, GROUP, one_pair, 0)

    maps[...] = jnp.zeros_like(maps)

    @pl.when(groups > 0)
    def _():
        fetch(0, 0)

    def step(g, _):
        slot = lax.rem(g, 2)

        @pl.when(g + 1 < groups)
        def _():
            fetch(g + 1, 1 - slot)

        pltpu.make_async_copy(q_in.at[slot], q_in.at[slot], q_sem.at[slot]).wait()
        pltpu.make_async_copy(v_in.at[slot], v_in.at[slot], v_sem.at[slot]).wait()
        for r in range(R):
            cols = pl.ds(r * width, width)
            q_rows[pl.ds(r * side, side), :] = q_in[slot, :, :, cols].reshape(side, width)
            v_rows[pl.ds(r * side, side), :] = v_in[slot, :, :, cols].reshape(side, width)

        def region(r, total):
            sim = lax.dot_general(
                q_rows[pl.ds(pl.multiple_of(r * side, side), side), :], v_rows[...],
                (((1,), (1,)), ((), ())), preferred_element_type=jnp.float32,
            )
            best = sim[:, :side]
            for s in range(1, R):
                best = jnp.maximum(best, sim[:, s * side:(s + 1) * side])
            return total + best

        total = lax.fori_loop(0, R, region, jnp.zeros((side, side), jnp.float32))
        cells = frames * frames
        same_pair = iota((side, side), 0) // frames == iota((side, side), 1) // frames
        lane, sub = iota((side, cells), 1), iota((side, cells), 0)
        spread = (lane % frames == sub % frames).astype(jnp.bfloat16)
        own_frame = lane // frames == sub % frames
        fold = (iota((GROUP, side), 1) // frames == iota((GROUP, side), 0)).astype(jnp.bfloat16)
        mean = jnp.where(same_pair, total * scale, 0.0).astype(jnp.bfloat16)
        wide = jnp.where(own_frame, dot(mean, spread), 0.0).astype(jnp.bfloat16)
        maps[pl.ds(pl.multiple_of(g * GROUP, GROUP), GROUP), :] = dot(fold, wide)
        return 0

    lax.fori_loop(0, groups, step, 0)

    def pooled(x):
        n = x.shape[1] // 4
        best = x[:, :n]
        for i in range(1, 4):
            best = jnp.maximum(best, x[:, i * n:(i + 1) * n])
        return jnp.maximum(best, 0.0).astype(jnp.bfloat16)

    first = pooled(dot(maps[...].astype(jnp.bfloat16), one_ref[...]))
    second = pooled(dot(first, two_ref[...]))
    final = jnp.clip(dot(second, three_ref[...]), -1.0, 1.0)
    best = jnp.maximum(final[:, :128], final[:, 128:])
    score = (best[:, 0:1] + best[:, 1:2]) * 0.5
    senders, pairs = out_ref.shape
    shape = (score.shape[0], pairs)
    score = jnp.broadcast_to(score, shape)
    place = jnp.broadcast_to(entry_ref[...], shape) - iota(shape, 1)
    for s in range(senders):
        out_ref[pl.ds(s, 1), :] = before_ref[pl.ds(s, 1), :] + jnp.sum(
            jnp.where(place == s * pairs, score, 0.0), axis=0, keepdims=True
        )


def pair_scores(blocks, own, other, rows, vids, count, entry, heads, before, q_dev, name):
    frames, width = own.shape[1], own.shape[2]
    cap = rows.shape[0]
    side = GROUP * frames
    scale = 1.0 / (math.sqrt(width // R) * R)
    smem = pl.BlockSpec(memory_space=pltpu.SMEM)
    vmem = pl.BlockSpec(memory_space=pltpu.VMEM)
    hbm = pl.BlockSpec(memory_space=pl.ANY)
    return pl.pallas_call(
        functools.partial(pair_kernel, frames, len(blocks), q_dev, scale),
        out_shape=jax.ShapeDtypeStruct(before.shape, jnp.float32),
        in_specs=[smem] * 3 + [vmem] * 5 + [hbm] * (2 + len(blocks)),
        out_specs=vmem,
        scratch_shapes=[
            pltpu.VMEM((2, GROUP, frames, width), jnp.bfloat16),
            pltpu.VMEM((2, GROUP, frames, width), jnp.bfloat16),
            pltpu.VMEM((R * side, width // R), jnp.bfloat16),
            pltpu.VMEM((R * side, width // R), jnp.bfloat16),
            pltpu.VMEM((cap, frames * frames), jnp.float32),
            pltpu.SemaphoreType.DMA((2,)),
            pltpu.SemaphoreType.DMA((2,)),
        ],
        compiler_params=pltpu.CompilerParams(vmem_limit_bytes=40 * 1024 * 1024),
        cost_estimate=pl.CostEstimate(
            flops=2 * cap * side * R * R * frames * (width // R),
            bytes_accessed=cap * frames * width * 4, transcendentals=0,
        ),
        name=name,
    )(rows, vids, count, entry, *heads, before, own, other, *blocks)


def chip_places(mesh):
    devices = list(mesh.devices.flat)[::2]
    places = [tuple(getattr(d, "coords", ()) or ()) for d in devices]
    if any(len(p) != 3 for p in places):
        return [(i, 0, 0) for i in range(len(devices))]
    return [tuple(reversed(p)) for p in places]


def ring_position(coordinate, size):
    if size <= 2:
        return coordinate
    order = list(range(1, size, 2)) + list(reversed(range(0, size, 2)))
    order = [0] + [c for c in order if c != 0]
    return order.index(coordinate)


def body(places, sizes, queries, index_videos, candidates, conv_one, conv_two, conv_three):
    devices = lax.axis_size("shard")
    q_dev, frames, width = queries.shape
    k_count = candidates.shape[1]
    idx_dev = index_videos.shape[0]
    pairs = q_dev * k_count
    chips = devices // 2
    per_holder = max(2, (2 * pairs + devices - 1) // devices)
    me = lax.axis_index("shard")
    chip, core = me // 2, me % 2
    same_core = [[2 * i + c for i in range(chips)] for c in range(2)]

    rings = [tuple(ring_position(c, n) for c, n in zip(p, sizes)) for p in places]
    where = {r: i for i, r in enumerate(rings)}
    offsets = [(z, y, x) for z in range(sizes[0]) for y in range(sizes[1]) for x in range(sizes[2])]
    back = np.array(
        [[where[tuple((r - o) % n for r, o, n in zip(ring, off, sizes))] for off in offsets]
         for ring in rings], np.int32,
    )

    def step_along(axis):
        out = []
        for i, ring in enumerate(rings):
            to = list(ring)
            to[axis] = (to[axis] + 1) % sizes[axis]
            out += [(2 * i + c, 2 * where[tuple(to)] + c) for c in range(2)]
        return out

    steps = [step_along(a) for a in range(3)]

    ids = lax.all_gather(
        candidates.reshape(1, pairs), "shard", axis=0, tiled=True, axis_index_groups=same_core
    )
    other = lax.ppermute(index_videos, "shard", [(d, d ^ 1) for d in range(devices)])

    parts = sum(n for _, n in ROUTES)
    starts, blocks = [], []
    start = 0
    for order, share in ROUTES:
        n = q_dev * share // parts
        have = {(0, 0, 0): queries[start:start + n]}
        for letter in order:
            axis = "zyx".index(letter)
            for off, block in list(have.items()):
                for k in range(1, sizes[axis]):
                    block = lax.ppermute(block, "shard", steps[axis])
                    off = off[:axis] + (k,) + off[axis + 1:]
                    have[off] = block
        starts.append(start)
        blocks.append(have)
        start += n
    routes = len(ROUTES)

    plane = sizes[1] * sizes[2]
    offsets_of = [offsets[z * plane:(z + 1) * plane] for z in range(sizes[0])]
    phases = []
    for z in range(sizes[0]):
        every = [(i, r) for i in range(plane) for r in range(routes)]
        late = []
        if z == sizes[0] - 1 and sizes[0] > 1:
            late = [
                (i, r) for i, r in every
                if offsets_of[z][i]["zyx".index(ROUTES[r][0][-1])] == sizes["zyx".index(ROUTES[r][0][-1])] - 1
            ]
        phases.append((z, [e for e in every if e not in late]))
        if late:
            phases.append((z, late))

    senders = lax.dynamic_index_in_dim(jnp.asarray(back), chip, 0, keepdims=False)
    flat = jnp.take(ids, senders, axis=0).reshape(sizes[0], plane * pairs)
    flat = jnp.take(flat, np.array([z for z, _ in phases]), axis=0)
    pos = np.arange(plane * pairs, dtype=np.int32)
    pair = pos % pairs
    route = np.sum(np.array(starts)[None, :] <= (pair // k_count)[:, None], axis=1) - 1
    inside = np.array(
        [[(int(p) // pairs, int(r)) in set(chosen) for p, r in zip(pos, route)]
         for _, chosen in phases], bool,
    )
    mine = (flat // (2 * idx_dev) == chip) & inside
    local = flat % (2 * idx_dev)
    local = jnp.where(local // idx_dev == core, local % idx_dev, local % idx_dev + idx_dev)
    code = jnp.where(mine, pos[None, :] * (2 * idx_dev) + local, NONE)
    cap = min(plane * 2 * per_holder, plane * pairs)
    cap = -(-cap // GROUP) * GROUP
    code = jnp.sort(code, axis=1)[:, :cap]
    count = jnp.sum(mine.astype(jnp.int32), axis=1)
    valid = code < NONE
    place = jnp.where(valid, code // (2 * idx_dev), 0)
    vids = jnp.where(valid, code % (2 * idx_dev), 0)
    number, pair = place // pairs, place % pairs
    query = pair // k_count
    sender = jnp.zeros_like(place)
    by_phase = senders.reshape(sizes[0], plane)[np.array([z for z, _ in phases])]
    for i in range(plane):
        sender = jnp.where(number == i, by_phase[:, i:i + 1], sender)
    entry = jnp.where(valid, sender * pairs + pair, NONE)
    rows = jnp.zeros_like(place)
    for p, (_, chosen) in enumerate(phases):
        for b, (i, r) in enumerate(chosen):
            end = starts[r + 1] if r + 1 < routes else q_dev
            hit = (number[p] == i) & (query[p] >= starts[r]) & (query[p] < end)
            rows = rows.at[p].set(
                jnp.where(hit & valid[p], b * q_dev + query[p] - starts[r], rows[p])
            )

    heads = head_matrices(conv_one, conv_two, conv_three)
    table = jnp.zeros((chips, pairs), jnp.float32)
    for p, (z, chosen) in enumerate(phases):
        table = pair_scores(
            [blocks[r][offsets_of[z][i]] for i, r in chosen], index_videos, other, rows[p], vids[p],
            count[p:p + 1], entry[p].reshape(cap, 1), heads, table, q_dev, "phase_" + str(p),
        )
    scores = lax.all_to_all(
        table, "shard", split_axis=0, concat_axis=0, tiled=True, axis_index_groups=same_core
    )
    return jnp.sum(scores, axis=0).reshape(q_dev, k_count)


def solution(mesh):
    places = chip_places(mesh)
    low = [min(p[a] for p in places) for a in range(3)]
    places = [tuple(c - m for c, m in zip(p, low)) for p in places]
    sizes = [max(p[a] for p in places) + 1 for a in range(3)]
    placed = (P("shard", None, None), P("shard", None, None), P("shard", None), P(), P(), P())
    return jax.shard_map(
        functools.partial(body, places, sizes), mesh=mesh, in_specs=placed,
        out_specs=P("shard", None), check_vma=False,
    )
```

```python
import functools
import math

import jax
import jax.numpy as jnp
import numpy as np
from jax import lax
from jax.experimental import pallas as pl
from jax.experimental.pallas import tpu as pltpu
from jax.sharding import PartitionSpec as P

R = 5
GROUP = 16
NONE = 1 << 30
ROUTES = (("zxy", 6), ("zyx", 6), ("xyz", 2), ("yxz", 2))
PHASE_ENDS = (0.45, 0.7, 0.88, 1.0)
IN_FLIGHT = 2
SLACK = 2.0


def dot(a, b):
    return jnp.dot(a, b, preferred_element_type=jnp.float32)


def iota(shape, dim):
    return lax.broadcasted_iota(jnp.int32, shape, dim)


def head_kernel(one_w, two_w, three_w, one_ref, two_ref, three_ref, one_acc, two_acc, three_acc):
    one_acc[...] = jnp.zeros_like(one_acc)
    two_acc[...] = jnp.zeros_like(two_acc)
    three_acc[...] = jnp.zeros_like(three_acc)
    c1, c2 = two_w.shape[1], two_w.shape[2]
    b1, b2 = c1.bit_length() - 1, c2.bit_length() - 1

    def tap(t, _):
        k = lax.div(t, 3) - 1
        l = lax.rem(t, 3) - 1

        n = one_acc.shape[1]
        row, col = iota((64, n), 0), iota((64, n), 1) >> b1
        y = ((col >> 2) & 3) * 2 + ((col >> 5) & 1)
        x = (col & 3) * 2 + ((col >> 4) & 1)
        hit = ((row >> 3) == y + k) & ((row & 7) == x + l)
        spread = ((iota((c1, n), 1) & (c1 - 1)) == iota((c1, n), 0)).astype(jnp.bfloat16)
        val = dot(jnp.broadcast_to(one_w[t], (16, c1)), spread)[:1]
        one_acc[...] = jnp.where(hit, val, one_acc[...])

        n = two_acc.shape[1]
        spread = ((iota((c2, n), 1) & (c2 - 1)) == iota((c2, n), 0)).astype(jnp.bfloat16)
        val = dot(two_w[t], spread)

        def cell(ij, _):
            col = iota((c1, n), 1) >> b2
            y = ((col >> 1) & 1) * 2 + ((col >> 3) & 1)
            x = (col & 1) * 2 + ((col >> 2) & 1)
            hit = (lax.div(ij, 4) == y + k) & (lax.rem(ij, 4) == x + l)
            rows = pl.ds(pl.multiple_of(ij * c1, c1), c1)
            two_acc[rows, :] = jnp.where(hit, val, two_acc[rows, :])
            return 0
        lax.fori_loop(0, 16, cell, 0)

        m, n = three_acc.shape
        pick = ((iota((m, c2), 0) & (c2 - 1)) == iota((m, c2), 1)).astype(jnp.bfloat16)
        val = lax.dot_general(
            pick, jnp.broadcast_to(three_w[t], (128, c2)), (((1,), (1,)), ((), ())),
            preferred_element_type=jnp.float32,
        )[:, :1]
        row, col = iota((m, n), 0) >> b2, iota((m, n), 1)
        y, x = col & 127, col >> 7
        hit = ((row >> 1) == y + k) & ((row & 1) == x + l) & (y < 2)
        three_acc[...] = jnp.where(hit, val, three_acc[...])
        return 0

    lax.fori_loop(0, 9, tap, 0)
    one_ref[...] = one_acc[...].astype(jnp.bfloat16)
    two_ref[...] = two_acc[...].astype(jnp.bfloat16)
    three_ref[...] = three_acc[...].astype(jnp.bfloat16)


def head_matrices(conv_one, conv_two, conv_three):
    c1, c2 = conv_two.shape[1], conv_two.shape[0]
    one_w = conv_one.transpose(2, 3, 1, 0).reshape(9, 1, c1)
    two_w = conv_two.transpose(2, 3, 1, 0).reshape(9, c1, c2)
    three_w = conv_three.transpose(2, 3, 0, 1).reshape(9, 1, c2)
    shapes = [(64, 64 * c1), (16 * c1, 16 * c2), (4 * c2, 256)]
    vmem = pl.BlockSpec(memory_space=pltpu.VMEM)
    return pl.pallas_call(
        head_kernel,
        out_shape=[jax.ShapeDtypeStruct(s, jnp.bfloat16) for s in shapes],
        in_specs=[vmem] * 3,
        out_specs=[vmem] * 3,
        scratch_shapes=[pltpu.VMEM(s, jnp.float32) for s in shapes],
        compiler_params=pltpu.CompilerParams(vmem_limit_bytes=24 * 1024 * 1024),
        cost_estimate=pl.CostEstimate(flops=10**9, bytes_accessed=3 * 10**6, transcendentals=0),
        name="head_matrices",
    )(one_w, two_w, three_w)


def pair_kernel(frames, buffers, stride, scale, rows_ref, vids_ref, count_ref, entry_ref, one_ref,
                two_ref, three_ref, before_ref, own_hbm, other_hbm, *rest):
    q_hbm, rest = rest[:buffers], rest[buffers:]
    out_ref, q_in, v_in, q_rows, v_rows, maps, q_sem, v_sem = rest
    idx_dev = own_hbm.shape[0]
    width = own_hbm.shape[2] // R
    side = GROUP * frames
    count = count_ref[0]
    groups = (count + GROUP - 1) // GROUP

    def fetch(step, slot):
        def one_pair(p, _):
            row = rows_ref[step * GROUP + p]
            vid = vids_ref[step * GROUP + p]
            buf, row = lax.div(row, stride), lax.rem(row, stride)
            for b in range(buffers):
                @pl.when(buf == b)
                def _():
                    pltpu.make_async_copy(
                        q_hbm[b].at[row], q_in.at[slot, p], q_sem.at[slot]
                    ).start()

            @pl.when(vid < idx_dev)
            def _():
                pltpu.make_async_copy(own_hbm.at[vid], v_in.at[slot, p], v_sem.at[slot]).start()

            @pl.when(vid >= idx_dev)
            def _():
                pltpu.make_async_copy(
                    other_hbm.at[vid - idx_dev], v_in.at[slot, p], v_sem.at[slot]
                ).start()
            return 0
        lax.fori_loop(0, GROUP, one_pair, 0)

    maps[...] = jnp.zeros_like(maps)

    @pl.when(groups > 0)
    def _():
        fetch(0, 0)

    def step(g, _):
        slot = lax.rem(g, 2)

        @pl.when(g + 1 < groups)
        def _():
            fetch(g + 1, 1 - slot)

        pltpu.make_async_copy(q_in.at[slot], q_in.at[slot], q_sem.at[slot]).wait()
        pltpu.make_async_copy(v_in.at[slot], v_in.at[slot], v_sem.at[slot]).wait()
        for r in range(R):
            cols = pl.ds(r * width, width)
            q_rows[pl.ds(r * side, side), :] = q_in[slot, :, :, cols].reshape(side, width)
            v_rows[pl.ds(r * side, side), :] = v_in[slot, :, :, cols].reshape(side, width)

        total = jnp.zeros((side, side), jnp.float32)
        for r in range(R):
            sim = lax.dot_general(
                q_rows[pl.ds(r * side, side), :], v_rows[...], (((1,), (1,)), ((), ())),
                preferred_element_type=jnp.float32,
            )
            best = sim[:, :side]
            for s in range(1, R):
                best = jnp.maximum(best, sim[:, s * side:(s + 1) * side])
            total = total + best
        cells = frames * frames
        same_pair = iota((side, side), 0) // frames == iota((side, side), 1) // frames
        lane, sub = iota((side, cells), 1), iota((side, cells), 0)
        spread = (lane % frames == sub % frames).astype(jnp.bfloat16)
        own_frame = lane // frames == sub % frames
        fold = (iota((GROUP, side), 1) // frames == iota((GROUP, side), 0)).astype(jnp.bfloat16)
        mean = jnp.where(same_pair, total * scale, 0.0).astype(jnp.bfloat16)
        wide = jnp.where(own_frame, dot(mean, spread), 0.0).astype(jnp.bfloat16)
        maps[pl.ds(pl.multiple_of(g * GROUP, GROUP), GROUP), :] = dot(fold, wide)
        return 0

    lax.fori_loop(0, groups, step, 0)

    def pooled(x):
        n = x.shape[1] // 4
        best = x[:, :n]
        for i in range(1, 4):
            best = jnp.maximum(best, x[:, i * n:(i + 1) * n])
        return jnp.maximum(best, 0.0).astype(jnp.bfloat16)

    first = pooled(dot(maps[...].astype(jnp.bfloat16), one_ref[...]))
    second = pooled(dot(first, two_ref[...]))
    final = jnp.clip(dot(second, three_ref[...]), -1.0, 1.0)
    best = jnp.maximum(final[:, :128], final[:, 128:])
    score = (best[:, 0:1] + best[:, 1:2]) * 0.5
    senders, pairs = out_ref.shape
    shape = (score.shape[0], pairs)
    score = jnp.broadcast_to(score, shape)
    place = jnp.broadcast_to(entry_ref[...], shape) - iota(shape, 1)
    for s in range(senders):
        out_ref[pl.ds(s, 1), :] = before_ref[pl.ds(s, 1), :] + jnp.sum(
            jnp.where(place == s * pairs, score, 0.0), axis=0, keepdims=True
        )


def pair_scores(blocks, own, other, rows, vids, count, entry, heads, before, stride, name):
    frames, width = own.shape[1], own.shape[2]
    cap = rows.shape[0]
    side = GROUP * frames
    scale = 1.0 / (math.sqrt(width // R) * R)
    smem = pl.BlockSpec(memory_space=pltpu.SMEM)
    vmem = pl.BlockSpec(memory_space=pltpu.VMEM)
    hbm = pl.BlockSpec(memory_space=pltpu.HBM)
    return pl.pallas_call(
        functools.partial(pair_kernel, frames, len(blocks), stride, scale),
        out_shape=jax.ShapeDtypeStruct(before.shape, jnp.float32),
        in_specs=[smem] * 3 + [vmem] * 5 + [hbm] * (2 + len(blocks)),
        out_specs=vmem,
        scratch_shapes=[
            pltpu.VMEM((2, GROUP, frames, width), jnp.bfloat16),
            pltpu.VMEM((2, GROUP, frames, width), jnp.bfloat16),
            pltpu.VMEM((R * side, width // R), jnp.bfloat16),
            pltpu.VMEM((R * side, width // R), jnp.bfloat16),
            pltpu.VMEM((cap, frames * frames), jnp.float32),
            pltpu.SemaphoreType.DMA((2,)),
            pltpu.SemaphoreType.DMA((2,)),
        ],
        compiler_params=pltpu.CompilerParams(vmem_limit_bytes=58 * 1024 * 1024),
        cost_estimate=pl.CostEstimate(
            flops=2 * cap * side * R * R * frames * (width // R),
            bytes_accessed=cap * frames * width * 4, transcendentals=0,
        ),
        name=name,
    )(rows, vids, count, entry, *heads, before, own, other, *blocks)


def chip_places(mesh):
    devices = list(mesh.devices.flat)[::2]
    places = [tuple(getattr(d, "coords", ()) or ()) for d in devices]
    if any(len(p) != 3 for p in places):
        return [(i, 0, 0) for i in range(len(devices))]
    return [tuple(reversed(p)) for p in places]


def ring_position(coordinate, size):
    if size <= 2:
        return coordinate
    order = list(range(1, size, 2)) + list(reversed(range(0, size, 2)))
    order = [0] + [c for c in order if c != 0]
    return order.index(coordinate)


def plan(sizes, q_dev):
    parts = sum(n for _, n in ROUTES)
    messages = []
    starts, start = [], 0
    for r, (order, share) in enumerate(ROUTES):
        n = q_dev * share // parts
        starts.append((start, n))
        start += n
        have = [(r, 0, 0, 0)]
        for at, letter in enumerate(order):
            axis = "zyx".index(letter)
            if letter == "z" and at == 2:
                for k in range(1, sizes[0]):
                    messages.append((0, (r, k - 1), (r, k), n * sizes[1] * sizes[2]))
                break
            for block in list(have):
                for k in range(1, sizes[axis]):
                    to = list(block)
                    to[1 + axis] = k
                    messages.append((axis, block, tuple(to), n))
                    block = tuple(to)
                    have.append(block)
    users = {}
    for m in messages:
        users.setdefault(m[1], []).append(m)

    def planes(block):
        r, z = block[:2]
        if len(block) == 4 and ROUTES[r][0][2] == "z":
            return users.get((r, 0), [])
        return []

    @functools.cache
    def tail(m):
        after = users.get(m[2], []) + planes(m[2])
        return m[3] + max([tail(a) for a in after], default=0)

    ready = {(r, 0, 0, 0): 0.0 for r in range(len(ROUTES))}
    free = [0.0, 0.0, 0.0]
    waiting, order = list(messages), []

    def when(block):
        if len(block) == 2 and block[1] == 0:
            cells = [(block[0], 0, y, x) for y in range(sizes[1]) for x in range(sizes[2])]
            return max(ready.get(c, math.inf) for c in cells)
        return ready.get(block, math.inf)

    begins = {}
    while waiting:
        best = min(waiting, key=lambda m: (max(free[m[0]], when(m[1])), -tail(m), m))
        begin = max(free[best[0]], when(best[1]))
        free[best[0]] = ready[best[2]] = begin + best[3] + 0.5
        begins[best] = begin
        order.append(best)
        waiting.remove(best)
    return starts, order, begins, ready


def body(places, sizes, queries, index_videos, candidates, conv_one, conv_two, conv_three):
    devices = lax.axis_size("shard")
    q_dev, frames, width = queries.shape
    k_count = candidates.shape[1]
    idx_dev = index_videos.shape[0]
    pairs = q_dev * k_count
    chips = devices // 2
    per_holder = max(2, (2 * pairs + devices - 1) // devices)
    me = lax.axis_index("shard")
    chip, core = me // 2, me % 2

    rings = [tuple(ring_position(c, n) for c, n in zip(p, sizes)) for p in places]
    where = {r: i for i, r in enumerate(rings)}

    def step_along(axis):
        out = []
        for i, ring in enumerate(rings):
            to = list(ring)
            to[axis] = (to[axis] + 1) % sizes[axis]
            out += [(2 * i + c, 2 * where[tuple(to)] + c) for c in range(2)]
        return out

    steps = [step_along(a) for a in range(3)]

    all_ids = lax.all_to_all(
        jnp.broadcast_to(candidates.reshape(1, pairs), (devices, pairs)), "shard", split_axis=0,
        concat_axis=0, tiled=True,
    )
    other = lax.ppermute(index_videos, "shard", [(d, d ^ 1) for d in range(devices)])

    starts, order, begins, arrival = plan(sizes, q_dev)
    plane = [(y, x) for y in range(sizes[1]) for x in range(sizes[2])]

    last = max(arrival.values())
    phase_of = lambda key: next(
        p for p, end in enumerate(PHASE_ENDS) if arrival[key] <= end * last + 1e-6
    )
    phases = [[] for _ in PHASE_ENDS]
    place = {}
    for r, (start, n) in enumerate(starts):
        for z in range(sizes[0]):
            whole = ROUTES[r][0][2] == "z" and z > 0
            for i, (y, x) in enumerate(plane):
                key = (r, z) if whole else (r, z, y, x)
                p = phase_of(key)
                if key not in phases[p]:
                    phases[p].append(key)
                for q in range(n):
                    place[(z, y, x), start + q] = (p, phases[p].index(key), q + (i * n if whole else 0))
    stride = 1 << max(4, (len(plane) * max(n for _, n in starts) - 1).bit_length())
    most = max(len(p) for p in phases)
    spot = np.zeros((chips, chips, q_dev), np.int32)
    caps = [0] * len(phases)
    offsets = sorted({off for off, _ in place})
    for off in offsets:
        for p in range(len(phases)):
            here = sum(place[off, q][0] == p for q in range(q_dev))
            caps[p] += min(here * k_count, 2 * per_holder)
    for c in range(chips):
        for s in range(chips):
            off = tuple((a - b) % n for a, b, n in zip(rings[c], rings[s], sizes))
            for q in range(q_dev):
                p, b, row = place[off, q]
                spot[c, s, q] = (p * most + b) * stride + row
    caps = [-(-c // GROUP) * GROUP for c in caps]

    spot = lax.dynamic_index_in_dim(jnp.asarray(spot), chip, 0, keepdims=False)
    spot = jnp.broadcast_to(spot[:, :, None], (chips, q_dev, k_count)).reshape(chips * pairs)
    ids = all_ids.reshape(chips, 2, pairs)
    ids = jnp.where(core == 0, ids[:, 0], ids[:, 1]).reshape(chips * pairs)
    mine = ids // (2 * idx_dev) == chip
    local = ids % (2 * idx_dev)
    local = jnp.where(local // idx_dev == core, local % idx_dev, local % idx_dev + idx_dev)
    code = jnp.where(mine, spot * (2 * idx_dev) + local, NONE)
    code, entry = lax.sort((code, jnp.arange(chips * pairs, dtype=jnp.int32)), num_keys=1)
    total = chips * 2 * per_holder
    code = jnp.concatenate([code[:total], jnp.full((max(caps),), NONE, jnp.int32)])
    entry = jnp.concatenate([entry[:total], jnp.zeros((max(caps),), jnp.int32)])
    spots = code // (2 * idx_dev)
    phase = jnp.where(code < NONE, spots // (most * stride), len(phases))
    counts = jnp.sum(
        (phase[:, None] == jnp.arange(len(phases))[None, :]).astype(jnp.int32), axis=0
    )
    firsts = jnp.cumsum(counts) - counts
    spots = spots % (most * stride)
    vids = code % (2 * idx_dev)

    heads = head_matrices(conv_one, conv_two, conv_three)
    tables = [jnp.zeros((chips, pairs), jnp.float32)]

    def score(p):
        cut = lambda a: lax.dynamic_slice(a, (firsts[p],), (caps[p],))
        valid = jnp.arange(caps[p]) < counts[p]
        rows, vid = jnp.where(valid, cut(spots), 0), jnp.where(valid, cut(vids), 0)
        entries = jnp.where(valid, cut(entry), NONE)
        tables.append(pair_scores(
            [blocks[k] for k in phases[p]], index_videos, other, rows, vid, counts[p:p + 1],
            entries.reshape(caps[p], 1), heads, tables[-1], stride, "phase_" + str(p),
        ))

    blocks = {}
    for r, (start, n) in enumerate(starts):
        blocks[(r, 0, 0, 0)] = queries[start:start + n]

    def block_of(key):
        if key not in blocks:
            blocks[key] = jnp.concatenate([blocks[(key[0], 0, y, x)] for y, x in plane], axis=0)
        return blocks[key]

    done = [[], [], []]
    for m in order:
        axis, source, target, _ = m
        behind = done[axis][-IN_FLIGHT:][:1] if len(done[axis]) >= IN_FLIGHT else []
        if len(done[axis]) == 1:
            behind.append(all_ids)
        if len(done[axis]) == 3 and axis == 0:
            behind.append(other)
        while len(tables) < len(phases) and begins[m] > PHASE_ENDS[len(tables) - 1] * last + SLACK:
            score(len(tables) - 1)
            behind.append(tables[-1])
        sent = block_of(source)
        if behind:
            sent = lax.optimization_barrier((sent, *behind))[0]
        blocks[target] = lax.ppermute(sent, "shard", steps[axis])
        done[axis].append(blocks[target])
    while len(tables) <= len(phases):
        score(len(tables) - 1)
    table = tables[-1]
    table = jnp.where(jnp.arange(2)[None, :, None] == core, table[:, None], 0.0)
    scores = lax.all_to_all(
        table.reshape(devices, pairs), "shard", split_axis=0, concat_axis=0, tiled=True
    )
    return jnp.sum(scores, axis=0).reshape(q_dev, k_count)


def solution(mesh):
    places = chip_places(mesh)
    low = [min(p[a] for p in places) for a in range(3)]
    places = [tuple(c - m for c, m in zip(p, low)) for p in places]
    sizes = [max(p[a] for p in places) + 1 for a in range(3)]
    placed = (P("shard", None, None), P("shard", None, None), P("shard", None), P(), P(), P())
    return jax.shard_map(
        functools.partial(body, places, sizes), mesh=mesh, in_specs=placed,
        out_specs=P("shard", None), check_vma=False,
    )
```

```python
import functools
import math

import jax
import jax.numpy as jnp
import numpy as np
from jax import lax
from jax.experimental import pallas as pl
from jax.experimental.pallas import tpu as pltpu
from jax.sharding import PartitionSpec as P

R = 5
GROUP = 16
NONE = 1 << 30
ROUTES = (("zxy", 6), ("zyx", 6), ("xyz", 2), ("yxz", 2))
PHASE_ENDS = (0.3, 0.5, 0.67, 0.82, 1.0)
IN_FLIGHT = 2
SLACK = 15.0
HEAD = 64
WEIGHT = 8


def dot(a, b):
    return jnp.dot(a, b, preferred_element_type=jnp.float32)


def iota(shape, dim):
    return lax.broadcasted_iota(jnp.int32, shape, dim)


def head_kernel(one_w, two_w, three_w, one_ref, two_ref, three_ref, one_acc, two_acc, three_acc):
    one_acc[...] = jnp.zeros_like(one_acc)
    two_acc[...] = jnp.zeros_like(two_acc)
    three_acc[...] = jnp.zeros_like(three_acc)
    c1, c2 = two_w.shape[1], two_w.shape[2]
    b1, b2 = c1.bit_length() - 1, c2.bit_length() - 1

    def tap(t, _):
        k = lax.div(t, 3) - 1
        l = lax.rem(t, 3) - 1

        n = one_acc.shape[1]
        row, col = iota((64, n), 0), iota((64, n), 1) >> b1
        y = ((col >> 2) & 3) * 2 + ((col >> 5) & 1)
        x = (col & 3) * 2 + ((col >> 4) & 1)
        hit = ((row >> 3) == y + k) & ((row & 7) == x + l)
        spread = ((iota((c1, n), 1) & (c1 - 1)) == iota((c1, n), 0)).astype(jnp.bfloat16)
        val = dot(jnp.broadcast_to(one_w[t], (16, c1)), spread)[:1]
        one_acc[...] = jnp.where(hit, val, one_acc[...])

        n = two_acc.shape[1]
        spread = ((iota((c2, n), 1) & (c2 - 1)) == iota((c2, n), 0)).astype(jnp.bfloat16)
        val = dot(two_w[t], spread)

        def cell(ij, _):
            col = iota((c1, n), 1) >> b2
            y = ((col >> 1) & 1) * 2 + ((col >> 3) & 1)
            x = (col & 1) * 2 + ((col >> 2) & 1)
            hit = (lax.div(ij, 4) == y + k) & (lax.rem(ij, 4) == x + l)
            rows = pl.ds(pl.multiple_of(ij * c1, c1), c1)
            two_acc[rows, :] = jnp.where(hit, val, two_acc[rows, :])
            return 0
        lax.fori_loop(0, 16, cell, 0)

        m, n = three_acc.shape
        pick = ((iota((m, c2), 0) & (c2 - 1)) == iota((m, c2), 1)).astype(jnp.bfloat16)
        val = lax.dot_general(
            pick, jnp.broadcast_to(three_w[t], (128, c2)), (((1,), (1,)), ((), ())),
            preferred_element_type=jnp.float32,
        )[:, :1]
        row, col = iota((m, n), 0) >> b2, iota((m, n), 1)
        y, x = col & 127, col >> 7
        hit = ((row >> 1) == y + k) & ((row & 1) == x + l) & (y < 2)
        three_acc[...] = jnp.where(hit, val, three_acc[...])
        return 0

    lax.fori_loop(0, 9, tap, 0)
    one_ref[...] = one_acc[...].astype(jnp.bfloat16)
    two_ref[...] = two_acc[...].astype(jnp.bfloat16)
    three_ref[...] = three_acc[...].astype(jnp.bfloat16)


def head_matrices(conv_one, conv_two, conv_three):
    c1, c2 = conv_two.shape[1], conv_two.shape[0]
    one_w = conv_one.transpose(2, 3, 1, 0).reshape(9, 1, c1)
    two_w = conv_two.transpose(2, 3, 1, 0).reshape(9, c1, c2)
    three_w = conv_three.transpose(2, 3, 0, 1).reshape(9, 1, c2)
    shapes = [(64, 64 * c1), (16 * c1, 16 * c2), (4 * c2, 256)]
    vmem = pl.BlockSpec(memory_space=pltpu.VMEM)
    return pl.pallas_call(
        head_kernel,
        out_shape=[jax.ShapeDtypeStruct(s, jnp.bfloat16) for s in shapes],
        in_specs=[vmem] * 3,
        out_specs=[vmem] * 3,
        scratch_shapes=[pltpu.VMEM(s, jnp.float32) for s in shapes],
        compiler_params=pltpu.CompilerParams(vmem_limit_bytes=24 * 1024 * 1024),
        cost_estimate=pl.CostEstimate(flops=10**9, bytes_accessed=3 * 10**6, transcendentals=0),
        name="head_matrices",
    )(one_w, two_w, three_w)


def pair_kernel(frames, buffers, scale, rows_ref, vids_ref, ends_ref, entry_ref, one_ref,
                two_ref, three_ref, before_ref, own_hbm, other_hbm, *rest):
    q_hbm, rest = rest[:buffers], rest[buffers:]
    out_ref, q_in, v_in, q_rows, v_rows, maps, q_sem, v_sem = rest
    idx_dev = own_hbm.shape[0]
    width = own_hbm.shape[2] // R
    side = GROUP * frames
    count = ends_ref[buffers - 1]
    groups = (count + GROUP - 1) // GROUP

    def fetch(step, slot):
        first = step * GROUP
        for b in range(buffers):
            low = 0 if b == 0 else jnp.clip(ends_ref[b - 1] - first, 0, GROUP)
            high = GROUP if b == buffers - 1 else jnp.clip(ends_ref[b] - first, 0, GROUP)

            def one_query(p, _):
                pltpu.make_async_copy(
                    q_hbm[b].at[rows_ref[first + p]], q_in.at[slot, p], q_sem.at[slot]
                ).start()
                return 0
            lax.fori_loop(low, high, one_query, 0)

        def one_video(p, _):
            vid = vids_ref[first + p]

            @pl.when(vid < idx_dev)
            def _():
                pltpu.make_async_copy(own_hbm.at[vid], v_in.at[slot, p], v_sem.at[slot]).start()

            @pl.when(vid >= idx_dev)
            def _():
                pltpu.make_async_copy(
                    other_hbm.at[vid - idx_dev], v_in.at[slot, p], v_sem.at[slot]
                ).start()
            return 0
        lax.fori_loop(0, GROUP, one_video, 0)

    maps[...] = jnp.zeros_like(maps)

    @pl.when(groups > 0)
    def _():
        fetch(0, 0)

    def step(g, _):
        slot = lax.rem(g, 2)

        @pl.when(g + 1 < groups)
        def _():
            fetch(g + 1, 1 - slot)

        pltpu.make_async_copy(q_in.at[slot], q_in.at[slot], q_sem.at[slot]).wait()
        pltpu.make_async_copy(v_in.at[slot], v_in.at[slot], v_sem.at[slot]).wait()
        for r in range(R):
            cols = pl.ds(r * width, width)
            q_rows[pl.ds(r * side, side), :] = q_in[slot, :, :, cols].reshape(side, width)
            v_rows[pl.ds(r * side, side), :] = v_in[slot, :, :, cols].reshape(side, width)

        sim = lax.dot_general(
            q_rows[...], v_rows[...], (((1,), (1,)), ((), ())), preferred_element_type=jnp.float32
        )
        best = sim[:, :side]
        for s in range(1, R):
            best = jnp.maximum(best, sim[:, s * side:(s + 1) * side])
        total = best[:side]
        for r in range(1, R):
            total = total + best[r * side:(r + 1) * side]
        cells = frames * frames
        same_pair = iota((side, side), 0) // frames == iota((side, side), 1) // frames
        lane, sub = iota((side, cells), 1), iota((side, cells), 0)
        spread = (lane % frames == sub % frames).astype(jnp.bfloat16)
        own_frame = lane // frames == sub % frames
        fold = (iota((GROUP, side), 1) // frames == iota((GROUP, side), 0)).astype(jnp.bfloat16)
        mean = jnp.where(same_pair, total * scale, 0.0).astype(jnp.bfloat16)
        wide = jnp.where(own_frame, dot(mean, spread), 0.0).astype(jnp.bfloat16)
        maps[pl.ds(pl.multiple_of(g * GROUP, GROUP), GROUP), :] = dot(fold, wide)
        return 0

    lax.fori_loop(0, groups, step, 0)

    def pooled(x):
        n = x.shape[1] // 4
        best = x[:, :n]
        for i in range(1, 4):
            best = jnp.maximum(best, x[:, i * n:(i + 1) * n])
        return jnp.maximum(best, 0.0).astype(jnp.bfloat16)

    out_ref[...] = before_ref[...]
    senders, pairs = out_ref.shape

    def head(g, _):
        here = pl.ds(pl.multiple_of(g * HEAD, HEAD), HEAD)
        first = pooled(dot(maps[here, :].astype(jnp.bfloat16), one_ref[...]))
        second = pooled(dot(first, two_ref[...]))
        final = jnp.clip(dot(second, three_ref[...]), -1.0, 1.0)
        best = jnp.maximum(final[:, :128], final[:, 128:])
        shape = (HEAD, pairs)
        score = jnp.broadcast_to((best[:, 0:1] + best[:, 1:2]) * 0.5, shape)
        place = jnp.broadcast_to(entry_ref[here, :], shape) - iota(shape, 1)
        for s in range(senders):
            out_ref[pl.ds(s, 1), :] = out_ref[pl.ds(s, 1), :] + jnp.sum(
                jnp.where(place == s * pairs, score, 0.0), axis=0, keepdims=True
            )
        return 0

    lax.fori_loop(0, (count + HEAD - 1) // HEAD, head, 0)


def pair_scores(blocks, own, other, rows, vids, ends, entry, heads, before, name):
    frames, width = own.shape[1], own.shape[2]
    cap = rows.shape[0]
    side = GROUP * frames
    scale = 1.0 / (math.sqrt(width // R) * R)
    smem = pl.BlockSpec(memory_space=pltpu.SMEM)
    vmem = pl.BlockSpec(memory_space=pltpu.VMEM)
    hbm = pl.BlockSpec(memory_space=pltpu.HBM)
    return pl.pallas_call(
        functools.partial(pair_kernel, frames, len(blocks), scale),
        out_shape=jax.ShapeDtypeStruct(before.shape, jnp.float32),
        in_specs=[smem] * 3 + [vmem] * 5 + [hbm] * (2 + len(blocks)),
        out_specs=vmem,
        scratch_shapes=[
            pltpu.VMEM((2, GROUP, frames, width), jnp.bfloat16),
            pltpu.VMEM((2, GROUP, frames, width), jnp.bfloat16),
            pltpu.VMEM((R * side, width // R), jnp.bfloat16),
            pltpu.VMEM((R * side, width // R), jnp.bfloat16),
            pltpu.VMEM((cap, frames * frames), jnp.float32),
            pltpu.SemaphoreType.DMA((2,)),
            pltpu.SemaphoreType.DMA((2,)),
        ],
        compiler_params=pltpu.CompilerParams(vmem_limit_bytes=58 * 1024 * 1024),
        cost_estimate=pl.CostEstimate(
            flops=WEIGHT * 2 * cap * side * R * R * frames * (width // R),
            bytes_accessed=cap * frames * width * 4, transcendentals=0,
        ),
        name=name,
    )(rows, vids, ends, entry, *heads, before, own, other, *blocks)


def chip_places(mesh):
    devices = list(mesh.devices.flat)[::2]
    places = [tuple(getattr(d, "coords", ()) or ()) for d in devices]
    if any(len(p) != 3 for p in places):
        return [(i, 0, 0) for i in range(len(devices))]
    return [tuple(reversed(p)) for p in places]


def ring_position(coordinate, size):
    if size <= 2:
        return coordinate
    order = list(range(1, size, 2)) + list(reversed(range(0, size, 2)))
    order = [0] + [c for c in order if c != 0]
    return order.index(coordinate)


def plan(sizes, q_dev):
    parts = sum(n for _, n in ROUTES)
    messages = []
    starts, start = [], 0
    for r, (order, share) in enumerate(ROUTES):
        n = q_dev * share // parts
        starts.append((start, n))
        start += n
        have = [(r, 0, 0, 0)]
        for at, letter in enumerate(order):
            axis = "zyx".index(letter)
            if letter == "z" and at == 2:
                for k in range(1, sizes[0]):
                    messages.append((0, (r, k - 1), (r, k), n * sizes[1] * sizes[2]))
                break
            for block in list(have):
                for k in range(1, sizes[axis]):
                    to = list(block)
                    to[1 + axis] = k
                    messages.append((axis, block, tuple(to), n))
                    block = tuple(to)
                    have.append(block)
    users = {}
    for m in messages:
        users.setdefault(m[1], []).append(m)

    def planes(block):
        r, z = block[:2]
        if len(block) == 4 and ROUTES[r][0][2] == "z":
            return users.get((r, 0), [])
        return []

    @functools.cache
    def tail(m):
        after = users.get(m[2], []) + planes(m[2])
        return m[3] + max([tail(a) for a in after], default=0)

    ready = {(r, 0, 0, 0): 0.0 for r in range(len(ROUTES))}
    free = [0.0, 0.0, 0.0]
    waiting, order = list(messages), []

    def when(block):
        if len(block) == 2 and block[1] == 0:
            cells = [(block[0], 0, y, x) for y in range(sizes[1]) for x in range(sizes[2])]
            return max(ready.get(c, math.inf) for c in cells)
        return ready.get(block, math.inf)

    begins = {}
    while waiting:
        best = min(waiting, key=lambda m: (max(free[m[0]], when(m[1])), -tail(m), m))
        begin = max(free[best[0]], when(best[1]))
        free[best[0]] = ready[best[2]] = begin + best[3] + 0.5
        begins[best] = begin
        order.append(best)
        waiting.remove(best)
    return starts, order, begins, ready


def body(places, sizes, queries, index_videos, candidates, conv_one, conv_two, conv_three):
    devices = lax.axis_size("shard")
    q_dev, frames, width = queries.shape
    k_count = candidates.shape[1]
    idx_dev = index_videos.shape[0]
    pairs = q_dev * k_count
    chips = devices // 2
    per_holder = max(2, (2 * pairs + devices - 1) // devices)
    me = lax.axis_index("shard")
    chip, core = me // 2, me % 2

    rings = [tuple(ring_position(c, n) for c, n in zip(p, sizes)) for p in places]
    where = {r: i for i, r in enumerate(rings)}

    def step_along(axis):
        out = []
        for i, ring in enumerate(rings):
            to = list(ring)
            to[axis] = (to[axis] + 1) % sizes[axis]
            out += [(2 * i + c, 2 * where[tuple(to)] + c) for c in range(2)]
        return out

    steps = [step_along(a) for a in range(3)]

    all_ids = lax.all_to_all(
        jnp.broadcast_to(candidates.reshape(1, pairs), (devices, pairs)), "shard", split_axis=0,
        concat_axis=0, tiled=True,
    )
    other = lax.ppermute(index_videos, "shard", [(d, d ^ 1) for d in range(devices)])

    starts, order, begins, arrival = plan(sizes, q_dev)
    plane = [(y, x) for y in range(sizes[1]) for x in range(sizes[2])]

    last = max(arrival.values())
    phase_of = lambda key: next(
        p for p, end in enumerate(PHASE_ENDS) if arrival[key] <= end * last + 1e-6
    )
    phases = [[] for _ in PHASE_ENDS]
    place = {}
    for r, (start, n) in enumerate(starts):
        for z in range(sizes[0]):
            whole = ROUTES[r][0][2] == "z" and z > 0
            for i, (y, x) in enumerate(plane):
                key = (r, z) if whole else (r, z, y, x)
                p = phase_of(key)
                if key not in phases[p]:
                    phases[p].append(key)
                for q in range(n):
                    place[(z, y, x), start + q] = (p, phases[p].index(key), q + (i * n if whole else 0))
    stride = 1 << max(4, (len(plane) * max(n for _, n in starts) - 1).bit_length())
    most = max(len(p) for p in phases)
    spot = np.zeros((chips, chips, q_dev), np.int32)
    caps = [0] * len(phases)
    offsets = sorted({off for off, _ in place})
    for off in offsets:
        for p in range(len(phases)):
            here = sum(place[off, q][0] == p for q in range(q_dev))
            caps[p] += min(here * k_count, 2 * per_holder)
    for c in range(chips):
        for s in range(chips):
            off = tuple((a - b) % n for a, b, n in zip(rings[c], rings[s], sizes))
            for q in range(q_dev):
                p, b, row = place[off, q]
                spot[c, s, q] = (p * most + b) * stride + row
    caps = [-(-c // HEAD) * HEAD for c in caps]

    spot = lax.dynamic_index_in_dim(jnp.asarray(spot), chip, 0, keepdims=False)
    spot = jnp.broadcast_to(spot[:, :, None], (chips, q_dev, k_count)).reshape(chips * pairs)
    ids = all_ids.reshape(chips, 2, pairs)
    ids = jnp.where(core == 0, ids[:, 0], ids[:, 1]).reshape(chips * pairs)
    mine = ids // (2 * idx_dev) == chip
    local = ids % (2 * idx_dev)
    local = jnp.where(local // idx_dev == core, local % idx_dev, local % idx_dev + idx_dev)
    code = jnp.where(mine, spot * (2 * idx_dev) + local, NONE)
    code, entry = lax.sort((code, jnp.arange(chips * pairs, dtype=jnp.int32)), num_keys=1)
    total = chips * 2 * per_holder
    code = jnp.concatenate([code[:total], jnp.full((max(caps),), NONE, jnp.int32)])
    entry = jnp.concatenate([entry[:total], jnp.zeros((max(caps),), jnp.int32)])
    spots = code // (2 * idx_dev)
    phase = jnp.where(code < NONE, spots // (most * stride), len(phases))
    counts = jnp.sum(
        (phase[:, None] == jnp.arange(len(phases))[None, :]).astype(jnp.int32), axis=0
    )
    firsts = jnp.cumsum(counts) - counts
    spots = spots % (most * stride)
    vids = code % (2 * idx_dev)

    heads = head_matrices(conv_one, conv_two, conv_three)
    tables = [jnp.zeros((chips, pairs), jnp.float32)]

    def score(p):
        cut = lambda a: lax.dynamic_slice(a, (firsts[p],), (caps[p],))
        valid = jnp.arange(caps[p]) < counts[p]
        spot, vid = cut(spots), jnp.where(valid, cut(vids), 0)
        rows = jnp.where(valid, spot % stride, 0)
        entries = jnp.where(valid, cut(entry), NONE)
        ends = jnp.sum(
            (valid[None, :] & (spot[None, :] // stride <= jnp.arange(len(phases[p]))[:, None]))
            .astype(jnp.int32), axis=1,
        )
        tables.append(pair_scores(
            [blocks[k] for k in phases[p]], index_videos, other, rows, vid, ends,
            entries.reshape(caps[p], 1), heads, tables[-1], "phase_" + str(p),
        ))

    blocks = {}
    for r, (start, n) in enumerate(starts):
        blocks[(r, 0, 0, 0)] = queries[start:start + n]

    def block_of(key):
        if key not in blocks:
            blocks[key] = jnp.concatenate([blocks[(key[0], 0, y, x)] for y, x in plane], axis=0)
        return blocks[key]

    done = [[], [], []]
    for m in order:
        axis, source, target, _ = m
        behind = done[axis][-IN_FLIGHT:][:1] if len(done[axis]) >= IN_FLIGHT else []
        if len(done[axis]) == 4:
            behind.append(all_ids)
        if len(done[axis]) == 3 and axis == 0:
            behind.append(other)
        while len(tables) < len(phases) and begins[m] > PHASE_ENDS[len(tables) - 1] * last + SLACK:
            score(len(tables) - 1)
            behind.append(tables[-1])
        sent = block_of(source)
        if behind:
            sent = lax.optimization_barrier((sent, *behind))[0]
        blocks[target] = lax.ppermute(sent, "shard", steps[axis])
        done[axis].append(blocks[target])
    while len(tables) <= len(phases):
        score(len(tables) - 1)
    table = tables[-1]
    table = jnp.where(jnp.arange(2)[None, :, None] == core, table[:, None], 0.0)
    scores = lax.all_to_all(
        table.reshape(devices, pairs), "shard", split_axis=0, concat_axis=0, tiled=True
    )
    return jnp.sum(scores, axis=0).reshape(q_dev, k_count)


def solution(mesh):
    places = chip_places(mesh)
    low = [min(p[a] for p in places) for a in range(3)]
    places = [tuple(c - m for c, m in zip(p, low)) for p in places]
    sizes = [max(p[a] for p in places) + 1 for a in range(3)]
    placed = (P("shard", None, None), P("shard", None, None), P("shard", None), P(), P(), P())
    return jax.shard_map(
        functools.partial(body, places, sizes), mesh=mesh, in_specs=placed,
        out_specs=P("shard", None), check_vma=False,
    )
```

```python
import functools
import math

import jax
import jax.numpy as jnp
import numpy as np
from jax import lax
from jax.experimental import pallas as pl
from jax.experimental.pallas import tpu as pltpu
from jax.sharding import PartitionSpec as P

R = 5
GROUP = 16
NONE = 1 << 30
SHARES = (7, 7, 1, 1)
HEAD = 64
WEIGHT = 8


def dot(a, b):
    return jnp.dot(a, b, preferred_element_type=jnp.float32)


def iota(shape, dim):
    return lax.broadcasted_iota(jnp.int32, shape, dim)


def head_kernel(one_w, two_w, three_w, one_ref, two_ref, three_ref, one_acc, two_acc, three_acc):
    one_acc[...] = jnp.zeros_like(one_acc)
    two_acc[...] = jnp.zeros_like(two_acc)
    three_acc[...] = jnp.zeros_like(three_acc)
    c1, c2 = two_w.shape[1], two_w.shape[2]
    b1, b2 = c1.bit_length() - 1, c2.bit_length() - 1

    def tap(t, _):
        k = lax.div(t, 3) - 1
        l = lax.rem(t, 3) - 1

        n = one_acc.shape[1]
        row, col = iota((64, n), 0), iota((64, n), 1) >> b1
        y = ((col >> 2) & 3) * 2 + ((col >> 5) & 1)
        x = (col & 3) * 2 + ((col >> 4) & 1)
        hit = ((row >> 3) == y + k) & ((row & 7) == x + l)
        spread = ((iota((c1, n), 1) & (c1 - 1)) == iota((c1, n), 0)).astype(jnp.bfloat16)
        val = dot(jnp.broadcast_to(one_w[t], (16, c1)), spread)[:1]
        one_acc[...] = jnp.where(hit, val, one_acc[...])

        n = two_acc.shape[1]
        spread = ((iota((c2, n), 1) & (c2 - 1)) == iota((c2, n), 0)).astype(jnp.bfloat16)
        val = dot(two_w[t], spread)

        def cell(ij, _):
            col = iota((c1, n), 1) >> b2
            y = ((col >> 1) & 1) * 2 + ((col >> 3) & 1)
            x = (col & 1) * 2 + ((col >> 2) & 1)
            hit = (lax.div(ij, 4) == y + k) & (lax.rem(ij, 4) == x + l)
            rows = pl.ds(pl.multiple_of(ij * c1, c1), c1)
            two_acc[rows, :] = jnp.where(hit, val, two_acc[rows, :])
            return 0
        lax.fori_loop(0, 16, cell, 0)

        m, n = three_acc.shape
        pick = ((iota((m, c2), 0) & (c2 - 1)) == iota((m, c2), 1)).astype(jnp.bfloat16)
        val = lax.dot_general(
            pick, jnp.broadcast_to(three_w[t], (128, c2)), (((1,), (1,)), ((), ())),
            preferred_element_type=jnp.float32,
        )[:, :1]
        row, col = iota((m, n), 0) >> b2, iota((m, n), 1)
        y, x = col & 127, col >> 7
        hit = ((row >> 1) == y + k) & ((row & 1) == x + l) & (y < 2)
        three_acc[...] = jnp.where(hit, val, three_acc[...])
        return 0

    lax.fori_loop(0, 9, tap, 0)
    one_ref[...] = one_acc[...].astype(jnp.bfloat16)
    two_ref[...] = two_acc[...].astype(jnp.bfloat16)
    three_ref[...] = three_acc[...].astype(jnp.bfloat16)


def head_matrices(conv_one, conv_two, conv_three):
    c1, c2 = conv_two.shape[1], conv_two.shape[0]
    one_w = conv_one.transpose(2, 3, 1, 0).reshape(9, 1, c1)
    two_w = conv_two.transpose(2, 3, 1, 0).reshape(9, c1, c2)
    three_w = conv_three.transpose(2, 3, 0, 1).reshape(9, 1, c2)
    shapes = [(64, 64 * c1), (16 * c1, 16 * c2), (4 * c2, 256)]
    vmem = pl.BlockSpec(memory_space=pltpu.VMEM)
    return pl.pallas_call(
        head_kernel,
        out_shape=[jax.ShapeDtypeStruct(s, jnp.bfloat16) for s in shapes],
        in_specs=[vmem] * 3,
        out_specs=[vmem] * 3,
        scratch_shapes=[pltpu.VMEM(s, jnp.float32) for s in shapes],
        compiler_params=pltpu.CompilerParams(vmem_limit_bytes=24 * 1024 * 1024),
        cost_estimate=pl.CostEstimate(flops=10**9, bytes_accessed=3 * 10**6, transcendentals=0),
        name="head_matrices",
    )(one_w, two_w, three_w)


def pair_kernel(frames, buffers, scale, rows_ref, vids_ref, ends_ref, entry_ref, one_ref,
                two_ref, three_ref, before_ref, v_hbm, *rest):
    q_hbm, rest = rest[:buffers], rest[buffers:]
    out_ref, q_in, v_in, q_rows, v_rows, maps, q_sem, v_sem = rest
    width = v_hbm.shape[2] // R
    side = GROUP * frames
    count = ends_ref[buffers - 1]
    groups = (count + GROUP - 1) // GROUP

    def fetch(step, slot):
        first = step * GROUP
        for b in range(buffers):
            low = 0 if b == 0 else jnp.clip(ends_ref[b - 1] - first, 0, GROUP)
            high = GROUP if b == buffers - 1 else jnp.clip(ends_ref[b] - first, 0, GROUP)

            def one_query(p, _):
                pltpu.make_async_copy(
                    q_hbm[b].at[rows_ref[first + p]], q_in.at[slot, p], q_sem.at[slot]
                ).start()
                return 0
            lax.fori_loop(low, high, one_query, 0)

        def one_video(p, _):
            pltpu.make_async_copy(
                v_hbm.at[vids_ref[first + p]], v_in.at[slot, p], v_sem.at[slot]
            ).start()
            return 0
        lax.fori_loop(0, GROUP, one_video, 0)

    maps[...] = jnp.zeros_like(maps)

    @pl.when(groups > 0)
    def _():
        fetch(0, 0)

    def step(g, _):
        slot = lax.rem(g, 2)

        @pl.when(g + 1 < groups)
        def _():
            fetch(g + 1, 1 - slot)

        pltpu.make_async_copy(q_in.at[slot], q_in.at[slot], q_sem.at[slot]).wait()
        pltpu.make_async_copy(v_in.at[slot], v_in.at[slot], v_sem.at[slot]).wait()
        for r in range(R):
            cols = pl.ds(r * width, width)
            q_rows[pl.ds(r * side, side), :] = q_in[slot, :, :, cols].reshape(side, width)
            v_rows[pl.ds(r * side, side), :] = v_in[slot, :, :, cols].reshape(side, width)

        sim = lax.dot_general(
            q_rows[...], v_rows[...], (((1,), (1,)), ((), ())), preferred_element_type=jnp.float32
        )
        best = sim[:, :side]
        for s in range(1, R):
            best = jnp.maximum(best, sim[:, s * side:(s + 1) * side])
        total = best[:side]
        for r in range(1, R):
            total = total + best[r * side:(r + 1) * side]
        cells = frames * frames
        same_pair = iota((side, side), 0) // frames == iota((side, side), 1) // frames
        lane, sub = iota((side, cells), 1), iota((side, cells), 0)
        spread = (lane % frames == sub % frames).astype(jnp.bfloat16)
        own_frame = lane // frames == sub % frames
        fold = (iota((GROUP, side), 1) // frames == iota((GROUP, side), 0)).astype(jnp.bfloat16)
        mean = jnp.where(same_pair, total * scale, 0.0).astype(jnp.bfloat16)
        wide = jnp.where(own_frame, dot(mean, spread), 0.0).astype(jnp.bfloat16)
        maps[pl.ds(pl.multiple_of(g * GROUP, GROUP), GROUP), :] = dot(fold, wide)
        return 0

    lax.fori_loop(0, groups, step, 0)

    def pooled(x):
        n = x.shape[1] // 4
        best = x[:, :n]
        for i in range(1, 4):
            best = jnp.maximum(best, x[:, i * n:(i + 1) * n])
        return jnp.maximum(best, 0.0).astype(jnp.bfloat16)

    out_ref[...] = before_ref[...]
    senders, pairs = out_ref.shape

    def head(g, _):
        here = pl.ds(pl.multiple_of(g * HEAD, HEAD), HEAD)
        first = pooled(dot(maps[here, :].astype(jnp.bfloat16), one_ref[...]))
        second = pooled(dot(first, two_ref[...]))
        final = jnp.clip(dot(second, three_ref[...]), -1.0, 1.0)
        best = jnp.maximum(final[:, :128], final[:, 128:])
        shape = (HEAD, pairs)
        score = jnp.broadcast_to((best[:, 0:1] + best[:, 1:2]) * 0.5, shape)
        place = jnp.broadcast_to(entry_ref[here, :], shape) - iota(shape, 1)
        for s in range(senders):
            out_ref[pl.ds(s, 1), :] = out_ref[pl.ds(s, 1), :] + jnp.sum(
                jnp.where(place == s * pairs, score, 0.0), axis=0, keepdims=True
            )
        return 0

    lax.fori_loop(0, (count + HEAD - 1) // HEAD, head, 0)


def pair_scores(blocks, videos, rows, vids, ends, entry, heads, before, name):
    frames, width = videos.shape[1], videos.shape[2]
    cap = rows.shape[0]
    side = GROUP * frames
    scale = 1.0 / (math.sqrt(width // R) * R)
    smem = pl.BlockSpec(memory_space=pltpu.SMEM)
    vmem = pl.BlockSpec(memory_space=pltpu.VMEM)
    hbm = pl.BlockSpec(memory_space=pltpu.HBM)
    return pl.pallas_call(
        functools.partial(pair_kernel, frames, len(blocks), scale),
        out_shape=jax.ShapeDtypeStruct(before.shape, jnp.float32),
        in_specs=[smem] * 3 + [vmem] * 5 + [hbm] * (1 + len(blocks)),
        out_specs=vmem,
        scratch_shapes=[
            pltpu.VMEM((2, GROUP, frames, width), jnp.bfloat16),
            pltpu.VMEM((2, GROUP, frames, width), jnp.bfloat16),
            pltpu.VMEM((R * side, width // R), jnp.bfloat16),
            pltpu.VMEM((R * side, width // R), jnp.bfloat16),
            pltpu.VMEM((cap, frames * frames), jnp.float32),
            pltpu.SemaphoreType.DMA((2,)),
            pltpu.SemaphoreType.DMA((2,)),
        ],
        compiler_params=pltpu.CompilerParams(vmem_limit_bytes=58 * 1024 * 1024),
        cost_estimate=pl.CostEstimate(
            flops=WEIGHT * 2 * cap * side * R * R * frames * (width // R),
            bytes_accessed=cap * frames * width * 4, transcendentals=0,
        ),
        name=name,
    )(rows, vids, ends, entry, *heads, before, videos, *blocks)


def chip_places(mesh):
    devices = list(mesh.devices.flat)[::2]
    places = [tuple(getattr(d, "coords", ()) or ()) for d in devices]
    if any(len(p) != 3 for p in places):
        return [(i, 0, 0) for i in range(len(devices))]
    return [tuple(reversed(p)) for p in places]


def ring_position(coordinate, size):
    if size <= 2:
        return coordinate
    order = list(range(1, size, 2)) + list(reversed(range(0, size, 2)))
    order = [0] + [c for c in order if c != 0]
    return order.index(coordinate)


class Gather:
    def __init__(self, sizes, steps, queries):
        self.steps = steps
        q_dev = queries.shape[0]
        depth, height, width = sizes
        counts = [q_dev * s // sum(SHARES) for s in SHARES]
        starts = [sum(counts[:r]) for r in range(4)]
        a = counts[0] + counts[1]
        self.blocks, self.cells, self.arrival = {}, {}, {}

        def put(key, array, cells, at):
            self.blocks[key], self.cells[key], self.arrival[key] = array, cells, at

        def moved(cells, axis, k):
            out = []
            for off, q, n in cells:
                off = list(off)
                off[axis] = k
                out.append((tuple(off), q, n))
            return out

        here = (0, 0, 0)
        put(("a", 0), queries[:a], [(here, 0, a)], -1)
        for r in (2, 3):
            put(("b", r), queries[starts[r]:starts[r] + counts[r]], [(here, starts[r], counts[r])], -1)

        self.describe = {}

        def ring(axis, source, name, cells):
            out = []
            for k in range(1, sizes[axis]):
                target = name + (k,)
                self.describe[target] = moved(cells, axis, k)
                out.append((axis, source, target))
                source = target
            return out

        first, second = [], []
        joins = {}
        for r, (p, q) in ((2, (2, 1)), (3, (1, 2))):
            cells = self.cells[("b", r)]
            line = ring(p, ("b", r), ("b", r, "line"), cells)
            first.append(line)
            joins[("b", r, "row")] = [("b", r)] + [m[2] for m in line]
            row = [c for k in range(sizes[p]) for c in moved(cells, p, k)]
            self.describe[("b", r, "row")] = row
            turn = ring(q, ("b", r, "row"), ("b", r, "turn"), row)
            second.append(turn)
            joins[("b", r, "plane")] = [("b", r, "row")] + [m[2] for m in turn]
            self.describe[("b", r, "plane")] = [c for k in range(sizes[q]) for c in moved(row, q, k)]
        joins[("b", 0)] = [("b", 2, "plane"), ("b", 3, "plane")]
        self.describe[("b", 0)] = [c for r in (2, 3) for c in self.describe[("b", r, "plane")]]
        self.joins = joins
        self.halves = {}

        rounds = []
        for k in range(depth):
            for r, (p, q) in ((0, (2, 1)), (1, (1, 2))):
                own = ("a", k, r)
                self.halves[own] = (("a", k), starts[r], counts[r])
                self.describe[own] = [((k, 0, 0), starts[r], counts[r])]
            lists = {1: [], 2: []}
            later = {1: [], 2: []}
            for r, (p, q) in ((0, (2, 1)), (1, (1, 2))):
                own = ("a", k, r)
                line = ring(p, own, ("a", k, r, "line"), self.describe[own])
                lists[p] += line
                for i, source in enumerate([own] + [m[2] for m in line]):
                    later[q] += ring(q, source, ("a", k, r, "turn", i), self.describe[source])
            both = [lists[axis] + later[axis] for axis in (2, 1)]
            for i in range(max(map(len, both))):
                rounds.append([l[i] for l in both if i < len(l)])
        pairs_of = lambda ls: [[l[i] for l in ls if i < len(l)] for i in range(max(map(len, ls)))]
        lead, middle = pairs_of(first), pairs_of(second)

        deep = ring(0, ("a", 0), ("a",), self.cells[("a", 0)]) + ring(
            0, ("b", 0), ("b",), self.describe[("b", 0)]
        )
        gap = max(1, len(rounds) // max(1, len(deep)))
        while len(rounds) < gap * len(deep):
            rounds.append([])
        for i, m in enumerate(deep):
            rounds[i * gap].append(m)
        self.per_plane = len(rounds) // depth
        at = min(2, len(rounds))
        self.rounds = lead + rounds[:at] + middle + rounds[at:]
        self.offset = len(lead) + len(middle)
        for i, messages in enumerate(self.rounds):
            for axis, _, target in messages:
                self.arrival[target] = i if axis else i + gap - 1
                self.cells[target] = self.describe[target]
        self.arrival[("b", 0)] = len(lead) + at + len(middle) - 1
        self.cells[("b", 0)] = self.describe[("b", 0)]

    def block(self, key):
        if key not in self.blocks:
            if key in self.joins:
                self.blocks[key] = jnp.concatenate([self.block(k) for k in self.joins[key]], axis=0)
            else:
                whole, start, n = self.halves[key]
                self.blocks[key] = self.block(whole)[start:start + n]
        return self.blocks[key]

    def buffers(self):
        keys = [k for k in self.arrival if k[0] == "a" and (len(k) == 2 or len(k) > 3)]
        return keys + [k for k in self.arrival if k[0] == "b" and len(k) == 2 and isinstance(k[1], int)]


def body(places, sizes, queries, index_videos, candidates, conv_one, conv_two, conv_three):
    devices = lax.axis_size("shard")
    q_dev, frames, width = queries.shape
    k_count = candidates.shape[1]
    idx_dev = index_videos.shape[0]
    pairs = q_dev * k_count
    chips = devices // 2
    per_holder = max(2, (2 * pairs + devices - 1) // devices)
    me = lax.axis_index("shard")
    chip, core = me // 2, me % 2

    rings = [tuple(ring_position(c, n) for c, n in zip(p, sizes)) for p in places]
    where = {r: i for i, r in enumerate(rings)}

    def step_along(axis):
        out = []
        for i, ring in enumerate(rings):
            to = list(ring)
            to[axis] = (to[axis] + 1) % sizes[axis]
            out += [(2 * i + c, 2 * where[tuple(to)] + c) for c in range(2)]
        return out

    videos = lax.all_gather(
        index_videos, "shard", axis=0, tiled=True,
        axis_index_groups=[[2 * c, 2 * c + 1] for c in range(chips)],
    )
    gather = Gather(sizes, [step_along(a) for a in range(3)], queries)
    rounds = gather.rounds

    total = len(rounds)
    ends = [gather.offset + gather.per_plane * (z + 1) - 1 for z in range(sizes[0] - 1)]
    ends = sorted({e for e in ends if 0 <= e < total - 2} | {total - 2, total - 1})
    phases = [[] for _ in ends]
    place = {}
    for key in gather.buffers():
        p = next(i for i, e in enumerate(ends) if gather.arrival[key] <= e)
        row = 0
        for off, first, n in gather.cells[key]:
            for q in range(first, first + n):
                place[off, q] = (p, len(phases[p]), row)
                row += 1
        phases[p].append(key)
    stride = 1 << max(row for _, _, row in place.values()).bit_length()
    most = max(len(p) for p in phases)
    caps = [0] * len(phases)
    for off in sorted({off for off, _ in place}):
        for p in range(len(phases)):
            here = sum(place[off, q][0] == p for q in range(q_dev))
            caps[p] += min(here * k_count, 2 * per_holder)
    caps = [-(-c // HEAD) * HEAD for c in caps]
    spot = np.zeros((chips, chips, q_dev), np.int32)
    for c in range(chips):
        for s in range(chips):
            off = tuple((a - b) % n for a, b, n in zip(rings[c], rings[s], sizes))
            for q in range(q_dev):
                p, b, row = place[off, q]
                spot[c, s, q] = (p * most + b) * stride + row

    state = {}

    def lists(all_ids):
        spots = lax.dynamic_index_in_dim(jnp.asarray(spot), chip, 0, keepdims=False)
        spots = jnp.broadcast_to(spots[:, :, None], (chips, q_dev, k_count)).reshape(chips * pairs)
        ids = all_ids.reshape(chips, 2, pairs)
        ids = jnp.where(core == 0, ids[:, 0], ids[:, 1]).reshape(chips * pairs)
        mine = ids // (2 * idx_dev) == chip
        code = jnp.where(mine, spots * (2 * idx_dev) + ids % (2 * idx_dev), NONE)
        code, entry = lax.sort((code, jnp.arange(chips * pairs, dtype=jnp.int32)), num_keys=1)
        keep = chips * 2 * per_holder
        code = jnp.concatenate([code[:keep], jnp.full((max(caps),), NONE, jnp.int32)])
        entry = jnp.concatenate([entry[:keep], jnp.zeros((max(caps),), jnp.int32)])
        spots = code // (2 * idx_dev)
        phase = jnp.where(code < NONE, spots // (most * stride), len(phases))
        counts = jnp.sum(
            (phase[:, None] == jnp.arange(len(phases))[None, :]).astype(jnp.int32), axis=0
        )
        return spots % (most * stride), code % (2 * idx_dev), entry, counts, jnp.cumsum(counts) - counts

    heads = head_matrices(conv_one, conv_two, conv_three)
    tables = [jnp.zeros((chips, pairs), jnp.float32)]

    def score():
        p = len(tables) - 1
        spots, vids, entry, counts, firsts = state["lists"]
        cut = lambda a: lax.dynamic_slice(a, (firsts[p],), (caps[p],))
        valid = jnp.arange(caps[p]) < counts[p]
        at, vid = cut(spots), jnp.where(valid, cut(vids), 0)
        rows = jnp.where(valid, at % stride, 0)
        entries = jnp.where(valid, cut(entry), NONE)
        upto = jnp.sum(
            (valid[None, :] & (at[None, :] // stride <= jnp.arange(len(phases[p]))[:, None]))
            .astype(jnp.int32), axis=1,
        )
        tables.append(pair_scores(
            [gather.block(k) for k in phases[p]], videos, rows, vid, upto,
            entries.reshape(caps[p], 1), heads, tables[-1], "phase_" + str(p),
        ))

    done, deep = [], []
    for i, messages in enumerate(rounds):
        behind = list(done[i - 2]) if i >= 2 else []
        if any(axis == 0 for axis, _, _ in messages):
            behind += deep[-1:]
        if len(tables) <= len(ends) and i >= 2:
            if i == min(ends[len(tables) - 1] + 4, total - 1) and ends[len(tables) - 1] <= i - 2:
                score()
                behind.append(tables[-1])
        sent = [gather.block(source) for _, source, _ in messages]
        sent = lax.optimization_barrier((*sent, *behind))[:len(sent)]
        done.append([])
        for (axis, _, target), block in zip(messages, sent):
            gather.blocks[target] = lax.ppermute(block, "shard", gather.steps[axis])
            (done[i] if axis else deep).append(gather.blocks[target])
        if i == 0:
            ids = lax.optimization_barrier((candidates, *done[0]))[0].reshape(1, pairs)
            state["lists"] = lists(lax.all_to_all(
                jnp.broadcast_to(ids, (devices, pairs)), "shard", split_axis=0, concat_axis=0,
                tiled=True,
            ))
    while len(tables) <= len(ends):
        score()
    table = jnp.where(jnp.arange(2)[None, :, None] == core, tables[-1][:, None], 0.0)
    scores = lax.all_to_all(
        table.reshape(devices, pairs), "shard", split_axis=0, concat_axis=0, tiled=True
    )
    return jnp.sum(scores, axis=0).reshape(q_dev, k_count)


def solution(mesh):
    places = chip_places(mesh)
    low = [min(p[a] for p in places) for a in range(3)]
    places = [tuple(c - m for c, m in zip(p, low)) for p in places]
    sizes = [max(p[a] for p in places) + 1 for a in range(3)]
    placed = (P("shard", None, None), P("shard", None, None), P("shard", None), P(), P(), P())
    return jax.shard_map(
        functools.partial(body, places, sizes), mesh=mesh, in_specs=placed,
        out_specs=P("shard", None), check_vma=False,
    )
```

```python
import functools
import math

import jax
import jax.numpy as jnp
import numpy as np
from jax import lax
from jax.experimental import pallas as pl
from jax.experimental.pallas import tpu as pltpu
from jax.sharding import PartitionSpec as P

R = 5
GROUP = 16
SHARES = (7, 7, 1, 1)
HEAD = 64
WEIGHT = 8


def dot(a, b):
    return jnp.dot(a, b, preferred_element_type=jnp.float32)


def iota(shape, dim):
    return lax.broadcasted_iota(jnp.int32, shape, dim)


def head_kernel(one_w, two_w, three_w, one_ref, two_ref, three_ref, one_acc, two_acc, three_acc):
    one_acc[...] = jnp.zeros_like(one_acc)
    two_acc[...] = jnp.zeros_like(two_acc)
    three_acc[...] = jnp.zeros_like(three_acc)
    c1, c2 = two_w.shape[1], two_w.shape[2]
    b1, b2 = c1.bit_length() - 1, c2.bit_length() - 1

    def tap(t, _):
        k = lax.div(t, 3) - 1
        l = lax.rem(t, 3) - 1

        n = one_acc.shape[1]
        row, col = iota((64, n), 0), iota((64, n), 1) >> b1
        y = ((col >> 2) & 3) * 2 + ((col >> 5) & 1)
        x = (col & 3) * 2 + ((col >> 4) & 1)
        hit = ((row >> 3) == y + k) & ((row & 7) == x + l)
        spread = ((iota((c1, n), 1) & (c1 - 1)) == iota((c1, n), 0)).astype(jnp.bfloat16)
        val = dot(jnp.broadcast_to(one_w[t], (16, c1)), spread)[:1]
        one_acc[...] = jnp.where(hit, val, one_acc[...])

        n = two_acc.shape[1]
        spread = ((iota((c2, n), 1) & (c2 - 1)) == iota((c2, n), 0)).astype(jnp.bfloat16)
        val = dot(two_w[t], spread)

        def cell(ij, _):
            col = iota((c1, n), 1) >> b2
            y = ((col >> 1) & 1) * 2 + ((col >> 3) & 1)
            x = (col & 1) * 2 + ((col >> 2) & 1)
            hit = (lax.div(ij, 4) == y + k) & (lax.rem(ij, 4) == x + l)
            rows = pl.ds(pl.multiple_of(ij * c1, c1), c1)
            two_acc[rows, :] = jnp.where(hit, val, two_acc[rows, :])
            return 0
        lax.fori_loop(0, 16, cell, 0)

        m, n = three_acc.shape
        pick = ((iota((m, c2), 0) & (c2 - 1)) == iota((m, c2), 1)).astype(jnp.bfloat16)
        val = lax.dot_general(
            pick, jnp.broadcast_to(three_w[t], (128, c2)), (((1,), (1,)), ((), ())),
            preferred_element_type=jnp.float32,
        )[:, :1]
        row, col = iota((m, n), 0) >> b2, iota((m, n), 1)
        y, x = col & 127, col >> 7
        hit = ((row >> 1) == y + k) & ((row & 1) == x + l) & (y < 2)
        three_acc[...] = jnp.where(hit, val, three_acc[...])
        return 0

    lax.fori_loop(0, 9, tap, 0)
    one_ref[...] = one_acc[...].astype(jnp.bfloat16)
    two_ref[...] = two_acc[...].astype(jnp.bfloat16)
    three_ref[...] = three_acc[...].astype(jnp.bfloat16)


def head_matrices(conv_one, conv_two, conv_three):
    c1, c2 = conv_two.shape[1], conv_two.shape[0]
    one_w = conv_one.transpose(2, 3, 1, 0).reshape(9, 1, c1)
    two_w = conv_two.transpose(2, 3, 1, 0).reshape(9, c1, c2)
    three_w = conv_three.transpose(2, 3, 0, 1).reshape(9, 1, c2)
    shapes = [(64, 64 * c1), (16 * c1, 16 * c2), (4 * c2, 256)]
    vmem = pl.BlockSpec(memory_space=pltpu.VMEM)
    return pl.pallas_call(
        head_kernel,
        out_shape=[jax.ShapeDtypeStruct(s, jnp.bfloat16) for s in shapes],
        in_specs=[vmem] * 3,
        out_specs=[vmem] * 3,
        scratch_shapes=[pltpu.VMEM(s, jnp.float32) for s in shapes],
        compiler_params=pltpu.CompilerParams(vmem_limit_bytes=24 * 1024 * 1024),
        cost_estimate=pl.CostEstimate(flops=10**9, bytes_accessed=3 * 10**6, transcendentals=0),
        name="head_matrices",
    )(one_w, two_w, three_w)


def pair_kernel(frames, idx_dev, k_count, bounds, scale, who_ref, ids_ref, queries_ref, one_ref,
                two_ref, three_ref, before_ref, v_hbm, *rest):
    buffers = len(bounds) - 1
    q_hbm, rest = rest[:buffers], rest[buffers:]
    (out_ref, q_in, v_in, q_rows, v_rows, maps, scores, rows_ref, vids_ref, entry_ref, ends_ref,
     q_sem, v_sem) = rest
    width = v_hbm.shape[2] // R
    side = GROUP * frames
    senders, pairs = out_ref.shape
    chip, core = who_ref[0], who_ref[1]

    count = jnp.int32(0)
    for b in range(buffers):
        def one_of(t, n):
            packed = queries_ref[t]
            row, query = packed & 255, (packed >> 8) & 255
            sender = who_ref[2 + (packed >> 16)]
            for k in range(k_count):
                pair = query * k_count + k
                vid = ids_ref[2 * sender + core, pair]
                rows_ref[n] = row
                vids_ref[n] = lax.rem(vid, 2 * idx_dev)
                entry_ref[n] = sender * pairs + pair
                n = n + (lax.div(vid, 2 * idx_dev) == chip).astype(jnp.int32)
            return n
        count = lax.fori_loop(bounds[b], bounds[b + 1], one_of, count)
        ends_ref[b] = count
    for p in range(GROUP):
        rows_ref[count + p] = 0
        vids_ref[count + p] = 0
    groups = (count + GROUP - 1) // GROUP

    def fetch(step, slot):
        first = step * GROUP
        for b in range(buffers):
            low = 0 if b == 0 else jnp.clip(ends_ref[b - 1] - first, 0, GROUP)
            high = GROUP if b == buffers - 1 else jnp.clip(ends_ref[b] - first, 0, GROUP)

            def one_query(p, _):
                pltpu.make_async_copy(
                    q_hbm[b].at[rows_ref[first + p]], q_in.at[slot, p], q_sem.at[slot]
                ).start()
                return 0
            lax.fori_loop(low, high, one_query, 0)

        def one_video(p, _):
            pltpu.make_async_copy(
                v_hbm.at[vids_ref[first + p]], v_in.at[slot, p], v_sem.at[slot]
            ).start()
            return 0
        lax.fori_loop(0, GROUP, one_video, 0)

    maps[...] = jnp.zeros_like(maps)

    @pl.when(groups > 0)
    def _():
        fetch(0, 0)

    def step(g, _):
        slot = lax.rem(g, 2)

        @pl.when(g + 1 < groups)
        def _():
            fetch(g + 1, 1 - slot)

        pltpu.make_async_copy(q_in.at[slot], q_in.at[slot], q_sem.at[slot]).wait()
        pltpu.make_async_copy(v_in.at[slot], v_in.at[slot], v_sem.at[slot]).wait()
        for r in range(R):
            cols = pl.ds(r * width, width)
            q_rows[pl.ds(r * side, side), :] = q_in[slot, :, :, cols].reshape(side, width)
            v_rows[pl.ds(r * side, side), :] = v_in[slot, :, :, cols].reshape(side, width)

        sim = lax.dot_general(
            q_rows[...], v_rows[...], (((1,), (1,)), ((), ())), preferred_element_type=jnp.float32
        )
        best = sim[:, :side]
        for s in range(1, R):
            best = jnp.maximum(best, sim[:, s * side:(s + 1) * side])
        total = best[:side]
        for r in range(1, R):
            total = total + best[r * side:(r + 1) * side]
        cells = frames * frames
        same_pair = iota((side, side), 0) // frames == iota((side, side), 1) // frames
        lane, sub = iota((side, cells), 1), iota((side, cells), 0)
        spread = (lane % frames == sub % frames).astype(jnp.bfloat16)
        own_frame = lane // frames == sub % frames
        fold = (iota((GROUP, side), 1) // frames == iota((GROUP, side), 0)).astype(jnp.bfloat16)
        mean = jnp.where(same_pair, total * scale, 0.0).astype(jnp.bfloat16)
        wide = jnp.where(own_frame, dot(mean, spread), 0.0).astype(jnp.bfloat16)
        maps[pl.ds(pl.multiple_of(g * GROUP, GROUP), GROUP), :] = dot(fold, wide)
        return 0

    lax.fori_loop(0, groups, step, 0)

    def pooled(x):
        n = x.shape[1] // 4
        best = x[:, :n]
        for i in range(1, 4):
            best = jnp.maximum(best, x[:, i * n:(i + 1) * n])
        return jnp.maximum(best, 0.0).astype(jnp.bfloat16)

    def head(g, _):
        here = pl.ds(pl.multiple_of(g * HEAD, HEAD), HEAD)
        first = pooled(dot(maps[here, :].astype(jnp.bfloat16), one_ref[...]))
        second = pooled(dot(first, two_ref[...]))
        final = jnp.clip(dot(second, three_ref[...]), -1.0, 1.0)
        best = jnp.maximum(final[:, :128], final[:, 128:])
        scores[here, :] = jnp.broadcast_to((best[:, 0:1] + best[:, 1:2]) * 0.5, (HEAD, pairs))
        return 0

    lax.fori_loop(0, (count + HEAD - 1) // HEAD, head, 0)

    out_ref[...] = before_ref[...]

    def write(i, _):
        entry = entry_ref[i]
        at = pl.ds(lax.div(entry, pairs), 1)
        hit = iota((1, pairs), 1) == lax.rem(entry, pairs)
        out_ref[at, :] = jnp.where(hit, scores[pl.ds(i, 1), :], out_ref[at, :])
        return 0

    lax.fori_loop(0, count, write, 0)


def pair_scores(blocks, videos, who, ids, queries, bounds, cap, heads, before, k_count, idx_dev, name):
    frames, width = videos.shape[1], videos.shape[2]
    pairs = before.shape[1]
    side = GROUP * frames
    scale = 1.0 / (math.sqrt(width // R) * R)
    smem = pl.BlockSpec(memory_space=pltpu.SMEM)
    vmem = pl.BlockSpec(memory_space=pltpu.VMEM)
    hbm = pl.BlockSpec(memory_space=pltpu.HBM)
    return pl.pallas_call(
        functools.partial(pair_kernel, frames, idx_dev, k_count, bounds, scale),
        out_shape=jax.ShapeDtypeStruct(before.shape, jnp.float32),
        in_specs=[smem] * 3 + [vmem] * 4 + [hbm] * (1 + len(blocks)),
        out_specs=vmem,
        scratch_shapes=[
            pltpu.VMEM((2, GROUP, frames, width), jnp.bfloat16),
            pltpu.VMEM((2, GROUP, frames, width), jnp.bfloat16),
            pltpu.VMEM((R * side, width // R), jnp.bfloat16),
            pltpu.VMEM((R * side, width // R), jnp.bfloat16),
            pltpu.VMEM((cap, frames * frames), jnp.float32),
            pltpu.VMEM((cap, pairs), jnp.float32),
            pltpu.SMEM((cap + GROUP,), jnp.int32),
            pltpu.SMEM((cap + GROUP,), jnp.int32),
            pltpu.SMEM((cap + GROUP,), jnp.int32),
            pltpu.SMEM((len(blocks),), jnp.int32),
            pltpu.SemaphoreType.DMA((2,)),
            pltpu.SemaphoreType.DMA((2,)),
        ],
        compiler_params=pltpu.CompilerParams(vmem_limit_bytes=58 * 1024 * 1024),
        cost_estimate=pl.CostEstimate(
            flops=WEIGHT * 2 * cap * side * R * R * frames * (width // R),
            bytes_accessed=cap * frames * width * 4, transcendentals=0,
        ),
        name=name,
    )(who, ids, queries, *heads, before, videos, *blocks)


def chip_places(mesh):
    devices = list(mesh.devices.flat)[::2]
    places = [tuple(getattr(d, "coords", ()) or ()) for d in devices]
    if any(len(p) != 3 for p in places):
        return [(i, 0, 0) for i in range(len(devices))]
    return [tuple(reversed(p)) for p in places]


def ring_position(coordinate, size):
    if size <= 2:
        return coordinate
    order = list(range(1, size, 2)) + list(reversed(range(0, size, 2)))
    order = [0] + [c for c in order if c != 0]
    return order.index(coordinate)


class Gather:
    def __init__(self, sizes, steps, queries):
        self.steps = steps
        q_dev = queries.shape[0]
        depth, height, width = sizes
        counts = [q_dev * s // sum(SHARES) for s in SHARES]
        starts = [sum(counts[:r]) for r in range(4)]
        a = counts[0] + counts[1]
        self.blocks, self.cells, self.arrival = {}, {}, {}

        def put(key, array, cells, at):
            self.blocks[key], self.cells[key], self.arrival[key] = array, cells, at

        def moved(cells, axis, k):
            out = []
            for off, q, n in cells:
                off = list(off)
                off[axis] = k
                out.append((tuple(off), q, n))
            return out

        here = (0, 0, 0)
        put(("a", 0), queries[:a], [(here, 0, a)], -1)
        for r in (2, 3):
            put(("b", r), queries[starts[r]:starts[r] + counts[r]], [(here, starts[r], counts[r])], -1)

        self.describe = {}

        def ring(axis, source, name, cells):
            out = []
            for k in range(1, sizes[axis]):
                target = name + (k,)
                self.describe[target] = moved(cells, axis, k)
                out.append((axis, source, target))
                source = target
            return out

        first, second = [], []
        joins = {}
        for r, (p, q) in ((2, (2, 1)), (3, (1, 2))):
            cells = self.cells[("b", r)]
            line = ring(p, ("b", r), ("b", r, "line"), cells)
            first.append(line)
            joins[("b", r, "row")] = [("b", r)] + [m[2] for m in line]
            row = [c for k in range(sizes[p]) for c in moved(cells, p, k)]
            self.describe[("b", r, "row")] = row
            turn = ring(q, ("b", r, "row"), ("b", r, "turn"), row)
            second.append(turn)
            joins[("b", r, "plane")] = [("b", r, "row")] + [m[2] for m in turn]
            self.describe[("b", r, "plane")] = [c for k in range(sizes[q]) for c in moved(row, q, k)]
        joins[("b", 0)] = [("b", 2, "plane"), ("b", 3, "plane")]
        self.describe[("b", 0)] = [c for r in (2, 3) for c in self.describe[("b", r, "plane")]]
        self.joins = joins
        self.halves = {}

        rounds = []
        for k in range(depth):
            for r, (p, q) in ((0, (2, 1)), (1, (1, 2))):
                own = ("a", k, r)
                self.halves[own] = (("a", k), starts[r], counts[r])
                self.describe[own] = [((k, 0, 0), starts[r], counts[r])]
            lists = {1: [], 2: []}
            later = {1: [], 2: []}
            for r, (p, q) in ((0, (2, 1)), (1, (1, 2))):
                own = ("a", k, r)
                line = ring(p, own, ("a", k, r, "line"), self.describe[own])
                lists[p] += line
                for i, source in enumerate([own] + [m[2] for m in line]):
                    later[q] += ring(q, source, ("a", k, r, "turn", i), self.describe[source])
            both = [lists[axis] + later[axis] for axis in (2, 1)]
            for i in range(max(map(len, both))):
                rounds.append([l[i] for l in both if i < len(l)])
        pairs_of = lambda ls: [[l[i] for l in ls if i < len(l)] for i in range(max(map(len, ls)))]
        lead, middle = pairs_of(first), pairs_of(second)

        deep = ring(0, ("a", 0), ("a",), self.cells[("a", 0)]) + ring(
            0, ("b", 0), ("b",), self.describe[("b", 0)]
        )
        gap = max(1, len(rounds) // max(1, len(deep)))
        while len(rounds) < gap * len(deep):
            rounds.append([])
        for i, m in enumerate(deep):
            rounds[i * gap].append(m)
        self.per_plane = len(rounds) // depth
        at = min(2, len(rounds))
        self.rounds = lead + rounds[:at] + middle + rounds[at:]
        self.offset = len(lead) + len(middle)
        for i, messages in enumerate(self.rounds):
            for axis, _, target in messages:
                self.arrival[target] = i if axis else i + gap - 1
                self.cells[target] = self.describe[target]
        self.arrival[("b", 0)] = len(lead) + at + len(middle) - 1
        self.cells[("b", 0)] = self.describe[("b", 0)]

    def block(self, key):
        if key not in self.blocks:
            if key in self.joins:
                self.blocks[key] = jnp.concatenate([self.block(k) for k in self.joins[key]], axis=0)
            else:
                whole, start, n = self.halves[key]
                self.blocks[key] = self.block(whole)[start:start + n]
        return self.blocks[key]

    def buffers(self):
        keys = [k for k in self.arrival if k[0] == "a" and (len(k) == 2 or len(k) > 3)]
        return keys + [k for k in self.arrival if k[0] == "b" and len(k) == 2 and isinstance(k[1], int)]


def body(places, sizes, queries, index_videos, candidates, conv_one, conv_two, conv_three):
    devices = lax.axis_size("shard")
    q_dev, frames, width = queries.shape
    k_count = candidates.shape[1]
    idx_dev = index_videos.shape[0]
    pairs = q_dev * k_count
    chips = devices // 2
    per_holder = max(2, (2 * pairs + devices - 1) // devices)
    me = lax.axis_index("shard")
    chip, core = me // 2, me % 2

    rings = [tuple(ring_position(c, n) for c, n in zip(p, sizes)) for p in places]
    where = {r: i for i, r in enumerate(rings)}

    def step_along(axis):
        out = []
        for i, ring in enumerate(rings):
            to = list(ring)
            to[axis] = (to[axis] + 1) % sizes[axis]
            out += [(2 * i + c, 2 * where[tuple(to)] + c) for c in range(2)]
        return out

    videos = lax.all_gather(
        index_videos, "shard", axis=0, tiled=True,
        axis_index_groups=[[2 * c, 2 * c + 1] for c in range(chips)],
    )
    gather = Gather(sizes, [step_along(a) for a in range(3)], queries)
    rounds = gather.rounds

    total = len(rounds)
    ends = [gather.offset + gather.per_plane * (z + 1) - 1 for z in range(sizes[0] - 1)]
    ends = sorted({e for e in ends if 0 <= e < total - 2} | {total - 2, total - 1})
    phases = [[] for _ in ends]
    for key in gather.buffers():
        phases[next(i for i, e in enumerate(ends) if gather.arrival[key] <= e)].append(key)
    offsets = [(z, y, x) for z in range(sizes[0]) for y in range(sizes[1]) for x in range(sizes[2])]
    back = np.array(
        [[where[tuple((r - o) % n for r, o, n in zip(ring, off, sizes))] for off in offsets]
         for ring in rings], np.int32,
    )
    who = jnp.concatenate(
        [jnp.stack([chip, core]), lax.dynamic_index_in_dim(jnp.asarray(back), chip, 0, keepdims=False)]
    )

    def contents(p):
        packed, bounds, found = [], [0], {}
        for key in phases[p]:
            row = 0
            for off, first, n in gather.cells[key]:
                found[off] = found.get(off, 0) + n
                for q in range(first, first + n):
                    packed.append((offsets.index(off) << 16) + (q << 8) + row)
                    row += 1
            bounds.append(len(packed))
        cap = sum(min(n * k_count, 2 * per_holder) for n in found.values())
        return jnp.asarray(np.array(packed, np.int32)), bounds, -(-cap // HEAD) * HEAD

    state = {}
    heads = head_matrices(conv_one, conv_two, conv_three)
    tables = [jnp.zeros((chips, pairs), jnp.float32)]

    def score():
        p = len(tables) - 1
        tables.append(pair_scores(
            [gather.block(k) for k in phases[p]], videos, who, state["ids"], *contents(p), heads,
            tables[-1], k_count, idx_dev, "phase_" + str(p),
        ))

    done, deep = [], []
    for i, messages in enumerate(rounds):
        behind = list(done[i - 2]) if i >= 2 else []
        if any(axis == 0 for axis, _, _ in messages):
            behind += deep[-1:]
        if len(tables) <= len(ends) and i >= 2:
            if i == min(ends[len(tables) - 1] + 4, total - 1) and ends[len(tables) - 1] <= i - 2:
                score()
                behind.append(tables[-1])
        sent = [gather.block(source) for _, source, _ in messages]
        sent = lax.optimization_barrier((*sent, *behind))[:len(sent)]
        done.append([])
        for (axis, _, target), block in zip(messages, sent):
            gather.blocks[target] = lax.ppermute(block, "shard", gather.steps[axis])
            (done[i] if axis else deep).append(gather.blocks[target])
        if i == 0:
            ids = lax.optimization_barrier((candidates, *done[0]))[0].reshape(1, pairs)
            state["ids"] = lax.all_to_all(
                jnp.broadcast_to(ids, (devices, pairs)), "shard", split_axis=0, concat_axis=0,
                tiled=True,
            )
    while len(tables) <= len(ends):
        score()
    table = jnp.where(jnp.arange(2)[None, :, None] == core, tables[-1][:, None], 0.0)
    scores = lax.all_to_all(
        table.reshape(devices, pairs), "shard", split_axis=0, concat_axis=0, tiled=True
    )
    return jnp.sum(scores, axis=0).reshape(q_dev, k_count)


def solution(mesh):
    places = chip_places(mesh)
    low = [min(p[a] for p in places) for a in range(3)]
    places = [tuple(c - m for c, m in zip(p, low)) for p in places]
    sizes = [max(p[a] for p in places) + 1 for a in range(3)]
    placed = (P("shard", None, None), P("shard", None, None), P("shard", None), P(), P(), P())
    return jax.shard_map(
        functools.partial(body, places, sizes), mesh=mesh, in_specs=placed,
        out_specs=P("shard", None), check_vma=False,
    )
```

```python
import functools
import math

import jax
import jax.numpy as jnp
import numpy as np
from jax import lax
from jax.experimental import pallas as pl
from jax.experimental.pallas import tpu as pltpu
from jax.sharding import PartitionSpec as P

R = 5
GROUP = 16
SHARES = (1, 7, 7, 1)
HEAD = 64
WEIGHT = 8


def dot(a, b):
    return jnp.dot(a, b, preferred_element_type=jnp.float32)


def iota(shape, dim):
    return lax.broadcasted_iota(jnp.int32, shape, dim)


def head_kernel(one_w, two_w, three_w, one_ref, two_ref, three_ref, one_acc, two_acc, three_acc):
    one_acc[...] = jnp.zeros_like(one_acc)
    two_acc[...] = jnp.zeros_like(two_acc)
    three_acc[...] = jnp.zeros_like(three_acc)
    c1, c2 = two_w.shape[1], two_w.shape[2]
    b1, b2 = c1.bit_length() - 1, c2.bit_length() - 1

    def tap(t, _):
        k = lax.div(t, 3) - 1
        l = lax.rem(t, 3) - 1

        n = one_acc.shape[1]
        row, col = iota((64, n), 0), iota((64, n), 1) >> b1
        y = ((col >> 2) & 3) * 2 + ((col >> 5) & 1)
        x = (col & 3) * 2 + ((col >> 4) & 1)
        hit = ((row >> 3) == y + k) & ((row & 7) == x + l)
        spread = ((iota((c1, n), 1) & (c1 - 1)) == iota((c1, n), 0)).astype(jnp.bfloat16)
        val = dot(jnp.broadcast_to(one_w[t], (16, c1)), spread)[:1]
        one_acc[...] = jnp.where(hit, val, one_acc[...])

        n = two_acc.shape[1]
        spread = ((iota((c2, n), 1) & (c2 - 1)) == iota((c2, n), 0)).astype(jnp.bfloat16)
        val = dot(two_w[t], spread)

        def cell(ij, _):
            col = iota((c1, n), 1) >> b2
            y = ((col >> 1) & 1) * 2 + ((col >> 3) & 1)
            x = (col & 1) * 2 + ((col >> 2) & 1)
            hit = (lax.div(ij, 4) == y + k) & (lax.rem(ij, 4) == x + l)
            rows = pl.ds(pl.multiple_of(ij * c1, c1), c1)
            two_acc[rows, :] = jnp.where(hit, val, two_acc[rows, :])
            return 0
        lax.fori_loop(0, 16, cell, 0)

        m, n = three_acc.shape
        pick = ((iota((m, c2), 0) & (c2 - 1)) == iota((m, c2), 1)).astype(jnp.bfloat16)
        val = lax.dot_general(
            pick, jnp.broadcast_to(three_w[t], (128, c2)), (((1,), (1,)), ((), ())),
            preferred_element_type=jnp.float32,
        )[:, :1]
        row, col = iota((m, n), 0) >> b2, iota((m, n), 1)
        y, x = col & 127, col >> 7
        hit = ((row >> 1) == y + k) & ((row & 1) == x + l) & (y < 2)
        three_acc[...] = jnp.where(hit, val, three_acc[...])
        return 0

    lax.fori_loop(0, 9, tap, 0)
    one_ref[...] = one_acc[...].astype(jnp.bfloat16)
    two_ref[...] = two_acc[...].astype(jnp.bfloat16)
    three_ref[...] = three_acc[...].astype(jnp.bfloat16)


def head_matrices(conv_one, conv_two, conv_three):
    c1, c2 = conv_two.shape[1], conv_two.shape[0]
    one_w = conv_one.transpose(2, 3, 1, 0).reshape(9, 1, c1)
    two_w = conv_two.transpose(2, 3, 1, 0).reshape(9, c1, c2)
    three_w = conv_three.transpose(2, 3, 0, 1).reshape(9, 1, c2)
    shapes = [(64, 64 * c1), (16 * c1, 16 * c2), (4 * c2, 256)]
    vmem = pl.BlockSpec(memory_space=pltpu.VMEM)
    return pl.pallas_call(
        head_kernel,
        out_shape=[jax.ShapeDtypeStruct(s, jnp.bfloat16) for s in shapes],
        in_specs=[vmem] * 3,
        out_specs=[vmem] * 3,
        scratch_shapes=[pltpu.VMEM(s, jnp.float32) for s in shapes],
        compiler_params=pltpu.CompilerParams(vmem_limit_bytes=24 * 1024 * 1024),
        cost_estimate=pl.CostEstimate(flops=10**9, bytes_accessed=3 * 10**6, transcendentals=0),
        name="head_matrices",
    )(one_w, two_w, three_w)


def pair_kernel(frames, idx_dev, k_count, bounds, scale, who_ref, ids_ref, queries_ref, one_ref,
                two_ref, three_ref, before_ref, v_hbm, *rest):
    buffers = len(bounds) - 1
    q_hbm, rest = rest[:buffers], rest[buffers:]
    out_ref, q_in, v_in, q_rows, v_rows, maps, scores, list_ref, ends_ref, q_sem, v_sem = rest
    width = v_hbm.shape[2] // R
    side = GROUP * frames
    senders, pairs = out_ref.shape
    chip, core = who_ref[0], who_ref[1]

    chip_videos = 2 * idx_dev
    bits = (chip_videos - 1).bit_length()
    assert chip_videos == 1 << bits and senders * pairs <= 1 << (23 - bits)
    begin = chip * chip_videos
    count = jnp.int32(0)
    for b in range(buffers):
        def one_of(t, n):
            packed = queries_ref[t]
            row, first = packed & 255, ((packed >> 8) & 255) * k_count
            sender = who_ref[2 + (packed >> 16)]
            base = ((sender * pairs + first) << (8 + bits)) + (row << bits)
            line = 2 * sender + core
            for k in range(k_count):
                vid = ids_ref[line, first + k] - begin
                list_ref[n] = base + (k << (8 + bits)) + (vid & (chip_videos - 1))
                n = n + ((vid >> bits) == 0).astype(jnp.int32)
            return n
        count = lax.fori_loop(bounds[b], bounds[b + 1], one_of, count)
        ends_ref[b] = count
    for p in range(GROUP):
        list_ref[count + p] = 0
    groups = (count + GROUP - 1) // GROUP

    def fetch(step, slot):
        first = step * GROUP
        for b in range(buffers):
            low = 0 if b == 0 else jnp.clip(ends_ref[b - 1] - first, 0, GROUP)
            high = GROUP if b == buffers - 1 else jnp.clip(ends_ref[b] - first, 0, GROUP)

            def one_query(p, _):
                pltpu.make_async_copy(
                    q_hbm[b].at[(list_ref[first + p] >> bits) & 255], q_in.at[slot, p],
                    q_sem.at[slot],
                ).start()
                return 0
            lax.fori_loop(low, high, one_query, 0)

        def one_video(p, _):
            vid = list_ref[first + p] & (chip_videos - 1)
            pltpu.make_async_copy(v_hbm.at[vid], v_in.at[slot, p], v_sem.at[slot]).start()
            return 0
        lax.fori_loop(0, GROUP, one_video, 0)

    maps[...] = jnp.zeros_like(maps)

    @pl.when(groups > 0)
    def _():
        fetch(0, 0)

    def step(g, _):
        slot = lax.rem(g, 2)

        @pl.when(g + 1 < groups)
        def _():
            fetch(g + 1, 1 - slot)

        pltpu.make_async_copy(q_in.at[slot], q_in.at[slot], q_sem.at[slot]).wait()
        pltpu.make_async_copy(v_in.at[slot], v_in.at[slot], v_sem.at[slot]).wait()
        for r in range(R):
            cols = pl.ds(r * width, width)
            q_rows[pl.ds(r * side, side), :] = q_in[slot, :, :, cols].reshape(side, width)
            v_rows[pl.ds(r * side, side), :] = v_in[slot, :, :, cols].reshape(side, width)

        sim = lax.dot_general(
            q_rows[...], v_rows[...], (((1,), (1,)), ((), ())), preferred_element_type=jnp.float32
        )
        best = sim[:, :side]
        for s in range(1, R):
            best = jnp.maximum(best, sim[:, s * side:(s + 1) * side])
        total = best[:side]
        for r in range(1, R):
            total = total + best[r * side:(r + 1) * side]
        cells = frames * frames
        same_pair = iota((side, side), 0) // frames == iota((side, side), 1) // frames
        lane, sub = iota((side, cells), 1), iota((side, cells), 0)
        spread = (lane % frames == sub % frames).astype(jnp.bfloat16)
        own_frame = lane // frames == sub % frames
        fold = (iota((GROUP, side), 1) // frames == iota((GROUP, side), 0)).astype(jnp.bfloat16)
        mean = jnp.where(same_pair, total * scale, 0.0).astype(jnp.bfloat16)
        wide = jnp.where(own_frame, dot(mean, spread), 0.0).astype(jnp.bfloat16)
        maps[pl.ds(pl.multiple_of(g * GROUP, GROUP), GROUP), :] = dot(fold, wide)
        return 0

    lax.fori_loop(0, groups, step, 0)

    def pooled(x):
        n = x.shape[1] // 4
        best = x[:, :n]
        for i in range(1, 4):
            best = jnp.maximum(best, x[:, i * n:(i + 1) * n])
        return jnp.maximum(best, 0.0).astype(jnp.bfloat16)

    def head(g, _):
        here = pl.ds(pl.multiple_of(g * HEAD, HEAD), HEAD)
        first = pooled(dot(maps[here, :].astype(jnp.bfloat16), one_ref[...]))
        second = pooled(dot(first, two_ref[...]))
        final = jnp.clip(dot(second, three_ref[...]), -1.0, 1.0)
        best = jnp.maximum(final[:, :128], final[:, 128:])
        scores[here, :] = jnp.broadcast_to((best[:, 0:1] + best[:, 1:2]) * 0.5, (HEAD, pairs))
        return 0

    lax.fori_loop(0, (count + HEAD - 1) // HEAD, head, 0)

    out_ref[...] = before_ref[...]

    def write(i, _):
        entry = list_ref[i] >> (8 + bits)
        at = pl.ds(lax.div(entry, pairs), 1)
        hit = iota((1, pairs), 1) == lax.rem(entry, pairs)
        out_ref[at, :] = jnp.where(hit, scores[pl.ds(i, 1), :], out_ref[at, :])
        return 0

    lax.fori_loop(0, count, write, 0)


def pair_scores(blocks, videos, who, ids, queries, bounds, cap, heads, before, k_count, idx_dev, name):
    frames, width = videos.shape[1], videos.shape[2]
    pairs = before.shape[1]
    side = GROUP * frames
    scale = 1.0 / (math.sqrt(width // R) * R)
    smem = pl.BlockSpec(memory_space=pltpu.SMEM)
    vmem = pl.BlockSpec(memory_space=pltpu.VMEM)
    hbm = pl.BlockSpec(memory_space=pltpu.HBM)
    return pl.pallas_call(
        functools.partial(pair_kernel, frames, idx_dev, k_count, bounds, scale),
        out_shape=jax.ShapeDtypeStruct(before.shape, jnp.float32),
        in_specs=[smem] * 3 + [vmem] * 4 + [hbm] * (1 + len(blocks)),
        out_specs=vmem,
        scratch_shapes=[
            pltpu.VMEM((2, GROUP, frames, width), jnp.bfloat16),
            pltpu.VMEM((2, GROUP, frames, width), jnp.bfloat16),
            pltpu.VMEM((R * side, width // R), jnp.bfloat16),
            pltpu.VMEM((R * side, width // R), jnp.bfloat16),
            pltpu.VMEM((cap, frames * frames), jnp.float32),
            pltpu.VMEM((cap, pairs), jnp.float32),
            pltpu.SMEM((cap + GROUP,), jnp.int32),
            pltpu.SMEM((len(blocks),), jnp.int32),
            pltpu.SemaphoreType.DMA((2,)),
            pltpu.SemaphoreType.DMA((2,)),
        ],
        compiler_params=pltpu.CompilerParams(vmem_limit_bytes=58 * 1024 * 1024),
        cost_estimate=pl.CostEstimate(
            flops=WEIGHT * 2 * cap * side * R * R * frames * (width // R),
            bytes_accessed=cap * frames * width * 4, transcendentals=0,
        ),
        name=name,
    )(who, ids, queries, *heads, before, videos, *blocks)


def chip_places(mesh):
    devices = list(mesh.devices.flat)[::2]
    places = [tuple(getattr(d, "coords", ()) or ()) for d in devices]
    if any(len(p) != 3 for p in places):
        return [(i, 0, 0) for i in range(len(devices))]
    return [tuple(reversed(p)) for p in places]


def ring_position(coordinate, size):
    if size <= 2:
        return coordinate
    order = list(range(1, size, 2)) + list(reversed(range(0, size, 2)))
    order = [0] + [c for c in order if c != 0]
    return order.index(coordinate)


class Gather:
    def __init__(self, sizes, steps, queries):
        self.steps = steps
        q_dev = queries.shape[0]
        depth, height, width = sizes
        b1, a1, a2, b2 = [q_dev * s // sum(SHARES) for s in SHARES]
        here = (0, 0, 0)
        self.blocks = {("a", 0): queries}
        self.cells = {("a", 0): [(here, 0, q_dev)]}
        self.arrival = {("a", 0): -1}
        self.pieces = {("deep",): [(("a", 0), b1, a1 + a2)]}

        def moved(cells, axis, k):
            out = []
            for off, q, n in cells:
                off = list(off)
                off[axis] = k
                out.append((tuple(off), q, n))
            return out

        def ring(axis, source, name, cells):
            out = []
            for k in range(1, sizes[axis]):
                target = name + (k,)
                self.cells[target] = moved(cells, axis, k)
                out.append((axis, source, target))
                source = target
            return out

        deep = ring(0, ("deep",), ("a",), [(here, b1, a1 + a2)])
        rounds = []
        planes = []
        for k in range(depth):
            lists, later = {1: [], 2: []}, {1: [], 2: []}
            for r, (p, q) in ((0, (2, 1)), (1, (1, 2))):
                own = ("half", k, r)
                if k == 0:
                    start, n = (0, b1 + a1) if r == 0 else (b1 + a1, a2 + b2)
                    first = start
                else:
                    start, n = (0, a1) if r == 0 else (a1, a2)
                    first = start + b1
                self.pieces[own] = [(("a", k), start, n)]
                self.cells[own] = [((k, 0, 0), first, n)]
                line = ring(p, own, ("a", k, r, "line"), self.cells[own])
                lists[p] += line
                found = [own] + [m[2] for m in line]
                for i, source in enumerate(list(found)):
                    turn = ring(q, source, ("a", k, r, "turn", i), self.cells[source])
                    later[q] += turn
                    found += [m[2] for m in turn]
                if k == 0:
                    planes += [(key, 0, b1) if r == 0 else (key, a2, b2) for key in found]
            both = [lists[axis] + later[axis] for axis in (2, 1)]
            for i in range(max(map(len, both))):
                rounds.append([l[i] for l in both if i < len(l)])
        self.pieces[("b", 0)] = planes
        cells = [(self.cells[key][0][0], self.cells[key][0][1] + at, n) for key, at, n in planes]
        deep += ring(0, ("b", 0), ("b",), cells)
        gap = max(1, len(rounds) // max(1, len(deep)))
        while len(rounds) < gap * len(deep):
            rounds.append([])
        for i, m in enumerate(deep):
            rounds[i * gap].append(m)
        self.per_plane = len(rounds) // depth
        self.rounds = rounds
        for i, messages in enumerate(rounds):
            for axis, _, target in messages:
                self.arrival[target] = i if axis else i + gap - 1

    def block(self, key):
        if key not in self.blocks:
            parts = [self.block(k)[at:at + n] for k, at, n in self.pieces[key]]
            self.blocks[key] = parts[0] if len(parts) == 1 else jnp.concatenate(parts, axis=0)
        return self.blocks[key]


def body(places, sizes, queries, index_videos, candidates, conv_one, conv_two, conv_three):
    devices = lax.axis_size("shard")
    q_dev, frames, width = queries.shape
    k_count = candidates.shape[1]
    idx_dev = index_videos.shape[0]
    pairs = q_dev * k_count
    chips = devices // 2
    per_holder = max(2, (2 * pairs + devices - 1) // devices)
    me = lax.axis_index("shard")
    chip, core = me // 2, me % 2

    rings = [tuple(ring_position(c, n) for c, n in zip(p, sizes)) for p in places]
    where = {r: i for i, r in enumerate(rings)}

    def step_along(axis):
        out = []
        for i, ring in enumerate(rings):
            to = list(ring)
            to[axis] = (to[axis] + 1) % sizes[axis]
            out += [(2 * i + c, 2 * where[tuple(to)] + c) for c in range(2)]
        return out

    videos = lax.all_gather(
        index_videos, "shard", axis=0, tiled=True,
        axis_index_groups=[[2 * c, 2 * c + 1] for c in range(chips)],
    )
    gather = Gather(sizes, [step_along(a) for a in range(3)], queries)
    rounds = gather.rounds

    total = len(rounds)
    ends = [gather.per_plane * (z + 1) - 1 for z in range(sizes[0] - 1)]
    ends = sorted({e for e in ends if 0 <= e < total - 2} | {total - 2, total - 1})
    phases = [[] for _ in ends]
    for key in gather.arrival:
        phases[next(i for i, e in enumerate(ends) if gather.arrival[key] <= e)].append(key)
    offsets = [(z, y, x) for z in range(sizes[0]) for y in range(sizes[1]) for x in range(sizes[2])]
    back = np.array(
        [[where[tuple((r - o) % n for r, o, n in zip(ring, off, sizes))] for off in offsets]
         for ring in rings], np.int32,
    )
    who = jnp.concatenate(
        [jnp.stack([chip, core]), lax.dynamic_index_in_dim(jnp.asarray(back), chip, 0, keepdims=False)]
    )

    def contents(p):
        packed, bounds, found = [], [0], {}
        for key in phases[p]:
            row = 0
            for off, first, n in gather.cells[key]:
                found[off] = found.get(off, 0) + n
                for q in range(first, first + n):
                    packed.append((offsets.index(off) << 16) + (q << 8) + row)
                    row += 1
            bounds.append(len(packed))
        cap = sum(min(n * k_count, 2 * per_holder) for n in found.values())
        return jnp.asarray(np.array(packed, np.int32)), bounds, -(-cap // HEAD) * HEAD

    state = {}
    heads = head_matrices(conv_one, conv_two, conv_three)
    tables = [jnp.zeros((chips, pairs), jnp.float32)]

    def score():
        p = len(tables) - 1
        tables.append(pair_scores(
            [gather.block(k) for k in phases[p]], videos, who, state["ids"], *contents(p), heads,
            tables[-1], k_count, idx_dev, "phase_" + str(p),
        ))

    done = []
    for i, messages in enumerate(rounds):
        behind = list(done[i - 2]) if i >= 2 else []
        if len(tables) <= len(ends) and i >= 2:
            if i == min(ends[len(tables) - 1] + 4, total - 1) and ends[len(tables) - 1] <= i - 2:
                score()
                behind.append(tables[-1])
        done.append([])
        for together in ([m for m in messages if m[0]], [m for m in messages if not m[0]]):
            sent = [gather.block(source) for _, source, _ in together]
            sent = lax.optimization_barrier((*sent, *behind))[:len(sent)] if sent else []
            for (axis, _, target), block in zip(together, sent):
                gather.blocks[target] = lax.ppermute(block, "shard", gather.steps[axis])
                if axis:
                    done[i].append(gather.blocks[target])
        if i == 0:
            ids = lax.optimization_barrier((candidates, *done[0]))[0].reshape(1, pairs)
            state["ids"] = lax.all_to_all(
                jnp.broadcast_to(ids, (devices, pairs)), "shard", split_axis=0, concat_axis=0,
                tiled=True,
            )
    while len(tables) <= len(ends):
        score()
    table = jnp.where(jnp.arange(2)[None, :, None] == core, tables[-1][:, None], 0.0)
    scores = lax.all_to_all(
        table.reshape(devices, pairs), "shard", split_axis=0, concat_axis=0, tiled=True
    )
    return jnp.sum(scores, axis=0).reshape(q_dev, k_count)


def solution(mesh):
    places = chip_places(mesh)
    low = [min(p[a] for p in places) for a in range(3)]
    places = [tuple(c - m for c, m in zip(p, low)) for p in places]
    sizes = [max(p[a] for p in places) + 1 for a in range(3)]
    placed = (P("shard", None, None), P("shard", None, None), P("shard", None), P(), P(), P())
    return jax.shard_map(
        functools.partial(body, places, sizes), mesh=mesh, in_specs=placed,
        out_specs=P("shard", None), check_vma=False,
    )
```

```python
import functools
import math

import jax
import jax.numpy as jnp
import numpy as np
from jax import lax
from jax.experimental import pallas as pl
from jax.experimental.pallas import tpu as pltpu
from jax.sharding import PartitionSpec as P

R = 5
GROUP = 16
SHARES = (1, 7, 6, 2)
HEAD = 64
LATER = 4
WEIGHT = 8


def dot(a, b):
    return jnp.dot(a, b, preferred_element_type=jnp.float32)


def iota(shape, dim):
    return lax.broadcasted_iota(jnp.int32, shape, dim)


def head_kernel(one_w, two_w, three_w, one_ref, two_ref, three_ref, one_acc, two_acc, three_acc):
    one_acc[...] = jnp.zeros_like(one_acc)
    two_acc[...] = jnp.zeros_like(two_acc)
    three_acc[...] = jnp.zeros_like(three_acc)
    c1, c2 = two_w.shape[1], two_w.shape[2]
    b1, b2 = c1.bit_length() - 1, c2.bit_length() - 1

    def tap(t, _):
        k = lax.div(t, 3) - 1
        l = lax.rem(t, 3) - 1

        n = one_acc.shape[1]
        row, col = iota((64, n), 0), iota((64, n), 1) >> b1
        y = ((col >> 2) & 3) * 2 + ((col >> 5) & 1)
        x = (col & 3) * 2 + ((col >> 4) & 1)
        hit = ((row >> 3) == y + k) & ((row & 7) == x + l)
        spread = ((iota((c1, n), 1) & (c1 - 1)) == iota((c1, n), 0)).astype(jnp.bfloat16)
        val = dot(jnp.broadcast_to(one_w[t], (16, c1)), spread)[:1]
        one_acc[...] = jnp.where(hit, val, one_acc[...])

        n = two_acc.shape[1]
        spread = ((iota((c2, n), 1) & (c2 - 1)) == iota((c2, n), 0)).astype(jnp.bfloat16)
        val = dot(two_w[t], spread)

        def cell(ij, _):
            col = iota((c1, n), 1) >> b2
            y = ((col >> 1) & 1) * 2 + ((col >> 3) & 1)
            x = (col & 1) * 2 + ((col >> 2) & 1)
            hit = (lax.div(ij, 4) == y + k) & (lax.rem(ij, 4) == x + l)
            rows = pl.ds(pl.multiple_of(ij * c1, c1), c1)
            two_acc[rows, :] = jnp.where(hit, val, two_acc[rows, :])
            return 0
        lax.fori_loop(0, 16, cell, 0)

        m, n = three_acc.shape
        pick = ((iota((m, c2), 0) & (c2 - 1)) == iota((m, c2), 1)).astype(jnp.bfloat16)
        val = lax.dot_general(
            pick, jnp.broadcast_to(three_w[t], (128, c2)), (((1,), (1,)), ((), ())),
            preferred_element_type=jnp.float32,
        )[:, :1]
        row, col = iota((m, n), 0) >> b2, iota((m, n), 1)
        y, x = col & 127, col >> 7
        hit = ((row >> 1) == y + k) & ((row & 1) == x + l) & (y < 2)
        three_acc[...] = jnp.where(hit, val, three_acc[...])
        return 0

    lax.fori_loop(0, 9, tap, 0)
    one_ref[...] = one_acc[...].astype(jnp.bfloat16)
    two_ref[...] = two_acc[...].astype(jnp.bfloat16)
    three_ref[...] = three_acc[...].astype(jnp.bfloat16)


def head_matrices(conv_one, conv_two, conv_three):
    c1, c2 = conv_two.shape[1], conv_two.shape[0]
    one_w = conv_one.transpose(2, 3, 1, 0).reshape(9, 1, c1)
    two_w = conv_two.transpose(2, 3, 1, 0).reshape(9, c1, c2)
    three_w = conv_three.transpose(2, 3, 0, 1).reshape(9, 1, c2)
    shapes = [(64, 64 * c1), (16 * c1, 16 * c2), (4 * c2, 256)]
    vmem = pl.BlockSpec(memory_space=pltpu.VMEM)
    return pl.pallas_call(
        head_kernel,
        out_shape=[jax.ShapeDtypeStruct(s, jnp.bfloat16) for s in shapes],
        in_specs=[vmem] * 3,
        out_specs=[vmem] * 3,
        scratch_shapes=[pltpu.VMEM(s, jnp.float32) for s in shapes],
        compiler_params=pltpu.CompilerParams(vmem_limit_bytes=24 * 1024 * 1024),
        cost_estimate=pl.CostEstimate(flops=10**9, bytes_accessed=3 * 10**6, transcendentals=0),
        name="head_matrices",
    )(one_w, two_w, three_w)


def pair_kernel(frames, idx_dev, k_count, bounds, scale, who_ref, ids_ref, queries_ref, one_ref,
                two_ref, three_ref, before_ref, v_hbm, *rest):
    buffers = len(bounds) - 1
    q_hbm, rest = rest[:buffers], rest[buffers:]
    out_ref, q_in, v_in, q_rows, v_rows, maps, scores, list_ref, ends_ref, q_sem, v_sem = rest
    width = v_hbm.shape[2] // R
    side = GROUP * frames
    senders, pairs = out_ref.shape
    chip, core = who_ref[0], who_ref[1]

    chip_videos = 2 * idx_dev
    bits = (chip_videos - 1).bit_length()
    assert chip_videos == 1 << bits and senders * pairs <= 1 << (23 - bits)
    begin = chip * chip_videos
    count = jnp.int32(0)
    for b in range(buffers):
        def one_of(t, n):
            packed = queries_ref[t]
            row, first = packed & 255, ((packed >> 8) & 255) * k_count
            sender = who_ref[2 + (packed >> 16)]
            base = ((sender * pairs + first) << (8 + bits)) + (row << bits)
            line = 2 * sender + core
            for k in range(k_count):
                vid = ids_ref[line, first + k] - begin
                list_ref[n] = base + (k << (8 + bits)) + (vid & (chip_videos - 1))
                n = n + ((vid >> bits) == 0).astype(jnp.int32)
            return n
        count = lax.fori_loop(bounds[b], bounds[b + 1], one_of, count)
        ends_ref[b] = count
    for p in range(GROUP):
        list_ref[count + p] = 0
    groups = (count + GROUP - 1) // GROUP

    def fetch(step, slot):
        first = step * GROUP
        for b in range(buffers):
            low = 0 if b == 0 else jnp.clip(ends_ref[b - 1] - first, 0, GROUP)
            high = GROUP if b == buffers - 1 else jnp.clip(ends_ref[b] - first, 0, GROUP)

            def one_query(p, _):
                pltpu.make_async_copy(
                    q_hbm[b].at[(list_ref[first + p] >> bits) & 255], q_in.at[slot, p],
                    q_sem.at[slot],
                ).start()
                return 0
            lax.fori_loop(low, high, one_query, 0)

        def one_video(p, _):
            vid = list_ref[first + p] & (chip_videos - 1)
            pltpu.make_async_copy(v_hbm.at[vid], v_in.at[slot, p], v_sem.at[slot]).start()
            return 0
        lax.fori_loop(0, GROUP, one_video, 0)

    maps[...] = jnp.zeros_like(maps)

    @pl.when(groups > 0)
    def _():
        fetch(0, 0)

    def step(g, _):
        slot = lax.rem(g, 2)

        @pl.when(g + 1 < groups)
        def _():
            fetch(g + 1, 1 - slot)

        pltpu.make_async_copy(q_in.at[slot], q_in.at[slot], q_sem.at[slot]).wait()
        pltpu.make_async_copy(v_in.at[slot], v_in.at[slot], v_sem.at[slot]).wait()
        for r in range(R):
            cols = pl.ds(r * width, width)
            q_rows[pl.ds(r * side, side), :] = q_in[slot, :, :, cols].reshape(side, width)
            v_rows[pl.ds(r * side, side), :] = v_in[slot, :, :, cols].reshape(side, width)

        sim = lax.dot_general(
            q_rows[...], v_rows[...], (((1,), (1,)), ((), ())), preferred_element_type=jnp.float32
        )
        best = sim[:, :side]
        for s in range(1, R):
            best = jnp.maximum(best, sim[:, s * side:(s + 1) * side])
        total = best[:side]
        for r in range(1, R):
            total = total + best[r * side:(r + 1) * side]
        cells = frames * frames
        same_pair = iota((side, side), 0) // frames == iota((side, side), 1) // frames
        lane, sub = iota((side, cells), 1), iota((side, cells), 0)
        spread = (lane % frames == sub % frames).astype(jnp.bfloat16)
        own_frame = lane // frames == sub % frames
        fold = (iota((GROUP, side), 1) // frames == iota((GROUP, side), 0)).astype(jnp.bfloat16)
        mean = jnp.where(same_pair, total * scale, 0.0).astype(jnp.bfloat16)
        wide = jnp.where(own_frame, dot(mean, spread), 0.0).astype(jnp.bfloat16)
        maps[pl.ds(pl.multiple_of(g * GROUP, GROUP), GROUP), :] = dot(fold, wide)
        return 0

    lax.fori_loop(0, groups, step, 0)

    def pooled(x):
        n = x.shape[1] // 4
        best = x[:, :n]
        for i in range(1, 4):
            best = jnp.maximum(best, x[:, i * n:(i + 1) * n])
        return jnp.maximum(best, 0.0).astype(jnp.bfloat16)

    def head(g, _):
        here = pl.ds(pl.multiple_of(g * HEAD, HEAD), HEAD)
        first = pooled(dot(maps[here, :].astype(jnp.bfloat16), one_ref[...]))
        second = pooled(dot(first, two_ref[...]))
        final = jnp.clip(dot(second, three_ref[...]), -1.0, 1.0)
        best = jnp.maximum(final[:, :128], final[:, 128:])
        scores[here, :] = jnp.broadcast_to((best[:, 0:1] + best[:, 1:2]) * 0.5, (HEAD, pairs))
        return 0

    lax.fori_loop(0, (count + HEAD - 1) // HEAD, head, 0)

    out_ref[...] = before_ref[...]

    def write(i, _):
        entry = list_ref[i] >> (8 + bits)
        at = pl.ds(lax.div(entry, pairs), 1)
        hit = iota((1, pairs), 1) == lax.rem(entry, pairs)
        out_ref[at, :] = jnp.where(hit, scores[pl.ds(i, 1), :], out_ref[at, :])
        return 0

    lax.fori_loop(0, count, write, 0)


def pair_scores(blocks, videos, who, ids, queries, bounds, cap, heads, before, k_count, idx_dev, name):
    frames, width = videos.shape[1], videos.shape[2]
    pairs = before.shape[1]
    side = GROUP * frames
    scale = 1.0 / (math.sqrt(width // R) * R)
    smem = pl.BlockSpec(memory_space=pltpu.SMEM)
    vmem = pl.BlockSpec(memory_space=pltpu.VMEM)
    hbm = pl.BlockSpec(memory_space=pltpu.HBM)
    return pl.pallas_call(
        functools.partial(pair_kernel, frames, idx_dev, k_count, bounds, scale),
        out_shape=jax.ShapeDtypeStruct(before.shape, jnp.float32),
        in_specs=[smem] * 3 + [vmem] * 4 + [hbm] * (1 + len(blocks)),
        out_specs=vmem,
        scratch_shapes=[
            pltpu.VMEM((2, GROUP, frames, width), jnp.bfloat16),
            pltpu.VMEM((2, GROUP, frames, width), jnp.bfloat16),
            pltpu.VMEM((R * side, width // R), jnp.bfloat16),
            pltpu.VMEM((R * side, width // R), jnp.bfloat16),
            pltpu.VMEM((cap, frames * frames), jnp.float32),
            pltpu.VMEM((cap, pairs), jnp.float32),
            pltpu.SMEM((cap + GROUP,), jnp.int32),
            pltpu.SMEM((len(blocks),), jnp.int32),
            pltpu.SemaphoreType.DMA((2,)),
            pltpu.SemaphoreType.DMA((2,)),
        ],
        compiler_params=pltpu.CompilerParams(vmem_limit_bytes=58 * 1024 * 1024),
        cost_estimate=pl.CostEstimate(
            flops=WEIGHT * 2 * cap * side * R * R * frames * (width // R),
            bytes_accessed=cap * frames * width * 4, transcendentals=0,
        ),
        name=name,
    )(who, ids, queries, *heads, before, videos, *blocks)


def chip_places(mesh):
    devices = list(mesh.devices.flat)[::2]
    places = [tuple(getattr(d, "coords", ()) or ()) for d in devices]
    if any(len(p) != 3 for p in places):
        return [(i, 0, 0) for i in range(len(devices))]
    return [tuple(reversed(p)) for p in places]


def ring_position(coordinate, size):
    if size <= 2:
        return coordinate
    order = list(range(1, size, 2)) + list(reversed(range(0, size, 2)))
    order = [0] + [c for c in order if c != 0]
    return order.index(coordinate)


class Gather:
    def __init__(self, sizes, steps, queries):
        self.steps = steps
        q_dev = queries.shape[0]
        depth, height, width = sizes
        b1, a1, a2, b2 = [q_dev * s // sum(SHARES) for s in SHARES]
        here = (0, 0, 0)
        self.blocks = {("a", 0): queries}
        self.cells = {("a", 0): [(here, 0, q_dev)]}
        self.arrival = {("a", 0): -1}
        self.pieces = {("deep",): [(("a", 0), b1, a1 + a2)]}

        def moved(cells, axis, k):
            out = []
            for off, q, n in cells:
                off = list(off)
                off[axis] = k
                out.append((tuple(off), q, n))
            return out

        def ring(axis, source, name, cells):
            out = []
            for k in range(1, sizes[axis]):
                target = name + (k,)
                self.cells[target] = moved(cells, axis, k)
                out.append((axis, source, target))
                source = target
            return out

        deep = ring(0, ("deep",), ("a",), [(here, b1, a1 + a2)])
        rounds = []
        planes = []
        for k in range(depth):
            lists, later = {1: [], 2: []}, {1: [], 2: []}
            for r, (p, q) in ((0, (2, 1)), (1, (1, 2))):
                own = ("half", k, r)
                if k == 0:
                    start, n = (0, b1 + a1) if r == 0 else (b1 + a1, a2 + b2)
                    first = start
                else:
                    start, n = (0, a1) if r == 0 else (a1, a2)
                    first = start + b1
                self.pieces[own] = [(("a", k), start, n)]
                self.cells[own] = [((k, 0, 0), first, n)]
                line = ring(p, own, ("a", k, r, "line"), self.cells[own])
                lists[p] += line
                found = [own] + [m[2] for m in line]
                for i, source in enumerate(list(found)):
                    turn = ring(q, source, ("a", k, r, "turn", i), self.cells[source])
                    later[q] += turn
                    found += [m[2] for m in turn]
                if k == 0:
                    planes += [(key, 0, b1) if r == 0 else (key, a2, b2) for key in found]
            both = [lists[axis] + later[axis] for axis in (2, 1)]
            for i in range(max(map(len, both))):
                rounds.append([l[i] for l in both if i < len(l)])
        self.pieces[("b", 0)] = planes
        cells = [(self.cells[key][0][0], self.cells[key][0][1] + at, n) for key, at, n in planes]
        deep += ring(0, ("b", 0), ("b",), cells)
        gap = max(1, len(rounds) // max(1, len(deep)))
        while len(rounds) < gap * len(deep):
            rounds.append([])
        for i, m in enumerate(deep):
            rounds[i * gap].append(m)
        self.per_plane = len(rounds) // depth
        self.rounds = rounds
        for i, messages in enumerate(rounds):
            for axis, _, target in messages:
                self.arrival[target] = i if axis else i + gap - 1

    def block(self, key):
        if key not in self.blocks:
            parts = [self.block(k)[at:at + n] for k, at, n in self.pieces[key]]
            self.blocks[key] = parts[0] if len(parts) == 1 else jnp.concatenate(parts, axis=0)
        return self.blocks[key]


def body(places, sizes, queries, index_videos, candidates, conv_one, conv_two, conv_three):
    devices = lax.axis_size("shard")
    q_dev, frames, width = queries.shape
    k_count = candidates.shape[1]
    idx_dev = index_videos.shape[0]
    pairs = q_dev * k_count
    chips = devices // 2
    per_holder = max(2, (2 * pairs + devices - 1) // devices)
    me = lax.axis_index("shard")
    chip, core = me // 2, me % 2

    rings = [tuple(ring_position(c, n) for c, n in zip(p, sizes)) for p in places]
    where = {r: i for i, r in enumerate(rings)}

    def step_along(axis):
        out = []
        for i, ring in enumerate(rings):
            to = list(ring)
            to[axis] = (to[axis] + 1) % sizes[axis]
            out += [(2 * i + c, 2 * where[tuple(to)] + c) for c in range(2)]
        return out

    videos = lax.all_gather(
        index_videos, "shard", axis=0, tiled=True,
        axis_index_groups=[[2 * c, 2 * c + 1] for c in range(chips)],
    )
    gather = Gather(sizes, [step_along(a) for a in range(3)], queries)
    rounds = gather.rounds

    total = len(rounds)
    ends = [gather.per_plane * (z + 1) - 1 for z in range(sizes[0] - 1)]
    ends = sorted({e for e in ends if 0 <= e < total - 2} | {total - 2, total - 1})
    phases = [[] for _ in ends]
    for key in gather.arrival:
        phases[next(i for i, e in enumerate(ends) if gather.arrival[key] <= e)].append(key)
    offsets = [(z, y, x) for z in range(sizes[0]) for y in range(sizes[1]) for x in range(sizes[2])]
    back = np.array(
        [[where[tuple((r - o) % n for r, o, n in zip(ring, off, sizes))] for off in offsets]
         for ring in rings], np.int32,
    )
    who = jnp.concatenate(
        [jnp.stack([chip, core]), lax.dynamic_index_in_dim(jnp.asarray(back), chip, 0, keepdims=False)]
    )

    def contents(p):
        packed, bounds, found = [], [0], {}
        for key in phases[p]:
            row = 0
            for off, first, n in gather.cells[key]:
                found[off] = found.get(off, 0) + n
                for q in range(first, first + n):
                    packed.append((offsets.index(off) << 16) + (q << 8) + row)
                    row += 1
            bounds.append(len(packed))
        cap = sum(min(n * k_count, 2 * per_holder) for n in found.values())
        return jnp.asarray(np.array(packed, np.int32)), bounds, -(-cap // HEAD) * HEAD

    state = {}
    heads = head_matrices(conv_one, conv_two, conv_three)
    tables = [jnp.zeros((chips, pairs), jnp.float32)]

    def score():
        p = len(tables) - 1
        tables.append(pair_scores(
            [gather.block(k) for k in phases[p]], videos, who, state["ids"], *contents(p), heads,
            tables[-1], k_count, idx_dev, "phase_" + str(p),
        ))

    done = []
    for i, messages in enumerate(rounds):
        behind = list(done[i - 2]) if i >= 2 else []
        if len(tables) <= len(ends) and i >= 2:
            if i == min(ends[len(tables) - 1] + LATER, total - 1) and ends[len(tables) - 1] <= i - 2:
                score()
                behind.append(tables[-1])
        done.append([])
        for together in ([m for m in messages if m[0]], [m for m in messages if not m[0]]):
            sent = [gather.block(source) for _, source, _ in together]
            sent = lax.optimization_barrier((*sent, *behind))[:len(sent)] if sent else []
            for (axis, _, target), block in zip(together, sent):
                gather.blocks[target] = lax.ppermute(block, "shard", gather.steps[axis])
                if axis:
                    done[i].append(gather.blocks[target])
        if i == 0:
            ids = lax.optimization_barrier((candidates, *done[0]))[0].reshape(1, pairs)
            state["ids"] = lax.all_to_all(
                jnp.broadcast_to(ids, (devices, pairs)), "shard", split_axis=0, concat_axis=0,
                tiled=True,
            )
    while len(tables) <= len(ends):
        score()
    table = jnp.where(jnp.arange(2)[None, :, None] == core, tables[-1][:, None], 0.0)
    scores = lax.all_to_all(
        table.reshape(devices, pairs), "shard", split_axis=0, concat_axis=0, tiled=True
    )
    return jnp.sum(scores, axis=0).reshape(q_dev, k_count)


def solution(mesh):
    places = chip_places(mesh)
    low = [min(p[a] for p in places) for a in range(3)]
    places = [tuple(c - m for c, m in zip(p, low)) for p in places]
    sizes = [max(p[a] for p in places) + 1 for a in range(3)]
    placed = (P("shard", None, None), P("shard", None, None), P("shard", None), P(), P(), P())
    return jax.shard_map(
        functools.partial(body, places, sizes), mesh=mesh, in_specs=placed,
        out_specs=P("shard", None), check_vma=False,
    )
```

```python
import functools
import math

import jax
import jax.numpy as jnp
import numpy as np
from jax import lax
from jax.experimental import pallas as pl
from jax.experimental.pallas import tpu as pltpu
from jax.sharding import PartitionSpec as P

R = 5
GROUP = 16
SHARES = (1, 7, 6, 2)
HEAD = 64
LATER = 4
WEIGHT = 8


def dot(a, b):
    return jnp.dot(a, b, preferred_element_type=jnp.float32)


def iota(shape, dim):
    return lax.broadcasted_iota(jnp.int32, shape, dim)


def head_kernel(one_w, two_w, three_w, one_ref, two_ref, three_ref, one_acc, two_acc, three_acc):
    one_acc[...] = jnp.zeros_like(one_acc)
    two_acc[...] = jnp.zeros_like(two_acc)
    three_acc[...] = jnp.zeros_like(three_acc)
    c1, c2 = two_w.shape[1], two_w.shape[2]
    b1, b2 = c1.bit_length() - 1, c2.bit_length() - 1

    def tap(t, _):
        k = lax.div(t, 3) - 1
        l = lax.rem(t, 3) - 1

        n = one_acc.shape[1]
        row, col = iota((64, n), 0), iota((64, n), 1) >> b1
        y = ((col >> 2) & 3) * 2 + ((col >> 5) & 1)
        x = (col & 3) * 2 + ((col >> 4) & 1)
        hit = ((row >> 3) == y + k) & ((row & 7) == x + l)
        spread = ((iota((c1, n), 1) & (c1 - 1)) == iota((c1, n), 0)).astype(jnp.bfloat16)
        val = dot(jnp.broadcast_to(one_w[t], (16, c1)), spread)[:1]
        one_acc[...] = jnp.where(hit, val, one_acc[...])

        n = two_acc.shape[1]
        spread = ((iota((c2, n), 1) & (c2 - 1)) == iota((c2, n), 0)).astype(jnp.bfloat16)
        val = dot(two_w[t], spread)

        def cell(ij, _):
            col = iota((c1, n), 1) >> b2
            y = ((col >> 1) & 1) * 2 + ((col >> 3) & 1)
            x = (col & 1) * 2 + ((col >> 2) & 1)
            hit = (lax.div(ij, 4) == y + k) & (lax.rem(ij, 4) == x + l)
            rows = pl.ds(pl.multiple_of(ij * c1, c1), c1)
            two_acc[rows, :] = jnp.where(hit, val, two_acc[rows, :])
            return 0
        lax.fori_loop(0, 16, cell, 0)

        m, n = three_acc.shape
        pick = ((iota((m, c2), 0) & (c2 - 1)) == iota((m, c2), 1)).astype(jnp.bfloat16)
        val = lax.dot_general(
            pick, jnp.broadcast_to(three_w[t], (128, c2)), (((1,), (1,)), ((), ())),
            preferred_element_type=jnp.float32,
        )[:, :1]
        row, col = iota((m, n), 0) >> b2, iota((m, n), 1)
        y, x = col & 127, col >> 7
        hit = ((row >> 1) == y + k) & ((row & 1) == x + l) & (y < 2)
        three_acc[...] = jnp.where(hit, val, three_acc[...])
        return 0

    lax.fori_loop(0, 9, tap, 0)
    one_ref[...] = one_acc[...].astype(jnp.bfloat16)
    two_ref[...] = two_acc[...].astype(jnp.bfloat16)
    three_ref[...] = three_acc[...].astype(jnp.bfloat16)


def head_matrices(conv_one, conv_two, conv_three):
    c1, c2 = conv_two.shape[1], conv_two.shape[0]
    one_w = conv_one.transpose(2, 3, 1, 0).reshape(9, 1, c1)
    two_w = conv_two.transpose(2, 3, 1, 0).reshape(9, c1, c2)
    three_w = conv_three.transpose(2, 3, 0, 1).reshape(9, 1, c2)
    shapes = [(64, 64 * c1), (16 * c1, 16 * c2), (4 * c2, 256)]
    vmem = pl.BlockSpec(memory_space=pltpu.VMEM)
    return pl.pallas_call(
        head_kernel,
        out_shape=[jax.ShapeDtypeStruct(s, jnp.bfloat16) for s in shapes],
        in_specs=[vmem] * 3,
        out_specs=[vmem] * 3,
        scratch_shapes=[pltpu.VMEM(s, jnp.float32) for s in shapes],
        compiler_params=pltpu.CompilerParams(vmem_limit_bytes=24 * 1024 * 1024),
        cost_estimate=pl.CostEstimate(flops=10**9, bytes_accessed=3 * 10**6, transcendentals=0),
        name="head_matrices",
    )(one_w, two_w, three_w)


def pair_kernel(frames, idx_dev, k_count, bounds, scale, who_ref, ids_ref, queries_ref, before_ref,
                one_hbm, two_hbm, three_hbm, own_hbm, other_hbm, *rest):
    buffers = len(bounds) - 1
    q_hbm, rest = rest[:buffers], rest[buffers:]
    (out_ref, q_in, v_in, q_rows, v_rows, maps, scores, one_ref, two_ref, three_ref, list_ref,
     ends_ref, q_sem, v_sem, head_sem) = rest
    heads = [
        pltpu.make_async_copy(a, b, head_sem.at[i])
        for i, (a, b) in enumerate(zip((one_hbm, two_hbm, three_hbm), (one_ref, two_ref, three_ref)))
    ]
    for copy in heads:
        copy.start()
    width = own_hbm.shape[2] // R
    side = GROUP * frames
    senders, pairs = out_ref.shape
    chip, core = who_ref[0], who_ref[1]

    chip_videos = 2 * idx_dev
    bits = (chip_videos - 1).bit_length()
    assert chip_videos == 1 << bits and senders * pairs <= 1 << (23 - bits)
    begin = chip * chip_videos
    turn = core * idx_dev
    count = jnp.int32(0)
    for b in range(buffers):
        def one_of(t, n):
            packed = queries_ref[t]
            row, first = packed & 255, ((packed >> 8) & 255) * k_count
            sender = who_ref[2 + (packed >> 16)]
            base = ((sender * pairs + first) << (8 + bits)) + (row << bits)
            line = 2 * sender + core
            for k in range(k_count):
                vid = ids_ref[line, first + k] - begin
                list_ref[n] = base + (k << (8 + bits)) + ((vid & (chip_videos - 1)) ^ turn)
                n = n + ((vid >> bits) == 0).astype(jnp.int32)
            return n
        count = lax.fori_loop(bounds[b], bounds[b + 1], one_of, count)
        ends_ref[b] = count
    for p in range(GROUP):
        list_ref[count + p] = 0
    groups = (count + GROUP - 1) // GROUP

    def fetch(step, slot):
        first = step * GROUP
        for b in range(buffers):
            low = 0 if b == 0 else jnp.clip(ends_ref[b - 1] - first, 0, GROUP)
            high = GROUP if b == buffers - 1 else jnp.clip(ends_ref[b] - first, 0, GROUP)

            def one_query(p, _):
                pltpu.make_async_copy(
                    q_hbm[b].at[(list_ref[first + p] >> bits) & 255], q_in.at[slot, p],
                    q_sem.at[slot],
                ).start()
                return 0
            lax.fori_loop(low, high, one_query, 0)

        def one_video(p, _):
            vid = list_ref[first + p] & (chip_videos - 1)

            @pl.when(vid < idx_dev)
            def _():
                pltpu.make_async_copy(own_hbm.at[vid], v_in.at[slot, p], v_sem.at[slot]).start()

            @pl.when(vid >= idx_dev)
            def _():
                pltpu.make_async_copy(
                    other_hbm.at[vid - idx_dev], v_in.at[slot, p], v_sem.at[slot]
                ).start()
            return 0
        lax.fori_loop(0, GROUP, one_video, 0)

    maps[...] = jnp.zeros_like(maps)

    @pl.when(groups > 0)
    def _():
        fetch(0, 0)

    def step(g, _):
        slot = lax.rem(g, 2)

        @pl.when(g + 1 < groups)
        def _():
            fetch(g + 1, 1 - slot)

        pltpu.make_async_copy(q_in.at[slot], q_in.at[slot], q_sem.at[slot]).wait()
        pltpu.make_async_copy(v_in.at[slot], v_in.at[slot], v_sem.at[slot]).wait()
        for r in range(R):
            cols = pl.ds(r * width, width)
            q_rows[pl.ds(r * side, side), :] = q_in[slot, :, :, cols].reshape(side, width)
            v_rows[pl.ds(r * side, side), :] = v_in[slot, :, :, cols].reshape(side, width)

        sim = lax.dot_general(
            q_rows[...], v_rows[...], (((1,), (1,)), ((), ())), preferred_element_type=jnp.float32
        )
        best = sim[:, :side]
        for s in range(1, R):
            best = jnp.maximum(best, sim[:, s * side:(s + 1) * side])
        total = best[:side]
        for r in range(1, R):
            total = total + best[r * side:(r + 1) * side]
        cells = frames * frames
        same_pair = iota((side, side), 0) // frames == iota((side, side), 1) // frames
        lane, sub = iota((side, cells), 1), iota((side, cells), 0)
        spread = (lane % frames == sub % frames).astype(jnp.bfloat16)
        own_frame = lane // frames == sub % frames
        fold = (iota((GROUP, side), 1) // frames == iota((GROUP, side), 0)).astype(jnp.bfloat16)
        mean = jnp.where(same_pair, total * scale, 0.0).astype(jnp.bfloat16)
        wide = jnp.where(own_frame, dot(mean, spread), 0.0).astype(jnp.bfloat16)
        maps[pl.ds(pl.multiple_of(g * GROUP, GROUP), GROUP), :] = dot(fold, wide)
        return 0

    lax.fori_loop(0, groups, step, 0)

    def pooled(x):
        n = x.shape[1] // 4
        best = x[:, :n]
        for i in range(1, 4):
            best = jnp.maximum(best, x[:, i * n:(i + 1) * n])
        return jnp.maximum(best, 0.0).astype(jnp.bfloat16)

    for copy in heads:
        copy.wait()

    def head(g, _):
        here = pl.ds(pl.multiple_of(g * HEAD, HEAD), HEAD)
        first = pooled(dot(maps[here, :].astype(jnp.bfloat16), one_ref[...]))
        second = pooled(dot(first, two_ref[...]))
        final = jnp.clip(dot(second, three_ref[...]), -1.0, 1.0)
        best = jnp.maximum(final[:, :128], final[:, 128:])
        scores[here, :] = jnp.broadcast_to((best[:, 0:1] + best[:, 1:2]) * 0.5, (HEAD, pairs))
        return 0

    lax.fori_loop(0, (count + HEAD - 1) // HEAD, head, 0)

    out_ref[...] = before_ref[...]

    def write(i, _):
        entry = list_ref[i] >> (8 + bits)
        at = pl.ds(lax.div(entry, pairs), 1)
        hit = iota((1, pairs), 1) == lax.rem(entry, pairs)
        out_ref[at, :] = jnp.where(hit, scores[pl.ds(i, 1), :], out_ref[at, :])
        return 0

    lax.fori_loop(0, count, write, 0)


def pair_scores(blocks, own, other, who, ids, queries, bounds, cap, heads, before, k_count, idx_dev, name):
    frames, width = own.shape[1], own.shape[2]
    pairs = before.shape[1]
    side = GROUP * frames
    scale = 1.0 / (math.sqrt(width // R) * R)
    smem = pl.BlockSpec(memory_space=pltpu.SMEM)
    vmem = pl.BlockSpec(memory_space=pltpu.VMEM)
    hbm = pl.BlockSpec(memory_space=pltpu.HBM)
    return pl.pallas_call(
        functools.partial(pair_kernel, frames, idx_dev, k_count, bounds, scale),
        out_shape=jax.ShapeDtypeStruct(before.shape, jnp.float32),
        in_specs=[smem] * 3 + [vmem] + [hbm] * (5 + len(blocks)),
        out_specs=vmem,
        scratch_shapes=[
            pltpu.VMEM((2, GROUP, frames, width), jnp.bfloat16),
            pltpu.VMEM((2, GROUP, frames, width), jnp.bfloat16),
            pltpu.VMEM((R * side, width // R), jnp.bfloat16),
            pltpu.VMEM((R * side, width // R), jnp.bfloat16),
            pltpu.VMEM((cap, frames * frames), jnp.float32),
            pltpu.VMEM((cap, pairs), jnp.float32),
            *[pltpu.VMEM(h.shape, jnp.bfloat16) for h in heads],
            pltpu.SMEM((cap + GROUP,), jnp.int32),
            pltpu.SMEM((len(blocks),), jnp.int32),
            pltpu.SemaphoreType.DMA((2,)),
            pltpu.SemaphoreType.DMA((2,)),
            pltpu.SemaphoreType.DMA((3,)),
        ],
        compiler_params=pltpu.CompilerParams(vmem_limit_bytes=58 * 1024 * 1024),
        cost_estimate=pl.CostEstimate(
            flops=WEIGHT * 2 * cap * side * R * R * frames * (width // R),
            bytes_accessed=cap * frames * width * 4, transcendentals=0,
        ),
        name=name,
    )(who, ids, queries, before, *heads, own, other, *blocks)


def chip_places(mesh):
    devices = list(mesh.devices.flat)[::2]
    places = [tuple(getattr(d, "coords", ()) or ()) for d in devices]
    if any(len(p) != 3 for p in places):
        return [(i, 0, 0) for i in range(len(devices))]
    return [tuple(reversed(p)) for p in places]


def ring_position(coordinate, size):
    if size <= 2:
        return coordinate
    order = list(range(1, size, 2)) + list(reversed(range(0, size, 2)))
    order = [0] + [c for c in order if c != 0]
    return order.index(coordinate)


class Gather:
    def __init__(self, sizes, steps, queries):
        self.steps = steps
        q_dev = queries.shape[0]
        depth, height, width = sizes
        b1, a1, a2, b2 = [q_dev * s // sum(SHARES) for s in SHARES]
        here = (0, 0, 0)
        self.blocks = {("a", 0): queries}
        self.cells = {("a", 0): [(here, 0, q_dev)]}
        self.arrival = {("a", 0): -1}
        self.pieces = {("deep",): [(("a", 0), b1, a1 + a2)]}

        def moved(cells, axis, k):
            out = []
            for off, q, n in cells:
                off = list(off)
                off[axis] = k
                out.append((tuple(off), q, n))
            return out

        def ring(axis, source, name, cells):
            out = []
            for k in range(1, sizes[axis]):
                target = name + (k,)
                self.cells[target] = moved(cells, axis, k)
                out.append((axis, source, target))
                source = target
            return out

        deep = ring(0, ("deep",), ("a",), [(here, b1, a1 + a2)])
        rounds = []
        planes = []
        for k in range(depth):
            lists, later = {1: [], 2: []}, {1: [], 2: []}
            for r, (p, q) in ((0, (2, 1)), (1, (1, 2))):
                own = ("half", k, r)
                if k == 0:
                    start, n = (0, b1 + a1) if r == 0 else (b1 + a1, a2 + b2)
                    first = start
                else:
                    start, n = (0, a1) if r == 0 else (a1, a2)
                    first = start + b1
                self.pieces[own] = [(("a", k), start, n)]
                self.cells[own] = [((k, 0, 0), first, n)]
                line = ring(p, own, ("a", k, r, "line"), self.cells[own])
                lists[p] += line
                found = [own] + [m[2] for m in line]
                for i, source in enumerate(list(found)):
                    turn = ring(q, source, ("a", k, r, "turn", i), self.cells[source])
                    later[q] += turn
                    found += [m[2] for m in turn]
                if k == 0:
                    planes += [(key, 0, b1) if r == 0 else (key, a2, b2) for key in found]
            both = [lists[axis] + later[axis] for axis in (2, 1)]
            for i in range(max(map(len, both))):
                rounds.append([l[i] for l in both if i < len(l)])
        self.pieces[("b", 0)] = planes
        cells = [(self.cells[key][0][0], self.cells[key][0][1] + at, n) for key, at, n in planes]
        deep += ring(0, ("b", 0), ("b",), cells)
        gap = max(1, len(rounds) // max(1, len(deep)))
        while len(rounds) < gap * len(deep):
            rounds.append([])
        for i, m in enumerate(deep):
            rounds[i * gap].append(m)
        self.per_plane = len(rounds) // depth
        self.rounds = rounds
        for i, messages in enumerate(rounds):
            for axis, _, target in messages:
                self.arrival[target] = i if axis else i + gap - 1

    def block(self, key):
        if key not in self.blocks:
            parts = [self.block(k)[at:at + n] for k, at, n in self.pieces[key]]
            self.blocks[key] = parts[0] if len(parts) == 1 else jnp.concatenate(parts, axis=0)
        return self.blocks[key]


def body(places, sizes, queries, index_videos, candidates, conv_one, conv_two, conv_three):
    devices = lax.axis_size("shard")
    q_dev, frames, width = queries.shape
    k_count = candidates.shape[1]
    idx_dev = index_videos.shape[0]
    pairs = q_dev * k_count
    chips = devices // 2
    per_holder = max(2, (2 * pairs + devices - 1) // devices)
    me = lax.axis_index("shard")
    chip, core = me // 2, me % 2

    rings = [tuple(ring_position(c, n) for c, n in zip(p, sizes)) for p in places]
    where = {r: i for i, r in enumerate(rings)}

    def step_along(axis):
        out = []
        for i, ring in enumerate(rings):
            to = list(ring)
            to[axis] = (to[axis] + 1) % sizes[axis]
            out += [(2 * i + c, 2 * where[tuple(to)] + c) for c in range(2)]
        return out

    other = lax.ppermute(index_videos, "shard", [(d, d ^ 1) for d in range(devices)])
    gather = Gather(sizes, [step_along(a) for a in range(3)], queries)
    rounds = gather.rounds

    total = len(rounds)
    ends = [gather.per_plane * (z + 1) - 1 for z in range(sizes[0] - 1)]
    ends = sorted({e for e in ends if 0 <= e < total - 2} | {total - 2, total - 1})
    phases = [[] for _ in ends]
    for key in gather.arrival:
        phases[next(i for i, e in enumerate(ends) if gather.arrival[key] <= e)].append(key)
    offsets = [(z, y, x) for z in range(sizes[0]) for y in range(sizes[1]) for x in range(sizes[2])]
    back = np.array(
        [[where[tuple((r - o) % n for r, o, n in zip(ring, off, sizes))] for off in offsets]
         for ring in rings], np.int32,
    )
    who = jnp.concatenate(
        [jnp.stack([chip, core]), lax.dynamic_index_in_dim(jnp.asarray(back), chip, 0, keepdims=False)]
    )

    def contents(p):
        packed, bounds, found = [], [0], {}
        for key in phases[p]:
            row = 0
            for off, first, n in gather.cells[key]:
                found[off] = found.get(off, 0) + n
                for q in range(first, first + n):
                    packed.append((offsets.index(off) << 16) + (q << 8) + row)
                    row += 1
            bounds.append(len(packed))
        cap = sum(min(n * k_count, 2 * per_holder) for n in found.values())
        return jnp.asarray(np.array(packed, np.int32)), bounds, -(-cap // HEAD) * HEAD

    state = {}
    heads = head_matrices(conv_one, conv_two, conv_three)
    tables = [jnp.zeros((chips, pairs), jnp.float32)]

    def score():
        p = len(tables) - 1
        tables.append(pair_scores(
            [gather.block(k) for k in phases[p]], index_videos, other, who, state["ids"], *contents(p), heads,
            tables[-1], k_count, idx_dev, "phase_" + str(p),
        ))

    done = []
    for i, messages in enumerate(rounds):
        behind = list(done[i - 2]) if i >= 2 else []
        if len(tables) <= len(ends) and i >= 2:
            if i == min(ends[len(tables) - 1] + LATER, total - 1) and ends[len(tables) - 1] <= i - 2:
                score()
                behind.append(tables[-1])
        done.append([])
        flat = [m for m in messages if m[0]]
        parts = [flat, [m for m in messages if not m[0]]]
        if i in (1, 2):
            parts = [flat[:1], flat[1:], parts[1]]
        for at, together in enumerate(parts):
            ties = list(behind)
            if i == 2 and at == 1 or i == 3:
                ties.append(other)
            sent = [gather.block(source) for _, source, _ in together]
            sent = lax.optimization_barrier((*sent, *ties))[:len(sent)] if sent else []
            for (axis, _, target), block in zip(together, sent):
                gather.blocks[target] = lax.ppermute(block, "shard", gather.steps[axis])
                if axis:
                    done[i].append(gather.blocks[target])
        if i == 0:
            ids = lax.optimization_barrier((candidates, *done[0]))[0].reshape(1, pairs)
            state["ids"] = lax.all_to_all(
                jnp.broadcast_to(ids, (devices, pairs)), "shard", split_axis=0, concat_axis=0,
                tiled=True,
            )
    while len(tables) <= len(ends):
        score()
    table = jnp.where(jnp.arange(2)[None, :, None] == core, tables[-1][:, None], 0.0)
    scores = lax.all_to_all(
        table.reshape(devices, pairs), "shard", split_axis=0, concat_axis=0, tiled=True
    )
    return jnp.sum(scores, axis=0).reshape(q_dev, k_count)


def solution(mesh):
    places = chip_places(mesh)
    low = [min(p[a] for p in places) for a in range(3)]
    places = [tuple(c - m for c, m in zip(p, low)) for p in places]
    sizes = [max(p[a] for p in places) + 1 for a in range(3)]
    placed = (P("shard", None, None), P("shard", None, None), P("shard", None), P(), P(), P())
    return jax.shard_map(
        functools.partial(body, places, sizes), mesh=mesh, in_specs=placed,
        out_specs=P("shard", None), check_vma=False,
    )
```

```python
import functools
import math

import jax
import jax.numpy as jnp
import numpy as np
from jax import lax
from jax.experimental import pallas as pl
from jax.experimental.pallas import tpu as pltpu
from jax.sharding import PartitionSpec as P

R = 5
GROUP = 16
SHARES = (1, 7, 6, 2)
HEAD = 64
LATER = 4
WEIGHT = 8


def dot(a, b):
    return jnp.dot(a, b, preferred_element_type=jnp.float32)


def iota(shape, dim):
    return lax.broadcasted_iota(jnp.int32, shape, dim)


def head_kernel(one_w, two_w, three_w, one_ref, two_ref, three_ref, one_acc, two_acc, three_acc):
    one_acc[...] = jnp.zeros_like(one_acc)
    two_acc[...] = jnp.zeros_like(two_acc)
    three_acc[...] = jnp.zeros_like(three_acc)
    c1, c2 = two_w.shape[1], two_w.shape[2]
    b1, b2 = c1.bit_length() - 1, c2.bit_length() - 1

    def tap(t, _):
        k = lax.div(t, 3) - 1
        l = lax.rem(t, 3) - 1

        n = one_acc.shape[1]
        row, col = iota((64, n), 0), iota((64, n), 1) >> b1
        y = ((col >> 2) & 3) * 2 + ((col >> 5) & 1)
        x = (col & 3) * 2 + ((col >> 4) & 1)
        hit = ((row >> 3) == y + k) & ((row & 7) == x + l)
        spread = ((iota((c1, n), 1) & (c1 - 1)) == iota((c1, n), 0)).astype(jnp.bfloat16)
        val = dot(jnp.broadcast_to(one_w[t], (16, c1)), spread)[:1]
        one_acc[...] = jnp.where(hit, val, one_acc[...])

        n = two_acc.shape[1]
        spread = ((iota((c2, n), 1) & (c2 - 1)) == iota((c2, n), 0)).astype(jnp.bfloat16)
        val = dot(two_w[t], spread)

        def cell(ij, _):
            col = iota((c1, n), 1) >> b2
            y = ((col >> 1) & 1) * 2 + ((col >> 3) & 1)
            x = (col & 1) * 2 + ((col >> 2) & 1)
            hit = (lax.div(ij, 4) == y + k) & (lax.rem(ij, 4) == x + l)
            rows = pl.ds(pl.multiple_of(ij * c1, c1), c1)
            two_acc[rows, :] = jnp.where(hit, val, two_acc[rows, :])
            return 0
        lax.fori_loop(0, 16, cell, 0)

        m, n = three_acc.shape
        pick = ((iota((m, c2), 0) & (c2 - 1)) == iota((m, c2), 1)).astype(jnp.bfloat16)
        val = lax.dot_general(
            pick, jnp.broadcast_to(three_w[t], (128, c2)), (((1,), (1,)), ((), ())),
            preferred_element_type=jnp.float32,
        )[:, :1]
        row, col = iota((m, n), 0) >> b2, iota((m, n), 1)
        y, x = col & 127, col >> 7
        hit = ((row >> 1) == y + k) & ((row & 1) == x + l) & (y < 2)
        three_acc[...] = jnp.where(hit, val, three_acc[...])
        return 0

    lax.fori_loop(0, 9, tap, 0)
    one_ref[...] = one_acc[...].astype(jnp.bfloat16)
    two_ref[...] = two_acc[...].astype(jnp.bfloat16)
    three_ref[...] = three_acc[...].astype(jnp.bfloat16)


def head_matrices(conv_one, conv_two, conv_three):
    c1, c2 = conv_two.shape[1], conv_two.shape[0]
    one_w = conv_one.transpose(2, 3, 1, 0).reshape(9, 1, c1)
    two_w = conv_two.transpose(2, 3, 1, 0).reshape(9, c1, c2)
    three_w = conv_three.transpose(2, 3, 0, 1).reshape(9, 1, c2)
    shapes = [(64, 64 * c1), (16 * c1, 16 * c2), (4 * c2, 256)]
    vmem = pl.BlockSpec(memory_space=pltpu.VMEM)
    return pl.pallas_call(
        head_kernel,
        out_shape=[jax.ShapeDtypeStruct(s, jnp.bfloat16) for s in shapes],
        in_specs=[vmem] * 3,
        out_specs=[vmem] * 3,
        scratch_shapes=[pltpu.VMEM(s, jnp.float32) for s in shapes],
        compiler_params=pltpu.CompilerParams(vmem_limit_bytes=24 * 1024 * 1024),
        cost_estimate=pl.CostEstimate(flops=10**9, bytes_accessed=3 * 10**6, transcendentals=0),
        name="head_matrices",
    )(one_w, two_w, three_w)


def list_kernel(idx_dev, k_count, pairs, bounds, who_ref, ids_ref, queries_ref, *lists):
    chip, core = who_ref[0], who_ref[1]
    bits = chip_bits(idx_dev)
    begin = chip << bits
    for p, list_ref in enumerate(lists):
        buffers = len(bounds[p]) - 1
        at = jnp.int32(buffers)
        for b in range(buffers):
            def one_of(t, n):
                packed = queries_ref[t]
                row, first = packed & 255, ((packed >> 8) & 255) * k_count
                sender = who_ref[2 + (packed >> 16)]
                base = ((sender * pairs + first) << (8 + bits)) + (row << bits)
                line = 2 * sender + core
                for k in range(k_count):
                    vid = ids_ref[line, first + k] - begin
                    list_ref[n] = base + (k << (8 + bits)) + (vid & ((1 << bits) - 1))
                    n = n + ((vid >> bits) == 0).astype(jnp.int32)
                return n
            at = lax.fori_loop(bounds[p][b], bounds[p][b + 1], one_of, at)
            list_ref[b] = at - buffers
        for i in range(GROUP):
            list_ref[at + i] = 0


def chip_bits(idx_dev):
    bits = (2 * idx_dev - 1).bit_length()
    assert 2 * idx_dev == 1 << bits
    return bits


def pair_lists(who, ids, queries, bounds, caps, k_count, idx_dev):
    smem = pl.BlockSpec(memory_space=pltpu.SMEM)
    sizes = [len(b) - 1 + cap + GROUP for b, cap in zip(bounds, caps)]
    return pl.pallas_call(
        functools.partial(list_kernel, idx_dev, k_count, ids.shape[1], bounds),
        out_shape=[jax.ShapeDtypeStruct((n,), jnp.int32) for n in sizes],
        in_specs=[smem] * 3,
        out_specs=[smem] * len(sizes),
        cost_estimate=pl.CostEstimate(flops=10**7, bytes_accessed=10**6, transcendentals=0),
        name="pair_lists",
    )(who, ids, queries)


def pair_kernel(frames, idx_dev, buffers, scale, list_ref, one_ref, two_ref, three_ref, before_ref,
                v_hbm, *rest):
    q_hbm, rest = rest[:buffers], rest[buffers:]
    out_ref, q_in, v_in, q_rows, v_rows, maps, scores, q_sem, v_sem = rest
    width = v_hbm.shape[2] // R
    side = GROUP * frames
    senders, pairs = out_ref.shape
    bits = chip_bits(idx_dev)
    assert senders * pairs <= 1 << (23 - bits)
    count = list_ref[buffers - 1]
    groups = (count + GROUP - 1) // GROUP

    def fetch(step, slot):
        first = step * GROUP
        for b in range(buffers):
            low = 0 if b == 0 else jnp.clip(list_ref[b - 1] - first, 0, GROUP)
            high = GROUP if b == buffers - 1 else jnp.clip(list_ref[b] - first, 0, GROUP)

            def one_query(p, _):
                pltpu.make_async_copy(
                    q_hbm[b].at[(list_ref[buffers + first + p] >> bits) & 255], q_in.at[slot, p],
                    q_sem.at[slot],
                ).start()
                return 0
            lax.fori_loop(low, high, one_query, 0)

        def one_video(p, _):
            vid = list_ref[buffers + first + p] & ((1 << bits) - 1)
            pltpu.make_async_copy(v_hbm.at[vid], v_in.at[slot, p], v_sem.at[slot]).start()
            return 0
        lax.fori_loop(0, GROUP, one_video, 0)

    maps[...] = jnp.zeros_like(maps)

    @pl.when(groups > 0)
    def _():
        fetch(0, 0)

    def step(g, _):
        slot = lax.rem(g, 2)

        @pl.when(g + 1 < groups)
        def _():
            fetch(g + 1, 1 - slot)

        pltpu.make_async_copy(q_in.at[slot], q_in.at[slot], q_sem.at[slot]).wait()
        pltpu.make_async_copy(v_in.at[slot], v_in.at[slot], v_sem.at[slot]).wait()
        for r in range(R):
            cols = pl.ds(r * width, width)
            q_rows[pl.ds(r * side, side), :] = q_in[slot, :, :, cols].reshape(side, width)
            v_rows[pl.ds(r * side, side), :] = v_in[slot, :, :, cols].reshape(side, width)

        sim = lax.dot_general(
            q_rows[...], v_rows[...], (((1,), (1,)), ((), ())), preferred_element_type=jnp.float32
        )
        best = sim[:, :side]
        for s in range(1, R):
            best = jnp.maximum(best, sim[:, s * side:(s + 1) * side])
        total = best[:side]
        for r in range(1, R):
            total = total + best[r * side:(r + 1) * side]
        cells = frames * frames
        same_pair = iota((side, side), 0) // frames == iota((side, side), 1) // frames
        lane, sub = iota((side, cells), 1), iota((side, cells), 0)
        spread = (lane % frames == sub % frames).astype(jnp.bfloat16)
        own_frame = lane // frames == sub % frames
        fold = (iota((GROUP, side), 1) // frames == iota((GROUP, side), 0)).astype(jnp.bfloat16)
        mean = jnp.where(same_pair, total * scale, 0.0).astype(jnp.bfloat16)
        wide = jnp.where(own_frame, dot(mean, spread), 0.0).astype(jnp.bfloat16)
        maps[pl.ds(pl.multiple_of(g * GROUP, GROUP), GROUP), :] = dot(fold, wide)
        return 0

    lax.fori_loop(0, groups, step, 0)

    def pooled(x):
        n = x.shape[1] // 4
        best = x[:, :n]
        for i in range(1, 4):
            best = jnp.maximum(best, x[:, i * n:(i + 1) * n])
        return jnp.maximum(best, 0.0).astype(jnp.bfloat16)

    def head(g, _):
        here = pl.ds(pl.multiple_of(g * HEAD, HEAD), HEAD)
        first = pooled(dot(maps[here, :].astype(jnp.bfloat16), one_ref[...]))
        second = pooled(dot(first, two_ref[...]))
        final = jnp.clip(dot(second, three_ref[...]), -1.0, 1.0)
        best = jnp.maximum(final[:, :128], final[:, 128:])
        scores[here, :] = jnp.broadcast_to((best[:, 0:1] + best[:, 1:2]) * 0.5, (HEAD, pairs))
        return 0

    lax.fori_loop(0, (count + HEAD - 1) // HEAD, head, 0)

    out_ref[...] = before_ref[...]

    def write(i, _):
        entry = list_ref[buffers + i] >> (8 + bits)
        at = pl.ds(lax.div(entry, pairs), 1)
        hit = iota((1, pairs), 1) == lax.rem(entry, pairs)
        out_ref[at, :] = jnp.where(hit, scores[pl.ds(i, 1), :], out_ref[at, :])
        return 0

    lax.fori_loop(0, count, write, 0)


def pair_scores(blocks, videos, pair_list, cap, heads, before, idx_dev, name):
    frames, width = videos.shape[1], videos.shape[2]
    pairs = before.shape[1]
    side = GROUP * frames
    scale = 1.0 / (math.sqrt(width // R) * R)
    smem = pl.BlockSpec(memory_space=pltpu.SMEM)
    vmem = pl.BlockSpec(memory_space=pltpu.VMEM)
    hbm = pl.BlockSpec(memory_space=pltpu.HBM)
    return pl.pallas_call(
        functools.partial(pair_kernel, frames, idx_dev, len(blocks), scale),
        out_shape=jax.ShapeDtypeStruct(before.shape, jnp.float32),
        in_specs=[smem] + [vmem] * 4 + [hbm] * (1 + len(blocks)),
        out_specs=vmem,
        scratch_shapes=[
            pltpu.VMEM((2, GROUP, frames, width), jnp.bfloat16),
            pltpu.VMEM((2, GROUP, frames, width), jnp.bfloat16),
            pltpu.VMEM((R * side, width // R), jnp.bfloat16),
            pltpu.VMEM((R * side, width // R), jnp.bfloat16),
            pltpu.VMEM((cap, frames * frames), jnp.float32),
            pltpu.VMEM((cap, pairs), jnp.float32),
            pltpu.SemaphoreType.DMA((2,)),
            pltpu.SemaphoreType.DMA((2,)),
        ],
        compiler_params=pltpu.CompilerParams(vmem_limit_bytes=58 * 1024 * 1024),
        cost_estimate=pl.CostEstimate(
            flops=WEIGHT * 2 * cap * side * R * R * frames * (width // R),
            bytes_accessed=cap * frames * width * 4, transcendentals=0,
        ),
        name=name,
    )(pair_list, *heads, before, videos, *blocks)


def chip_places(mesh):
    devices = list(mesh.devices.flat)[::2]
    places = [tuple(getattr(d, "coords", ()) or ()) for d in devices]
    if any(len(p) != 3 for p in places):
        return [(i, 0, 0) for i in range(len(devices))]
    return [tuple(reversed(p)) for p in places]


def ring_position(coordinate, size):
    if size <= 2:
        return coordinate
    order = list(range(1, size, 2)) + list(reversed(range(0, size, 2)))
    order = [0] + [c for c in order if c != 0]
    return order.index(coordinate)


class Gather:
    def __init__(self, sizes, steps, queries):
        self.steps = steps
        q_dev = queries.shape[0]
        depth, height, width = sizes
        b1, a1, a2, b2 = [q_dev * s // sum(SHARES) for s in SHARES]
        here = (0, 0, 0)
        self.blocks = {("a", 0): queries}
        self.cells = {("a", 0): [(here, 0, q_dev)]}
        self.arrival = {("a", 0): -1}
        self.pieces = {("deep",): [(("a", 0), b1, a1 + a2)]}

        def moved(cells, axis, k):
            out = []
            for off, q, n in cells:
                off = list(off)
                off[axis] = k
                out.append((tuple(off), q, n))
            return out

        def ring(axis, source, name, cells):
            out = []
            for k in range(1, sizes[axis]):
                target = name + (k,)
                self.cells[target] = moved(cells, axis, k)
                out.append((axis, source, target))
                source = target
            return out

        deep = ring(0, ("deep",), ("a",), [(here, b1, a1 + a2)])
        rounds = []
        planes = []
        for k in range(depth):
            lists, later = {1: [], 2: []}, {1: [], 2: []}
            for r, (p, q) in ((0, (2, 1)), (1, (1, 2))):
                own = ("half", k, r)
                if k == 0:
                    start, n = (0, b1 + a1) if r == 0 else (b1 + a1, a2 + b2)
                    first = start
                else:
                    start, n = (0, a1) if r == 0 else (a1, a2)
                    first = start + b1
                self.pieces[own] = [(("a", k), start, n)]
                self.cells[own] = [((k, 0, 0), first, n)]
                line = ring(p, own, ("a", k, r, "line"), self.cells[own])
                lists[p] += line
                found = [own] + [m[2] for m in line]
                for i, source in enumerate(list(found)):
                    turn = ring(q, source, ("a", k, r, "turn", i), self.cells[source])
                    later[q] += turn
                    found += [m[2] for m in turn]
                if k == 0:
                    planes += [(key, 0, b1) if r == 0 else (key, a2, b2) for key in found]
            both = [lists[axis] + later[axis] for axis in (2, 1)]
            for i in range(max(map(len, both))):
                rounds.append([l[i] for l in both if i < len(l)])
        self.pieces[("b", 0)] = planes
        cells = [(self.cells[key][0][0], self.cells[key][0][1] + at, n) for key, at, n in planes]
        deep += ring(0, ("b", 0), ("b",), cells)
        gap = max(1, len(rounds) // max(1, len(deep)))
        while len(rounds) < gap * len(deep):
            rounds.append([])
        for i, m in enumerate(deep):
            rounds[i * gap].append(m)
        self.per_plane = len(rounds) // depth
        self.rounds = rounds
        for i, messages in enumerate(rounds):
            for axis, _, target in messages:
                self.arrival[target] = i if axis else i + gap - 1

    def block(self, key):
        if key not in self.blocks:
            whole = [self.block(k) for k, _, _ in self.pieces[key]]
            if len(whole) > 1:
                whole = lax.optimization_barrier(whole)
            parts = [b[at:at + n] for b, (_, at, n) in zip(whole, self.pieces[key])]
            self.blocks[key] = parts[0] if len(parts) == 1 else jnp.concatenate(parts, axis=0)
        return self.blocks[key]


def body(places, sizes, queries, index_videos, candidates, conv_one, conv_two, conv_three):
    devices = lax.axis_size("shard")
    q_dev, frames, width = queries.shape
    k_count = candidates.shape[1]
    idx_dev = index_videos.shape[0]
    pairs = q_dev * k_count
    chips = devices // 2
    per_holder = max(2, (2 * pairs + devices - 1) // devices)
    me = lax.axis_index("shard")
    chip, core = me // 2, me % 2

    rings = [tuple(ring_position(c, n) for c, n in zip(p, sizes)) for p in places]
    where = {r: i for i, r in enumerate(rings)}

    def step_along(axis):
        out = []
        for i, ring in enumerate(rings):
            to = list(ring)
            to[axis] = (to[axis] + 1) % sizes[axis]
            out += [(2 * i + c, 2 * where[tuple(to)] + c) for c in range(2)]
        return out

    videos = lax.all_gather(
        index_videos, "shard", axis=0, tiled=True,
        axis_index_groups=[[2 * c, 2 * c + 1] for c in range(chips)],
    )
    gather = Gather(sizes, [step_along(a) for a in range(3)], queries)
    rounds = gather.rounds

    total = len(rounds)
    ends = [gather.per_plane * (z + 1) - 1 for z in range(sizes[0] - 1)]
    ends = sorted({e for e in ends if 0 <= e < total - 2} | {total - 2, total - 1})
    phases = [[] for _ in ends]
    for key in gather.arrival:
        phases[next(i for i, e in enumerate(ends) if gather.arrival[key] <= e)].append(key)
    offsets = [(z, y, x) for z in range(sizes[0]) for y in range(sizes[1]) for x in range(sizes[2])]
    back = np.array(
        [[where[tuple((r - o) % n for r, o, n in zip(ring, off, sizes))] for off in offsets]
         for ring in rings], np.int32,
    )
    who = jnp.concatenate(
        [jnp.stack([chip, core]), lax.dynamic_index_in_dim(jnp.asarray(back), chip, 0, keepdims=False)]
    )

    contents, bounds, caps = [], [], []
    for keys in phases:
        found = {}
        bounds.append([len(contents)])
        for key in keys:
            row = 0
            for off, first, n in gather.cells[key]:
                found[off] = found.get(off, 0) + n
                for q in range(first, first + n):
                    contents.append((offsets.index(off) << 16) + (q << 8) + row)
                    row += 1
            bounds[-1].append(len(contents))
        cap = sum(min(n * k_count, 2 * per_holder) for n in found.values())
        caps.append(-(-cap // HEAD) * HEAD)
    contents = jnp.asarray(np.array(contents, np.int32))

    state = {}
    heads = head_matrices(conv_one, conv_two, conv_three)
    tables = [jnp.zeros((chips, pairs), jnp.float32)]

    def score():
        p = len(tables) - 1
        tables.append(pair_scores(
            [gather.block(k) for k in phases[p]], videos, state["lists"][p], caps[p], heads,
            tables[-1], idx_dev, "phase_" + str(p),
        ))

    done = []
    for i, messages in enumerate(rounds):
        behind = list(done[i - 2]) if i >= 2 else []
        if len(tables) <= len(ends) and i >= 2:
            if i == min(ends[len(tables) - 1] + LATER, total - 1) and ends[len(tables) - 1] <= i - 2:
                score()
                behind.append(tables[-1])
        done.append([])
        for together in ([m for m in messages if m[0]], [m for m in messages if not m[0]]):
            sent = [gather.block(source) for _, source, _ in together]
            sent = lax.optimization_barrier((*sent, *behind))[:len(sent)] if sent else []
            for (axis, _, target), block in zip(together, sent):
                gather.blocks[target] = lax.ppermute(block, "shard", gather.steps[axis])
                if axis:
                    done[i].append(gather.blocks[target])
        if i == 0:
            ids = lax.optimization_barrier((candidates, *done[0]))[0].reshape(1, pairs)
            ids = lax.all_to_all(
                jnp.broadcast_to(ids, (devices, pairs)), "shard", split_axis=0, concat_axis=0,
                tiled=True,
            )
            state["lists"] = pair_lists(who, ids, contents, bounds, caps, k_count, idx_dev)
    while len(tables) <= len(ends):
        score()
    table = jnp.where(jnp.arange(2)[None, :, None] == core, tables[-1][:, None], 0.0)
    scores = lax.all_to_all(
        table.reshape(devices, pairs), "shard", split_axis=0, concat_axis=0, tiled=True
    )
    return jnp.sum(scores, axis=0).reshape(q_dev, k_count)


def solution(mesh):
    places = chip_places(mesh)
    low = [min(p[a] for p in places) for a in range(3)]
    places = [tuple(c - m for c, m in zip(p, low)) for p in places]
    sizes = [max(p[a] for p in places) + 1 for a in range(3)]
    placed = (P("shard", None, None), P("shard", None, None), P("shard", None), P(), P(), P())
    return jax.shard_map(
        functools.partial(body, places, sizes), mesh=mesh, in_specs=placed,
        out_specs=P("shard", None), check_vma=False,
    )
```

```python
import functools
import math

import jax
import jax.numpy as jnp
import numpy as np
from jax import lax
from jax.experimental import pallas as pl
from jax.experimental.pallas import tpu as pltpu
from jax.sharding import PartitionSpec as P

R = 5
GROUP = 16
SHARES = (1, 7, 6, 2)
HEAD = 64
LATER = 4
LISTS = 2
WAITS = 5
WEIGHT = 8


def dot(a, b):
    return jnp.dot(a, b, preferred_element_type=jnp.float32)


def iota(shape, dim):
    return lax.broadcasted_iota(jnp.int32, shape, dim)


def head_kernel(one_w, two_w, three_w, one_ref, two_ref, three_ref, one_acc, two_acc, three_acc):
    one_acc[...] = jnp.zeros_like(one_acc)
    two_acc[...] = jnp.zeros_like(two_acc)
    three_acc[...] = jnp.zeros_like(three_acc)
    c1, c2 = two_w.shape[1], two_w.shape[2]
    b1, b2 = c1.bit_length() - 1, c2.bit_length() - 1

    def tap(t, _):
        k = lax.div(t, 3) - 1
        l = lax.rem(t, 3) - 1

        n = one_acc.shape[1]
        row, col = iota((64, n), 0), iota((64, n), 1) >> b1
        y = ((col >> 2) & 3) * 2 + ((col >> 5) & 1)
        x = (col & 3) * 2 + ((col >> 4) & 1)
        hit = ((row >> 3) == y + k) & ((row & 7) == x + l)
        spread = ((iota((c1, n), 1) & (c1 - 1)) == iota((c1, n), 0)).astype(jnp.bfloat16)
        val = dot(jnp.broadcast_to(one_w[t], (16, c1)), spread)[:1]
        one_acc[...] = jnp.where(hit, val, one_acc[...])

        n = two_acc.shape[1]
        spread = ((iota((c2, n), 1) & (c2 - 1)) == iota((c2, n), 0)).astype(jnp.bfloat16)
        val = dot(two_w[t], spread)

        def cell(ij, _):
            col = iota((c1, n), 1) >> b2
            y = ((col >> 1) & 1) * 2 + ((col >> 3) & 1)
            x = (col & 1) * 2 + ((col >> 2) & 1)
            hit = (lax.div(ij, 4) == y + k) & (lax.rem(ij, 4) == x + l)
            rows = pl.ds(pl.multiple_of(ij * c1, c1), c1)
            two_acc[rows, :] = jnp.where(hit, val, two_acc[rows, :])
            return 0
        lax.fori_loop(0, 16, cell, 0)

        m, n = three_acc.shape
        pick = ((iota((m, c2), 0) & (c2 - 1)) == iota((m, c2), 1)).astype(jnp.bfloat16)
        val = lax.dot_general(
            pick, jnp.broadcast_to(three_w[t], (128, c2)), (((1,), (1,)), ((), ())),
            preferred_element_type=jnp.float32,
        )[:, :1]
        row, col = iota((m, n), 0) >> b2, iota((m, n), 1)
        y, x = col & 127, col >> 7
        hit = ((row >> 1) == y + k) & ((row & 1) == x + l) & (y < 2)
        three_acc[...] = jnp.where(hit, val, three_acc[...])
        return 0

    lax.fori_loop(0, 9, tap, 0)
    one_ref[...] = one_acc[...].astype(jnp.bfloat16)
    two_ref[...] = two_acc[...].astype(jnp.bfloat16)
    three_ref[...] = three_acc[...].astype(jnp.bfloat16)


def head_matrices(conv_one, conv_two, conv_three):
    c1, c2 = conv_two.shape[1], conv_two.shape[0]
    one_w = conv_one.transpose(2, 3, 1, 0).reshape(9, 1, c1)
    two_w = conv_two.transpose(2, 3, 1, 0).reshape(9, c1, c2)
    three_w = conv_three.transpose(2, 3, 0, 1).reshape(9, 1, c2)
    shapes = [(64, 64 * c1), (16 * c1, 16 * c2), (4 * c2, 256)]
    vmem = pl.BlockSpec(memory_space=pltpu.VMEM)
    return pl.pallas_call(
        head_kernel,
        out_shape=[jax.ShapeDtypeStruct(s, jnp.bfloat16) for s in shapes],
        in_specs=[vmem] * 3,
        out_specs=[vmem] * 3,
        scratch_shapes=[pltpu.VMEM(s, jnp.float32) for s in shapes],
        compiler_params=pltpu.CompilerParams(vmem_limit_bytes=24 * 1024 * 1024),
        cost_estimate=pl.CostEstimate(flops=10**9, bytes_accessed=3 * 10**6, transcendentals=0),
        name="head_matrices",
    )(one_w, two_w, three_w)


def list_kernel(idx_dev, k_count, pairs, bounds, who_ref, ids_ref, queries_ref, *lists):
    chip, core = who_ref[0], who_ref[1]
    bits = chip_bits(idx_dev)
    begin = chip << bits
    for p, list_ref in enumerate(lists):
        buffers = len(bounds[p]) - 1
        at = jnp.int32(buffers)
        for b in range(buffers):
            def one_of(t, n):
                packed = queries_ref[t]
                row, first = packed & 255, ((packed >> 8) & 255) * k_count
                sender = who_ref[2 + (packed >> 16)]
                base = ((sender * pairs + first) << (8 + bits)) + (row << bits)
                line = 2 * sender + core
                for k in range(k_count):
                    vid = ids_ref[line, first + k] - begin
                    list_ref[n] = base + (k << (8 + bits)) + (vid & ((1 << bits) - 1))
                    n = n + ((vid >> bits) == 0).astype(jnp.int32)
                return n
            at = lax.fori_loop(bounds[p][b], bounds[p][b + 1], one_of, at)
            list_ref[b] = at - buffers
        for i in range(GROUP):
            list_ref[at + i] = 0


def chip_bits(idx_dev):
    bits = (2 * idx_dev - 1).bit_length()
    assert 2 * idx_dev == 1 << bits
    return bits


def pair_lists(who, ids, queries, bounds, caps, k_count, idx_dev):
    smem = pl.BlockSpec(memory_space=pltpu.SMEM)
    sizes = [len(b) - 1 + cap + GROUP for b, cap in zip(bounds, caps)]
    return pl.pallas_call(
        functools.partial(list_kernel, idx_dev, k_count, ids.shape[1], bounds),
        out_shape=[jax.ShapeDtypeStruct((n,), jnp.int32) for n in sizes],
        in_specs=[smem] * 3,
        out_specs=[smem] * len(sizes),
        cost_estimate=pl.CostEstimate(flops=10**7, bytes_accessed=10**6, transcendentals=0),
        name="pair_lists",
    )(who, ids, queries)


def pair_kernel(frames, idx_dev, buffers, scale, list_ref, one_ref, two_ref, three_ref, before_ref,
                v_hbm, *rest):
    q_hbm, rest = rest[:buffers], rest[buffers:]
    out_ref, q_in, v_in, q_rows, v_rows, maps, scores, q_sem, v_sem = rest
    width = v_hbm.shape[2] // R
    side = GROUP * frames
    senders, pairs = out_ref.shape
    bits = chip_bits(idx_dev)
    assert senders * pairs <= 1 << (23 - bits)
    count = list_ref[buffers - 1]
    groups = (count + GROUP - 1) // GROUP

    def fetch(step, slot):
        first = step * GROUP
        for b in range(buffers):
            low = 0 if b == 0 else jnp.clip(list_ref[b - 1] - first, 0, GROUP)
            high = GROUP if b == buffers - 1 else jnp.clip(list_ref[b] - first, 0, GROUP)

            def one_query(p, _):
                pltpu.make_async_copy(
                    q_hbm[b].at[(list_ref[buffers + first + p] >> bits) & 255], q_in.at[slot, p],
                    q_sem.at[slot],
                ).start()
                return 0
            lax.fori_loop(low, high, one_query, 0)

        def one_video(p, _):
            vid = list_ref[buffers + first + p] & ((1 << bits) - 1)
            pltpu.make_async_copy(v_hbm.at[vid], v_in.at[slot, p], v_sem.at[slot]).start()
            return 0
        lax.fori_loop(0, GROUP, one_video, 0)

    maps[...] = jnp.zeros_like(maps)

    @pl.when(groups > 0)
    def _():
        fetch(0, 0)

    def step(g, _):
        slot = lax.rem(g, 2)

        @pl.when(g + 1 < groups)
        def _():
            fetch(g + 1, 1 - slot)

        pltpu.make_async_copy(q_in.at[slot], q_in.at[slot], q_sem.at[slot]).wait()
        pltpu.make_async_copy(v_in.at[slot], v_in.at[slot], v_sem.at[slot]).wait()
        for r in range(R):
            cols = pl.ds(r * width, width)
            q_rows[pl.ds(r * side, side), :] = q_in[slot, :, :, cols].reshape(side, width)
            v_rows[pl.ds(r * side, side), :] = v_in[slot, :, :, cols].reshape(side, width)

        sim = lax.dot_general(
            q_rows[...], v_rows[...], (((1,), (1,)), ((), ())), preferred_element_type=jnp.float32
        )
        best = sim[:, :side]
        for s in range(1, R):
            best = jnp.maximum(best, sim[:, s * side:(s + 1) * side])
        total = best[:side]
        for r in range(1, R):
            total = total + best[r * side:(r + 1) * side]
        cells = frames * frames
        same_pair = iota((side, side), 0) // frames == iota((side, side), 1) // frames
        lane, sub = iota((side, cells), 1), iota((side, cells), 0)
        spread = (lane % frames == sub % frames).astype(jnp.bfloat16)
        own_frame = lane // frames == sub % frames
        fold = (iota((GROUP, side), 1) // frames == iota((GROUP, side), 0)).astype(jnp.bfloat16)
        mean = jnp.where(same_pair, total * scale, 0.0).astype(jnp.bfloat16)
        wide = jnp.where(own_frame, dot(mean, spread), 0.0).astype(jnp.bfloat16)
        maps[pl.ds(pl.multiple_of(g * GROUP, GROUP), GROUP), :] = dot(fold, wide)
        return 0

    lax.fori_loop(0, groups, step, 0)

    def pooled(x):
        n = x.shape[1] // 4
        best = x[:, :n]
        for i in range(1, 4):
            best = jnp.maximum(best, x[:, i * n:(i + 1) * n])
        return jnp.maximum(best, 0.0).astype(jnp.bfloat16)

    def head(g, _):
        here = pl.ds(pl.multiple_of(g * HEAD, HEAD), HEAD)
        first = pooled(dot(maps[here, :].astype(jnp.bfloat16), one_ref[...]))
        second = pooled(dot(first, two_ref[...]))
        final = jnp.clip(dot(second, three_ref[...]), -1.0, 1.0)
        best = jnp.maximum(final[:, :128], final[:, 128:])
        scores[here, :] = jnp.broadcast_to((best[:, 0:1] + best[:, 1:2]) * 0.5, (HEAD, pairs))
        return 0

    lax.fori_loop(0, (count + HEAD - 1) // HEAD, head, 0)

    out_ref[...] = before_ref[...]

    def write(i, _):
        entry = list_ref[buffers + i] >> (8 + bits)
        at = pl.ds(lax.div(entry, pairs), 1)
        hit = iota((1, pairs), 1) == lax.rem(entry, pairs)
        out_ref[at, :] = jnp.where(hit, scores[pl.ds(i, 1), :], out_ref[at, :])
        return 0

    lax.fori_loop(0, count, write, 0)


def pair_scores(blocks, videos, pair_list, cap, heads, before, idx_dev, name):
    frames, width = videos.shape[1], videos.shape[2]
    pairs = before.shape[1]
    side = GROUP * frames
    scale = 1.0 / (math.sqrt(width // R) * R)
    smem = pl.BlockSpec(memory_space=pltpu.SMEM)
    vmem = pl.BlockSpec(memory_space=pltpu.VMEM)
    hbm = pl.BlockSpec(memory_space=pltpu.HBM)
    return pl.pallas_call(
        functools.partial(pair_kernel, frames, idx_dev, len(blocks), scale),
        out_shape=jax.ShapeDtypeStruct(before.shape, jnp.float32),
        in_specs=[smem] + [vmem] * 4 + [hbm] * (1 + len(blocks)),
        out_specs=vmem,
        scratch_shapes=[
            pltpu.VMEM((2, GROUP, frames, width), jnp.bfloat16),
            pltpu.VMEM((2, GROUP, frames, width), jnp.bfloat16),
            pltpu.VMEM((R * side, width // R), jnp.bfloat16),
            pltpu.VMEM((R * side, width // R), jnp.bfloat16),
            pltpu.VMEM((cap, frames * frames), jnp.float32),
            pltpu.VMEM((cap, pairs), jnp.float32),
            pltpu.SemaphoreType.DMA((2,)),
            pltpu.SemaphoreType.DMA((2,)),
        ],
        compiler_params=pltpu.CompilerParams(vmem_limit_bytes=58 * 1024 * 1024),
        cost_estimate=pl.CostEstimate(
            flops=WEIGHT * 2 * cap * side * R * R * frames * (width // R),
            bytes_accessed=cap * frames * width * 4, transcendentals=0,
        ),
        name=name,
    )(pair_list, *heads, before, videos, *blocks)


def chip_places(mesh):
    devices = list(mesh.devices.flat)[::2]
    places = [tuple(getattr(d, "coords", ()) or ()) for d in devices]
    if any(len(p) != 3 for p in places):
        return [(i, 0, 0) for i in range(len(devices))]
    return [tuple(reversed(p)) for p in places]


def ring_position(coordinate, size):
    if size <= 2:
        return coordinate
    order = list(range(1, size, 2)) + list(reversed(range(0, size, 2)))
    order = [0] + [c for c in order if c != 0]
    return order.index(coordinate)


class Gather:
    def __init__(self, sizes, steps, queries):
        self.steps = steps
        q_dev = queries.shape[0]
        depth, height, width = sizes
        b1, a1, a2, b2 = [q_dev * s // sum(SHARES) for s in SHARES]
        here = (0, 0, 0)
        self.blocks = {("a", 0): queries}
        self.cells = {("a", 0): [(here, 0, q_dev)]}
        self.arrival = {("a", 0): -1}
        self.pieces = {("deep",): [(("a", 0), b1, a1 + a2)]}

        def moved(cells, axis, k):
            out = []
            for off, q, n in cells:
                off = list(off)
                off[axis] = k
                out.append((tuple(off), q, n))
            return out

        def ring(axis, source, name, cells):
            out = []
            for k in range(1, sizes[axis]):
                target = name + (k,)
                self.cells[target] = moved(cells, axis, k)
                out.append((axis, source, target))
                source = target
            return out

        deep = ring(0, ("deep",), ("a",), [(here, b1, a1 + a2)])
        rounds = []
        planes = []
        for k in range(depth):
            lists, later = {1: [], 2: []}, {1: [], 2: []}
            for r, (p, q) in ((0, (2, 1)), (1, (1, 2))):
                own = ("half", k, r)
                if k == 0:
                    start, n = (0, b1 + a1) if r == 0 else (b1 + a1, a2 + b2)
                    first = start
                else:
                    start, n = (0, a1) if r == 0 else (a1, a2)
                    first = start + b1
                self.pieces[own] = [(("a", k), start, n)]
                self.cells[own] = [((k, 0, 0), first, n)]
                line = ring(p, own, ("a", k, r, "line"), self.cells[own])
                lists[p] += line
                found = [own] + [m[2] for m in line]
                for i, source in enumerate(list(found)):
                    turn = ring(q, source, ("a", k, r, "turn", i), self.cells[source])
                    later[q] += turn
                    found += [m[2] for m in turn]
                if k == 0:
                    planes += [(key, 0, b1) if r == 0 else (key, a2, b2) for key in found]
            both = [lists[axis] + later[axis] for axis in (2, 1)]
            for i in range(max(map(len, both))):
                rounds.append([l[i] for l in both if i < len(l)])
        self.pieces[("b", 0)] = planes
        cells = [(self.cells[key][0][0], self.cells[key][0][1] + at, n) for key, at, n in planes]
        deep += ring(0, ("b", 0), ("b",), cells)
        gap = max(1, len(rounds) // max(1, len(deep)))
        while len(rounds) < gap * len(deep):
            rounds.append([])
        for i, m in enumerate(deep):
            rounds[i * gap].append(m)
        self.per_plane = len(rounds) // depth
        self.rounds, self.gap = rounds, gap
        for i, messages in enumerate(rounds):
            for axis, _, target in messages:
                self.arrival[target] = i if axis else i + gap - 1

    def block(self, key):
        if key not in self.blocks:
            whole = [self.block(k) for k, _, _ in self.pieces[key]]
            if len(whole) > 1:
                whole = lax.optimization_barrier(whole)
            parts = [b[at:at + n] for b, (_, at, n) in zip(whole, self.pieces[key])]
            self.blocks[key] = parts[0] if len(parts) == 1 else jnp.concatenate(parts, axis=0)
        return self.blocks[key]


def body(places, sizes, queries, index_videos, candidates, conv_one, conv_two, conv_three):
    devices = lax.axis_size("shard")
    q_dev, frames, width = queries.shape
    k_count = candidates.shape[1]
    idx_dev = index_videos.shape[0]
    pairs = q_dev * k_count
    chips = devices // 2
    per_holder = max(2, (2 * pairs + devices - 1) // devices)
    me = lax.axis_index("shard")
    chip, core = me // 2, me % 2

    rings = [tuple(ring_position(c, n) for c, n in zip(p, sizes)) for p in places]
    where = {r: i for i, r in enumerate(rings)}

    def step_along(axis):
        out = []
        for i, ring in enumerate(rings):
            to = list(ring)
            to[axis] = (to[axis] + 1) % sizes[axis]
            out += [(2 * i + c, 2 * where[tuple(to)] + c) for c in range(2)]
        return out

    videos = lax.all_gather(
        index_videos, "shard", axis=0, tiled=True,
        axis_index_groups=[[2 * c, 2 * c + 1] for c in range(chips)],
    )
    gather = Gather(sizes, [step_along(a) for a in range(3)], queries)
    rounds = gather.rounds

    total = len(rounds)
    ends = [gather.per_plane * (z + 1) - 1 for z in range(sizes[0] - 1)]
    ends = sorted({e for e in ends if 0 <= e < total - 2} | {total - 2, total - 1})
    phases = [[] for _ in ends]
    for key in gather.arrival:
        phases[next(i for i, e in enumerate(ends) if gather.arrival[key] <= e)].append(key)
    offsets = [(z, y, x) for z in range(sizes[0]) for y in range(sizes[1]) for x in range(sizes[2])]
    back = np.array(
        [[where[tuple((r - o) % n for r, o, n in zip(ring, off, sizes))] for off in offsets]
         for ring in rings], np.int32,
    )
    who = jnp.concatenate(
        [jnp.stack([chip, core]), lax.dynamic_index_in_dim(jnp.asarray(back), chip, 0, keepdims=False)]
    )

    contents, bounds, caps = [], [], []
    for keys in phases:
        found = {}
        bounds.append([len(contents)])
        for key in keys:
            row = 0
            for off, first, n in gather.cells[key]:
                found[off] = found.get(off, 0) + n
                for q in range(first, first + n):
                    contents.append((offsets.index(off) << 16) + (q << 8) + row)
                    row += 1
            bounds[-1].append(len(contents))
        cap = sum(min(n * k_count, 2 * per_holder) for n in found.values())
        caps.append(-(-cap // HEAD) * HEAD)
    contents = jnp.asarray(np.array(contents, np.int32))

    state = {}
    heads = head_matrices(conv_one, conv_two, conv_three)
    tables = [jnp.zeros((chips, pairs), jnp.float32)]

    def score():
        p = len(tables) - 1
        tables.append(pair_scores(
            [gather.block(k) for k in phases[p]], videos, state["lists"][p], caps[p], heads,
            tables[-1], idx_dev, "phase_" + str(p),
        ))

    done, deep = [], []
    for i, messages in enumerate(rounds):
        behind = list(done[i - 2]) if i >= 2 else []
        if len(tables) <= len(ends) and i >= 2:
            if i == min(ends[len(tables) - 1] + LATER, total - 1) and ends[len(tables) - 1] <= i - 2:
                score()
                behind.append(tables[-1])
        done.append([])
        for together in ([m for m in messages if m[0]], [m for m in messages if not m[0]]):
            sent = [gather.block(source) for _, source, _ in together]
            ties = list(behind)
            if together and together[0][0] and i >= WAITS and (i - WAITS) % gather.gap == 0:
                ties.append(deep[(i - 1) // gather.gap - 1])
            sent = lax.optimization_barrier((*sent, *ties))[:len(sent)] if sent else []
            for (axis, _, target), block in zip(together, sent):
                gather.blocks[target] = lax.ppermute(block, "shard", gather.steps[axis])
                (done[i] if axis else deep).append(gather.blocks[target])
        if i == 0:
            ids = lax.optimization_barrier((candidates, *done[0]))[0].reshape(1, pairs)
            state["ids"] = lax.all_to_all(
                jnp.broadcast_to(ids, (devices, pairs)), "shard", split_axis=0, concat_axis=0,
                tiled=True,
            )
        if i == min(LISTS, total - 1):
            later = lax.optimization_barrier((who, *done[i]))[0]
            state["lists"] = pair_lists(
                later, state["ids"], contents, bounds, caps, k_count, idx_dev
            )
    while len(tables) <= len(ends):
        score()
    table = jnp.where(jnp.arange(2)[None, :, None] == core, tables[-1][:, None], 0.0)
    scores = lax.all_to_all(
        table.reshape(devices, pairs), "shard", split_axis=0, concat_axis=0, tiled=True
    )
    return jnp.sum(scores, axis=0).reshape(q_dev, k_count)


def solution(mesh):
    places = chip_places(mesh)
    low = [min(p[a] for p in places) for a in range(3)]
    places = [tuple(c - m for c, m in zip(p, low)) for p in places]
    sizes = [max(p[a] for p in places) + 1 for a in range(3)]
    placed = (P("shard", None, None), P("shard", None, None), P("shard", None), P(), P(), P())
    return jax.shard_map(
        functools.partial(body, places, sizes), mesh=mesh, in_specs=placed,
        out_specs=P("shard", None), check_vma=False,
    )
```

```python
import functools
import math

import jax
import jax.numpy as jnp
import numpy as np
from jax import lax
from jax.experimental import pallas as pl
from jax.experimental.pallas import tpu as pltpu
from jax.sharding import PartitionSpec as P

R = 5
GROUP = 16
SHARES = (1, 7, 6, 2)
HEAD = 64
LATER = 4
LISTS = 2
WAITS = 5
WEIGHT = 8


def dot(a, b):
    return jnp.dot(a, b, preferred_element_type=jnp.float32)


def iota(shape, dim):
    return lax.broadcasted_iota(jnp.int32, shape, dim)


def head_kernel(one_w, two_w, three_w, one_ref, two_ref, three_ref, one_acc, two_acc, three_acc):
    one_acc[...] = jnp.zeros_like(one_acc)
    two_acc[...] = jnp.zeros_like(two_acc)
    three_acc[...] = jnp.zeros_like(three_acc)
    c1, c2 = two_w.shape[1], two_w.shape[2]
    b1, b2 = c1.bit_length() - 1, c2.bit_length() - 1

    def tap(t, _):
        k = lax.div(t, 3) - 1
        l = lax.rem(t, 3) - 1

        n = one_acc.shape[1]
        row, col = iota((64, n), 0), iota((64, n), 1) >> b1
        y = ((col >> 2) & 3) * 2 + ((col >> 5) & 1)
        x = (col & 3) * 2 + ((col >> 4) & 1)
        hit = ((row >> 3) == y + k) & ((row & 7) == x + l)
        spread = ((iota((c1, n), 1) & (c1 - 1)) == iota((c1, n), 0)).astype(jnp.bfloat16)
        val = dot(jnp.broadcast_to(one_w[t], (16, c1)), spread)[:1]
        one_acc[...] = jnp.where(hit, val, one_acc[...])

        n = two_acc.shape[1]
        spread = ((iota((c2, n), 1) & (c2 - 1)) == iota((c2, n), 0)).astype(jnp.bfloat16)
        val = dot(two_w[t], spread)

        def cell(ij, _):
            col = iota((c1, n), 1) >> b2
            y = ((col >> 1) & 1) * 2 + ((col >> 3) & 1)
            x = (col & 1) * 2 + ((col >> 2) & 1)
            hit = (lax.div(ij, 4) == y + k) & (lax.rem(ij, 4) == x + l)
            rows = pl.ds(pl.multiple_of(ij * c1, c1), c1)
            two_acc[rows, :] = jnp.where(hit, val, two_acc[rows, :])
            return 0
        lax.fori_loop(0, 16, cell, 0)

        m, n = three_acc.shape
        pick = ((iota((m, c2), 0) & (c2 - 1)) == iota((m, c2), 1)).astype(jnp.bfloat16)
        val = lax.dot_general(
            pick, jnp.broadcast_to(three_w[t], (128, c2)), (((1,), (1,)), ((), ())),
            preferred_element_type=jnp.float32,
        )[:, :1]
        row, col = iota((m, n), 0) >> b2, iota((m, n), 1)
        y, x = col & 127, col >> 7
        hit = ((row >> 1) == y + k) & ((row & 1) == x + l) & (y < 2)
        three_acc[...] = jnp.where(hit, val, three_acc[...])
        return 0

    lax.fori_loop(0, 9, tap, 0)
    one_ref[...] = one_acc[...].astype(jnp.bfloat16)
    two_ref[...] = two_acc[...].astype(jnp.bfloat16)
    three_ref[...] = three_acc[...].astype(jnp.bfloat16)


def head_matrices(conv_one, conv_two, conv_three):
    c1, c2 = conv_two.shape[1], conv_two.shape[0]
    one_w = conv_one.transpose(2, 3, 1, 0).reshape(9, 1, c1)
    two_w = conv_two.transpose(2, 3, 1, 0).reshape(9, c1, c2)
    three_w = conv_three.transpose(2, 3, 0, 1).reshape(9, 1, c2)
    shapes = [(64, 64 * c1), (16 * c1, 16 * c2), (4 * c2, 256)]
    vmem = pl.BlockSpec(memory_space=pltpu.VMEM)
    return pl.pallas_call(
        head_kernel,
        out_shape=[jax.ShapeDtypeStruct(s, jnp.bfloat16) for s in shapes],
        in_specs=[vmem] * 3,
        out_specs=[vmem] * 3,
        scratch_shapes=[pltpu.VMEM(s, jnp.float32) for s in shapes],
        compiler_params=pltpu.CompilerParams(vmem_limit_bytes=24 * 1024 * 1024),
        cost_estimate=pl.CostEstimate(flops=10**9, bytes_accessed=3 * 10**6, transcendentals=0),
        name="head_matrices",
    )(one_w, two_w, three_w)


def list_kernel(idx_dev, k_count, pairs, bounds, who_ref, ids_ref, any_ref, queries_ref, *lists):
    chip, core = who_ref[0], who_ref[1]
    bits = chip_bits(idx_dev)
    begin = chip << bits
    for p, list_ref in enumerate(lists):
        buffers = len(bounds[p]) - 1
        at = jnp.int32(buffers)
        for b in range(buffers):
            def one_of(t, n):
                packed = queries_ref[t]
                query = (packed >> 8) & 255
                sender = who_ref[2 + (packed >> 16)]
                line = 2 * sender + core

                def some(n):
                    first = query * k_count
                    base = ((sender * pairs + first) << (8 + bits)) + ((packed & 255) << bits)
                    for k in range(k_count):
                        vid = ids_ref[line, first + k] - begin
                        list_ref[n] = base + (k << (8 + bits)) + (vid & ((1 << bits) - 1))
                        n = n + ((vid >> bits) == 0).astype(jnp.int32)
                    return n

                return lax.cond(any_ref[line, query] > 0, some, lambda n: n, n)
            at = lax.fori_loop(bounds[p][b], bounds[p][b + 1], one_of, at)
            list_ref[b] = at - buffers
        for i in range(GROUP):
            list_ref[at + i] = 0


def chip_bits(idx_dev):
    bits = (2 * idx_dev - 1).bit_length()
    assert 2 * idx_dev == 1 << bits
    return bits


def pair_lists(who, ids, chip, queries, bounds, caps, k_count, idx_dev):
    smem = pl.BlockSpec(memory_space=pltpu.SMEM)
    sizes = [len(b) - 1 + cap + GROUP for b, cap in zip(bounds, caps)]
    found = (ids // (2 * idx_dev) == chip).astype(jnp.int32)
    found = jnp.sum(found.reshape(ids.shape[0], -1, k_count), axis=2)
    return pl.pallas_call(
        functools.partial(list_kernel, idx_dev, k_count, ids.shape[1], bounds),
        out_shape=[jax.ShapeDtypeStruct((n,), jnp.int32) for n in sizes],
        in_specs=[smem] * 4,
        out_specs=[smem] * len(sizes),
        cost_estimate=pl.CostEstimate(flops=10**7, bytes_accessed=10**6, transcendentals=0),
        name="pair_lists",
    )(who, ids, found, queries)


def pair_kernel(frames, idx_dev, buffers, scale, list_ref, one_ref, two_ref, three_ref, before_ref,
                v_hbm, *rest):
    q_hbm, rest = rest[:buffers], rest[buffers:]
    out_ref, q_in, v_in, q_rows, v_rows, maps, scores, q_sem, v_sem = rest
    width = v_hbm.shape[2] // R
    side = GROUP * frames
    senders, pairs = out_ref.shape
    bits = chip_bits(idx_dev)
    assert senders * pairs <= 1 << (23 - bits)
    count = list_ref[buffers - 1]
    groups = (count + GROUP - 1) // GROUP

    def fetch(step, slot):
        first = step * GROUP
        for b in range(buffers):
            low = 0 if b == 0 else jnp.clip(list_ref[b - 1] - first, 0, GROUP)
            high = GROUP if b == buffers - 1 else jnp.clip(list_ref[b] - first, 0, GROUP)

            def one_query(p, _):
                pltpu.make_async_copy(
                    q_hbm[b].at[(list_ref[buffers + first + p] >> bits) & 255], q_in.at[slot, p],
                    q_sem.at[slot],
                ).start()
                return 0
            lax.fori_loop(low, high, one_query, 0)

        def one_video(p, _):
            vid = list_ref[buffers + first + p] & ((1 << bits) - 1)
            pltpu.make_async_copy(v_hbm.at[vid], v_in.at[slot, p], v_sem.at[slot]).start()
            return 0
        lax.fori_loop(0, GROUP, one_video, 0)

    maps[...] = jnp.zeros_like(maps)

    @pl.when(groups > 0)
    def _():
        fetch(0, 0)

    def step(g, _):
        slot = lax.rem(g, 2)

        @pl.when(g + 1 < groups)
        def _():
            fetch(g + 1, 1 - slot)

        pltpu.make_async_copy(q_in.at[slot], q_in.at[slot], q_sem.at[slot]).wait()
        pltpu.make_async_copy(v_in.at[slot], v_in.at[slot], v_sem.at[slot]).wait()
        for r in range(R):
            cols = pl.ds(r * width, width)
            q_rows[pl.ds(r * side, side), :] = q_in[slot, :, :, cols].reshape(side, width)
            v_rows[pl.ds(r * side, side), :] = v_in[slot, :, :, cols].reshape(side, width)

        sim = lax.dot_general(
            q_rows[...], v_rows[...], (((1,), (1,)), ((), ())), preferred_element_type=jnp.float32
        )
        best = sim[:, :side]
        for s in range(1, R):
            best = jnp.maximum(best, sim[:, s * side:(s + 1) * side])
        total = best[:side]
        for r in range(1, R):
            total = total + best[r * side:(r + 1) * side]
        cells = frames * frames
        same_pair = iota((side, side), 0) // frames == iota((side, side), 1) // frames
        lane, sub = iota((side, cells), 1), iota((side, cells), 0)
        spread = (lane % frames == sub % frames).astype(jnp.bfloat16)
        own_frame = lane // frames == sub % frames
        fold = (iota((GROUP, side), 1) // frames == iota((GROUP, side), 0)).astype(jnp.bfloat16)
        mean = jnp.where(same_pair, total * scale, 0.0).astype(jnp.bfloat16)
        wide = jnp.where(own_frame, dot(mean, spread), 0.0).astype(jnp.bfloat16)
        maps[pl.ds(pl.multiple_of(g * GROUP, GROUP), GROUP), :] = dot(fold, wide)
        return 0

    lax.fori_loop(0, groups, step, 0)

    def pooled(x):
        n = x.shape[1] // 4
        best = x[:, :n]
        for i in range(1, 4):
            best = jnp.maximum(best, x[:, i * n:(i + 1) * n])
        return jnp.maximum(best, 0.0).astype(jnp.bfloat16)

    def head(g, _):
        here = pl.ds(pl.multiple_of(g * HEAD, HEAD), HEAD)
        first = pooled(dot(maps[here, :].astype(jnp.bfloat16), one_ref[...]))
        second = pooled(dot(first, two_ref[...]))
        final = jnp.clip(dot(second, three_ref[...]), -1.0, 1.0)
        best = jnp.maximum(final[:, :128], final[:, 128:])
        scores[here, :] = jnp.broadcast_to((best[:, 0:1] + best[:, 1:2]) * 0.5, (HEAD, pairs))
        return 0

    lax.fori_loop(0, (count + HEAD - 1) // HEAD, head, 0)

    out_ref[...] = before_ref[...]

    def write(i, _):
        entry = list_ref[buffers + i] >> (8 + bits)
        at = pl.ds(lax.div(entry, pairs), 1)
        hit = iota((1, pairs), 1) == lax.rem(entry, pairs)
        out_ref[at, :] = jnp.where(hit, scores[pl.ds(i, 1), :], out_ref[at, :])
        return 0

    lax.fori_loop(0, count, write, 0)


def pair_scores(blocks, videos, pair_list, cap, heads, before, idx_dev, name):
    frames, width = videos.shape[1], videos.shape[2]
    pairs = before.shape[1]
    side = GROUP * frames
    scale = 1.0 / (math.sqrt(width // R) * R)
    smem = pl.BlockSpec(memory_space=pltpu.SMEM)
    vmem = pl.BlockSpec(memory_space=pltpu.VMEM)
    hbm = pl.BlockSpec(memory_space=pltpu.HBM)
    return pl.pallas_call(
        functools.partial(pair_kernel, frames, idx_dev, len(blocks), scale),
        out_shape=jax.ShapeDtypeStruct(before.shape, jnp.float32),
        in_specs=[smem] + [vmem] * 4 + [hbm] * (1 + len(blocks)),
        out_specs=vmem,
        scratch_shapes=[
            pltpu.VMEM((2, GROUP, frames, width), jnp.bfloat16),
            pltpu.VMEM((2, GROUP, frames, width), jnp.bfloat16),
            pltpu.VMEM((R * side, width // R), jnp.bfloat16),
            pltpu.VMEM((R * side, width // R), jnp.bfloat16),
            pltpu.VMEM((cap, frames * frames), jnp.float32),
            pltpu.VMEM((cap, pairs), jnp.float32),
            pltpu.SemaphoreType.DMA((2,)),
            pltpu.SemaphoreType.DMA((2,)),
        ],
        compiler_params=pltpu.CompilerParams(vmem_limit_bytes=58 * 1024 * 1024),
        cost_estimate=pl.CostEstimate(
            flops=WEIGHT * 2 * cap * side * R * R * frames * (width // R),
            bytes_accessed=cap * frames * width * 4, transcendentals=0,
        ),
        name=name,
    )(pair_list, *heads, before, videos, *blocks)


def chip_places(mesh):
    devices = list(mesh.devices.flat)[::2]
    places = [tuple(getattr(d, "coords", ()) or ()) for d in devices]
    if any(len(p) != 3 for p in places):
        return [(i, 0, 0) for i in range(len(devices))]
    return [tuple(reversed(p)) for p in places]


def ring_position(coordinate, size):
    if size <= 2:
        return coordinate
    order = list(range(1, size, 2)) + list(reversed(range(0, size, 2)))
    order = [0] + [c for c in order if c != 0]
    return order.index(coordinate)


class Gather:
    def __init__(self, sizes, steps, queries):
        self.steps = steps
        q_dev = queries.shape[0]
        depth, height, width = sizes
        b1, a1, a2, b2 = [q_dev * s // sum(SHARES) for s in SHARES]
        here = (0, 0, 0)
        self.blocks = {("a", 0): queries}
        self.cells = {("a", 0): [(here, 0, q_dev)]}
        self.arrival = {("a", 0): -1}
        self.pieces = {("deep",): [(("a", 0), b1, a1 + a2)]}

        def moved(cells, axis, k):
            out = []
            for off, q, n in cells:
                off = list(off)
                off[axis] = k
                out.append((tuple(off), q, n))
            return out

        def ring(axis, source, name, cells):
            out = []
            for k in range(1, sizes[axis]):
                target = name + (k,)
                self.cells[target] = moved(cells, axis, k)
                out.append((axis, source, target))
                source = target
            return out

        deep = ring(0, ("deep",), ("a",), [(here, b1, a1 + a2)])
        rounds = []
        planes = []
        for k in range(depth):
            lists, later = {1: [], 2: []}, {1: [], 2: []}
            for r, (p, q) in ((0, (2, 1)), (1, (1, 2))):
                own = ("half", k, r)
                if k == 0:
                    start, n = (0, b1 + a1) if r == 0 else (b1 + a1, a2 + b2)
                    first = start
                else:
                    start, n = (0, a1) if r == 0 else (a1, a2)
                    first = start + b1
                self.pieces[own] = [(("a", k), start, n)]
                self.cells[own] = [((k, 0, 0), first, n)]
                line = ring(p, own, ("a", k, r, "line"), self.cells[own])
                lists[p] += line
                found = [own] + [m[2] for m in line]
                for i, source in enumerate(list(found)):
                    turn = ring(q, source, ("a", k, r, "turn", i), self.cells[source])
                    later[q] += turn
                    found += [m[2] for m in turn]
                if k == 0:
                    planes += [(key, 0, b1) if r == 0 else (key, a2, b2) for key in found]
            both = [lists[axis] + later[axis] for axis in (2, 1)]
            for i in range(max(map(len, both))):
                rounds.append([l[i] for l in both if i < len(l)])
        self.pieces[("b", 0)] = planes
        cells = [(self.cells[key][0][0], self.cells[key][0][1] + at, n) for key, at, n in planes]
        deep += ring(0, ("b", 0), ("b",), cells)
        gap = max(1, len(rounds) // max(1, len(deep)))
        while len(rounds) < gap * len(deep):
            rounds.append([])
        for i, m in enumerate(deep):
            rounds[i * gap].append(m)
        self.per_plane = len(rounds) // depth
        self.rounds, self.gap = rounds, gap
        for i, messages in enumerate(rounds):
            for axis, _, target in messages:
                self.arrival[target] = i if axis else i + gap - 1

    def block(self, key):
        if key not in self.blocks:
            whole = [self.block(k) for k, _, _ in self.pieces[key]]
            if len(whole) > 1:
                whole = lax.optimization_barrier(whole)
            parts = [b[at:at + n] for b, (_, at, n) in zip(whole, self.pieces[key])]
            self.blocks[key] = parts[0] if len(parts) == 1 else jnp.concatenate(parts, axis=0)
        return self.blocks[key]


def body(places, sizes, queries, index_videos, candidates, conv_one, conv_two, conv_three):
    devices = lax.axis_size("shard")
    q_dev, frames, width = queries.shape
    k_count = candidates.shape[1]
    idx_dev = index_videos.shape[0]
    pairs = q_dev * k_count
    chips = devices // 2
    per_holder = max(2, (2 * pairs + devices - 1) // devices)
    me = lax.axis_index("shard")
    chip, core = me // 2, me % 2

    rings = [[tuple(ring_position(c, n) for c, n in zip(p, sizes)) for p in places]] * 2
    if sizes[1] == sizes[2]:
        rings[1] = [(z, x, y) for z, y, x in rings[0]]
    where = [{r: i for i, r in enumerate(rings[c])} for c in range(2)]

    def step_along(axis):
        out = []
        for i in range(chips):
            for c in range(2):
                to = list(rings[c][i])
                to[axis] = (to[axis] + 1) % sizes[axis]
                out.append((2 * i + c, 2 * where[c][tuple(to)] + c))
        return out

    videos = lax.all_gather(
        index_videos, "shard", axis=0, tiled=True,
        axis_index_groups=[[2 * c, 2 * c + 1] for c in range(chips)],
    )
    gather = Gather(sizes, [step_along(a) for a in range(3)], queries)
    rounds = gather.rounds

    total = len(rounds)
    ends = [gather.per_plane * (z + 1) - 1 for z in range(sizes[0] - 1)]
    ends = sorted({e for e in ends if 0 <= e < total - 2} | {total - 2, total - 1})
    phases = [[] for _ in ends]
    for key in gather.arrival:
        phases[next(i for i, e in enumerate(ends) if gather.arrival[key] <= e)].append(key)
    offsets = [(z, y, x) for z in range(sizes[0]) for y in range(sizes[1]) for x in range(sizes[2])]
    back = np.array(
        [[where[c][tuple((r - o) % n for r, o, n in zip(rings[c][i], off, sizes))] for off in offsets]
         for i in range(chips) for c in range(2)], np.int32,
    )
    who = jnp.concatenate(
        [jnp.stack([chip, core]), lax.dynamic_index_in_dim(jnp.asarray(back), me, 0, keepdims=False)]
    )

    contents, bounds, caps = [], [], []
    for keys in phases:
        found = {}
        bounds.append([len(contents)])
        for key in keys:
            row = 0
            for off, first, n in gather.cells[key]:
                found[off] = found.get(off, 0) + n
                for q in range(first, first + n):
                    contents.append((offsets.index(off) << 16) + (q << 8) + row)
                    row += 1
            bounds[-1].append(len(contents))
        cap = sum(min(n * k_count, 2 * per_holder) for n in found.values())
        caps.append(-(-cap // HEAD) * HEAD)
    contents = jnp.asarray(np.array(contents, np.int32))

    state = {}
    heads = head_matrices(conv_one, conv_two, conv_three)
    tables = [jnp.zeros((chips, pairs), jnp.float32)]

    def score():
        p = len(tables) - 1
        tables.append(pair_scores(
            [gather.block(k) for k in phases[p]], videos, state["lists"][p], caps[p], heads,
            tables[-1], idx_dev, "phase_" + str(p),
        ))

    done, deep = [], []
    for i, messages in enumerate(rounds):
        behind = list(done[i - 2]) if i >= 2 else []
        if len(tables) <= len(ends) and i >= 2:
            if i == min(ends[len(tables) - 1] + LATER, total - 1) and ends[len(tables) - 1] <= i - 2:
                score()
                behind.append(tables[-1])
        done.append([])
        for together in ([m for m in messages if m[0]], [m for m in messages if not m[0]]):
            sent = [gather.block(source) for _, source, _ in together]
            ties = list(behind)
            if together and together[0][0] and i >= WAITS and (i - WAITS) % gather.gap == 0:
                ties.append(deep[(i - 1) // gather.gap - 1])
            sent = lax.optimization_barrier((*sent, *ties))[:len(sent)] if sent else []
            for (axis, _, target), block in zip(together, sent):
                gather.blocks[target] = lax.ppermute(block, "shard", gather.steps[axis])
                (done[i] if axis else deep).append(gather.blocks[target])
        if i == 0:
            ids = lax.optimization_barrier((candidates, *done[0]))[0].reshape(1, pairs)
            state["ids"] = lax.all_to_all(
                jnp.broadcast_to(ids, (devices, pairs)), "shard", split_axis=0, concat_axis=0,
                tiled=True,
            )
        if i == min(LISTS, total - 1):
            later = lax.optimization_barrier((who, *done[i]))[0]
            state["lists"] = pair_lists(
                later, state["ids"], chip, contents, bounds, caps, k_count, idx_dev
            )
    while len(tables) <= len(ends):
        score()
    table = jnp.where(jnp.arange(2)[None, :, None] == core, tables[-1][:, None], 0.0)
    scores = lax.all_to_all(
        table.reshape(devices, pairs), "shard", split_axis=0, concat_axis=0, tiled=True
    )
    return jnp.sum(scores, axis=0).reshape(q_dev, k_count)


def solution(mesh):
    places = chip_places(mesh)
    low = [min(p[a] for p in places) for a in range(3)]
    places = [tuple(c - m for c, m in zip(p, low)) for p in places]
    sizes = [max(p[a] for p in places) + 1 for a in range(3)]
    placed = (P("shard", None, None), P("shard", None, None), P("shard", None), P(), P(), P())
    return jax.shard_map(
        functools.partial(body, places, sizes), mesh=mesh, in_specs=placed,
        out_specs=P("shard", None), check_vma=False,
    )
```

```python
import functools
import math

import jax
import jax.numpy as jnp
import numpy as np
from jax import lax
from jax.experimental import pallas as pl
from jax.experimental.pallas import tpu as pltpu
from jax.sharding import PartitionSpec as P

R = 5
GROUP = 16
SHARES = (1, 7, 6, 2)
HEAD = 64
LATER = 4
LISTS = 2
WAITS = 5
LIST_FLOPS = 10**11
WEIGHT = 8


def dot(a, b):
    return jnp.dot(a, b, preferred_element_type=jnp.float32)


def iota(shape, dim):
    return lax.broadcasted_iota(jnp.int32, shape, dim)


def head_kernel(one_w, two_w, three_w, one_ref, two_ref, three_ref, one_acc, two_acc, three_acc):
    one_acc[...] = jnp.zeros_like(one_acc)
    two_acc[...] = jnp.zeros_like(two_acc)
    three_acc[...] = jnp.zeros_like(three_acc)
    c1, c2 = two_w.shape[1], two_w.shape[2]
    b1, b2 = c1.bit_length() - 1, c2.bit_length() - 1

    def tap(t, _):
        k = lax.div(t, 3) - 1
        l = lax.rem(t, 3) - 1

        n = one_acc.shape[1]
        row, col = iota((64, n), 0), iota((64, n), 1) >> b1
        y = ((col >> 2) & 3) * 2 + ((col >> 5) & 1)
        x = (col & 3) * 2 + ((col >> 4) & 1)
        hit = ((row >> 3) == y + k) & ((row & 7) == x + l)
        spread = ((iota((c1, n), 1) & (c1 - 1)) == iota((c1, n), 0)).astype(jnp.bfloat16)
        val = dot(jnp.broadcast_to(one_w[t], (16, c1)), spread)[:1]
        one_acc[...] = jnp.where(hit, val, one_acc[...])

        n = two_acc.shape[1]
        spread = ((iota((c2, n), 1) & (c2 - 1)) == iota((c2, n), 0)).astype(jnp.bfloat16)
        val = dot(two_w[t], spread)

        def cell(ij, _):
            col = iota((c1, n), 1) >> b2
            y = ((col >> 1) & 1) * 2 + ((col >> 3) & 1)
            x = (col & 1) * 2 + ((col >> 2) & 1)
            hit = (lax.div(ij, 4) == y + k) & (lax.rem(ij, 4) == x + l)
            rows = pl.ds(pl.multiple_of(ij * c1, c1), c1)
            two_acc[rows, :] = jnp.where(hit, val, two_acc[rows, :])
            return 0
        lax.fori_loop(0, 16, cell, 0)

        m, n = three_acc.shape
        pick = ((iota((m, c2), 0) & (c2 - 1)) == iota((m, c2), 1)).astype(jnp.bfloat16)
        val = lax.dot_general(
            pick, jnp.broadcast_to(three_w[t], (128, c2)), (((1,), (1,)), ((), ())),
            preferred_element_type=jnp.float32,
        )[:, :1]
        row, col = iota((m, n), 0) >> b2, iota((m, n), 1)
        y, x = col & 127, col >> 7
        hit = ((row >> 1) == y + k) & ((row & 1) == x + l) & (y < 2)
        three_acc[...] = jnp.where(hit, val, three_acc[...])
        return 0

    lax.fori_loop(0, 9, tap, 0)
    one_ref[...] = one_acc[...].astype(jnp.bfloat16)
    two_ref[...] = two_acc[...].astype(jnp.bfloat16)
    three_ref[...] = three_acc[...].astype(jnp.bfloat16)


def head_matrices(conv_one, conv_two, conv_three):
    c1, c2 = conv_two.shape[1], conv_two.shape[0]
    one_w = conv_one.transpose(2, 3, 1, 0).reshape(9, 1, c1)
    two_w = conv_two.transpose(2, 3, 1, 0).reshape(9, c1, c2)
    three_w = conv_three.transpose(2, 3, 0, 1).reshape(9, 1, c2)
    shapes = [(64, 64 * c1), (16 * c1, 16 * c2), (4 * c2, 256)]
    vmem = pl.BlockSpec(memory_space=pltpu.VMEM)
    return pl.pallas_call(
        head_kernel,
        out_shape=[jax.ShapeDtypeStruct(s, jnp.bfloat16) for s in shapes],
        in_specs=[vmem] * 3,
        out_specs=[vmem] * 3,
        scratch_shapes=[pltpu.VMEM(s, jnp.float32) for s in shapes],
        compiler_params=pltpu.CompilerParams(vmem_limit_bytes=24 * 1024 * 1024),
        cost_estimate=pl.CostEstimate(flops=10**9, bytes_accessed=3 * 10**6, transcendentals=0),
        name="head_matrices",
    )(one_w, two_w, three_w)


def list_kernel(idx_dev, k_count, pairs, bounds, who_ref, ids_ref, queries_ref, *lists):
    chip, core = who_ref[0], who_ref[1]
    bits = chip_bits(idx_dev)
    begin = chip << bits
    for p, list_ref in enumerate(lists):
        buffers = len(bounds[p]) - 1
        at = jnp.int32(buffers)
        for b in range(buffers):
            def one_of(t, n):
                packed = queries_ref[t]
                row, first = packed & 255, ((packed >> 8) & 255) * k_count
                sender = who_ref[2 + (packed >> 16)]
                base = ((sender * pairs + first) << (8 + bits)) + (row << bits)
                line = 2 * sender + core
                for k in range(k_count):
                    vid = ids_ref[line, first + k] - begin
                    list_ref[n] = base + (k << (8 + bits)) + (vid & ((1 << bits) - 1))
                    n = n + ((vid >> bits) == 0).astype(jnp.int32)
                return n
            at = lax.fori_loop(bounds[p][b], bounds[p][b + 1], one_of, at)
            list_ref[b] = at - buffers
        for i in range(GROUP):
            list_ref[at + i] = 0


def chip_bits(idx_dev):
    bits = (2 * idx_dev - 1).bit_length()
    assert 2 * idx_dev == 1 << bits
    return bits


def pair_lists(who, ids, queries, bounds, caps, k_count, idx_dev):
    smem = pl.BlockSpec(memory_space=pltpu.SMEM)
    sizes = [len(b) - 1 + cap + GROUP for b, cap in zip(bounds, caps)]
    return pl.pallas_call(
        functools.partial(list_kernel, idx_dev, k_count, ids.shape[1], bounds),
        out_shape=[jax.ShapeDtypeStruct((n,), jnp.int32) for n in sizes],
        in_specs=[smem] * 3,
        out_specs=[smem] * len(sizes),
        cost_estimate=pl.CostEstimate(flops=LIST_FLOPS, bytes_accessed=10**6, transcendentals=0),
        name="pair_lists",
    )(who, ids, queries)


def pair_kernel(frames, idx_dev, buffers, scale, list_ref, one_ref, two_ref, three_ref, before_ref,
                v_hbm, *rest):
    q_hbm, rest = rest[:buffers], rest[buffers:]
    out_ref, q_in, v_in, q_rows, v_rows, maps, scores, q_sem, v_sem = rest
    width = v_hbm.shape[2] // R
    side = GROUP * frames
    senders, pairs = out_ref.shape
    bits = chip_bits(idx_dev)
    assert senders * pairs <= 1 << (23 - bits)
    count = list_ref[buffers - 1]
    groups = (count + GROUP - 1) // GROUP

    def fetch(step, slot):
        first = step * GROUP
        for b in range(buffers):
            low = 0 if b == 0 else jnp.clip(list_ref[b - 1] - first, 0, GROUP)
            high = GROUP if b == buffers - 1 else jnp.clip(list_ref[b] - first, 0, GROUP)

            def one_query(p, _):
                pltpu.make_async_copy(
                    q_hbm[b].at[(list_ref[buffers + first + p] >> bits) & 255], q_in.at[slot, p],
                    q_sem.at[slot],
                ).start()
                return 0
            lax.fori_loop(low, high, one_query, 0)

        def one_video(p, _):
            vid = list_ref[buffers + first + p] & ((1 << bits) - 1)
            pltpu.make_async_copy(v_hbm.at[vid], v_in.at[slot, p], v_sem.at[slot]).start()
            return 0
        lax.fori_loop(0, GROUP, one_video, 0)

    maps[...] = jnp.zeros_like(maps)

    @pl.when(groups > 0)
    def _():
        fetch(0, 0)

    def step(g, _):
        slot = lax.rem(g, 2)

        @pl.when(g + 1 < groups)
        def _():
            fetch(g + 1, 1 - slot)

        pltpu.make_async_copy(q_in.at[slot], q_in.at[slot], q_sem.at[slot]).wait()
        pltpu.make_async_copy(v_in.at[slot], v_in.at[slot], v_sem.at[slot]).wait()
        for r in range(R):
            cols = pl.ds(r * width, width)
            q_rows[pl.ds(r * side, side), :] = q_in[slot, :, :, cols].reshape(side, width)
            v_rows[pl.ds(r * side, side), :] = v_in[slot, :, :, cols].reshape(side, width)

        sim = lax.dot_general(
            q_rows[...], v_rows[...], (((1,), (1,)), ((), ())), preferred_element_type=jnp.float32
        )
        best = sim[:, :side]
        for s in range(1, R):
            best = jnp.maximum(best, sim[:, s * side:(s + 1) * side])
        total = best[:side]
        for r in range(1, R):
            total = total + best[r * side:(r + 1) * side]
        cells = frames * frames
        same_pair = iota((side, side), 0) // frames == iota((side, side), 1) // frames
        lane, sub = iota((side, cells), 1), iota((side, cells), 0)
        spread = (lane % frames == sub % frames).astype(jnp.bfloat16)
        own_frame = lane // frames == sub % frames
        fold = (iota((GROUP, side), 1) // frames == iota((GROUP, side), 0)).astype(jnp.bfloat16)
        mean = jnp.where(same_pair, total * scale, 0.0).astype(jnp.bfloat16)
        wide = jnp.where(own_frame, dot(mean, spread), 0.0).astype(jnp.bfloat16)
        maps[pl.ds(pl.multiple_of(g * GROUP, GROUP), GROUP), :] = dot(fold, wide)
        return 0

    lax.fori_loop(0, groups, step, 0)

    def pooled(x):
        n = x.shape[1] // 4
        best = x[:, :n]
        for i in range(1, 4):
            best = jnp.maximum(best, x[:, i * n:(i + 1) * n])
        return jnp.maximum(best, 0.0).astype(jnp.bfloat16)

    def head(g, _):
        here = pl.ds(pl.multiple_of(g * HEAD, HEAD), HEAD)
        first = pooled(dot(maps[here, :].astype(jnp.bfloat16), one_ref[...]))
        second = pooled(dot(first, two_ref[...]))
        final = jnp.clip(dot(second, three_ref[...]), -1.0, 1.0)
        best = jnp.maximum(final[:, :128], final[:, 128:])
        scores[here, :] = jnp.broadcast_to((best[:, 0:1] + best[:, 1:2]) * 0.5, (HEAD, pairs))
        return 0

    lax.fori_loop(0, (count + HEAD - 1) // HEAD, head, 0)

    out_ref[...] = before_ref[...]

    def write(i, _):
        entry = list_ref[buffers + i] >> (8 + bits)
        at = pl.ds(lax.div(entry, pairs), 1)
        hit = iota((1, pairs), 1) == lax.rem(entry, pairs)
        out_ref[at, :] = jnp.where(hit, scores[pl.ds(i, 1), :], out_ref[at, :])
        return 0

    lax.fori_loop(0, count, write, 0)


def pair_scores(blocks, videos, pair_list, cap, heads, before, idx_dev, name):
    frames, width = videos.shape[1], videos.shape[2]
    pairs = before.shape[1]
    side = GROUP * frames
    scale = 1.0 / (math.sqrt(width // R) * R)
    smem = pl.BlockSpec(memory_space=pltpu.SMEM)
    vmem = pl.BlockSpec(memory_space=pltpu.VMEM)
    hbm = pl.BlockSpec(memory_space=pltpu.HBM)
    return pl.pallas_call(
        functools.partial(pair_kernel, frames, idx_dev, len(blocks), scale),
        out_shape=jax.ShapeDtypeStruct(before.shape, jnp.float32),
        in_specs=[smem] + [vmem] * 4 + [hbm] * (1 + len(blocks)),
        out_specs=vmem,
        scratch_shapes=[
            pltpu.VMEM((2, GROUP, frames, width), jnp.bfloat16),
            pltpu.VMEM((2, GROUP, frames, width), jnp.bfloat16),
            pltpu.VMEM((R * side, width // R), jnp.bfloat16),
            pltpu.VMEM((R * side, width // R), jnp.bfloat16),
            pltpu.VMEM((cap, frames * frames), jnp.float32),
            pltpu.VMEM((cap, pairs), jnp.float32),
            pltpu.SemaphoreType.DMA((2,)),
            pltpu.SemaphoreType.DMA((2,)),
        ],
        compiler_params=pltpu.CompilerParams(vmem_limit_bytes=58 * 1024 * 1024),
        cost_estimate=pl.CostEstimate(
            flops=WEIGHT * 2 * cap * side * R * R * frames * (width // R),
            bytes_accessed=cap * frames * width * 4, transcendentals=0,
        ),
        name=name,
    )(pair_list, *heads, before, videos, *blocks)


def chip_places(mesh):
    devices = list(mesh.devices.flat)[::2]
    places = [tuple(getattr(d, "coords", ()) or ()) for d in devices]
    if any(len(p) != 3 for p in places):
        return [(i, 0, 0) for i in range(len(devices))]
    return [tuple(reversed(p)) for p in places]


def ring_position(coordinate, size):
    if size <= 2:
        return coordinate
    order = list(range(1, size, 2)) + list(reversed(range(0, size, 2)))
    order = [0] + [c for c in order if c != 0]
    return order.index(coordinate)


class Gather:
    def __init__(self, sizes, steps, queries):
        self.steps = steps
        q_dev = queries.shape[0]
        depth, height, width = sizes
        b1, a1, a2, b2 = [q_dev * s // sum(SHARES) for s in SHARES]
        here = (0, 0, 0)
        self.blocks = {("a", 0): queries}
        self.cells = {("a", 0): [(here, 0, q_dev)]}
        self.arrival = {("a", 0): -1}
        self.pieces = {("deep",): [(("a", 0), b1, a1 + a2)]}

        def moved(cells, axis, k):
            out = []
            for off, q, n in cells:
                off = list(off)
                off[axis] = k
                out.append((tuple(off), q, n))
            return out

        def ring(axis, source, name, cells):
            out = []
            for k in range(1, sizes[axis]):
                target = name + (k,)
                self.cells[target] = moved(cells, axis, k)
                out.append((axis, source, target))
                source = target
            return out

        deep = ring(0, ("deep",), ("a",), [(here, b1, a1 + a2)])
        rounds = []
        planes = []
        for k in range(depth):
            lists, later = {1: [], 2: []}, {1: [], 2: []}
            for r, (p, q) in ((0, (2, 1)), (1, (1, 2))):
                own = ("half", k, r)
                if k == 0:
                    start, n = (0, b1 + a1) if r == 0 else (b1 + a1, a2 + b2)
                    first = start
                else:
                    start, n = (0, a1) if r == 0 else (a1, a2)
                    first = start + b1
                self.pieces[own] = [(("a", k), start, n)]
                self.cells[own] = [((k, 0, 0), first, n)]
                line = ring(p, own, ("a", k, r, "line"), self.cells[own])
                lists[p] += line
                found = [own] + [m[2] for m in line]
                for i, source in enumerate(list(found)):
                    turn = ring(q, source, ("a", k, r, "turn", i), self.cells[source])
                    later[q] += turn
                    found += [m[2] for m in turn]
                if k == 0:
                    planes += [(key, 0, b1) if r == 0 else (key, a2, b2) for key in found]
            both = [lists[axis] + later[axis] for axis in (2, 1)]
            for i in range(max(map(len, both))):
                rounds.append([l[i] for l in both if i < len(l)])
        self.pieces[("b", 0)] = planes
        cells = [(self.cells[key][0][0], self.cells[key][0][1] + at, n) for key, at, n in planes]
        deep += ring(0, ("b", 0), ("b",), cells)
        gap = max(1, len(rounds) // max(1, len(deep)))
        while len(rounds) < gap * len(deep):
            rounds.append([])
        for i, m in enumerate(deep):
            rounds[i * gap].append(m)
        self.per_plane = len(rounds) // depth
        self.rounds, self.gap = rounds, gap
        for i, messages in enumerate(rounds):
            for axis, _, target in messages:
                self.arrival[target] = i if axis else i + gap - 1

    def block(self, key, after=()):
        if key not in self.blocks:
            whole = [self.block(k) for k, _, _ in self.pieces[key]]
            if len(whole) > 1:
                whole = lax.optimization_barrier((*whole, *after))[:len(whole)]
            parts = [b[at:at + n] for b, (_, at, n) in zip(whole, self.pieces[key])]
            self.blocks[key] = parts[0] if len(parts) == 1 else jnp.concatenate(parts, axis=0)
        return self.blocks[key]


def body(places, sizes, queries, index_videos, candidates, conv_one, conv_two, conv_three):
    devices = lax.axis_size("shard")
    q_dev, frames, width = queries.shape
    k_count = candidates.shape[1]
    idx_dev = index_videos.shape[0]
    pairs = q_dev * k_count
    chips = devices // 2
    per_holder = max(2, (2 * pairs + devices - 1) // devices)
    me = lax.axis_index("shard")
    chip, core = me // 2, me % 2

    rings = [[tuple(ring_position(c, n) for c, n in zip(p, sizes)) for p in places]] * 2
    if sizes[1] == sizes[2]:
        rings[1] = [(z, x, y) for z, y, x in rings[0]]
    where = [{r: i for i, r in enumerate(rings[c])} for c in range(2)]

    def step_along(axis):
        out = []
        for i in range(chips):
            for c in range(2):
                to = list(rings[c][i])
                to[axis] = (to[axis] + 1) % sizes[axis]
                out.append((2 * i + c, 2 * where[c][tuple(to)] + c))
        return out

    videos = lax.all_gather(
        index_videos, "shard", axis=0, tiled=True,
        axis_index_groups=[[2 * c, 2 * c + 1] for c in range(chips)],
    )
    gather = Gather(sizes, [step_along(a) for a in range(3)], queries)
    rounds = gather.rounds

    total = len(rounds)
    ends = [gather.per_plane * (z + 1) - 1 for z in range(sizes[0] - 1)]
    ends = sorted({e for e in ends if 0 <= e < total - 2} | {total - 2, total - 1})
    phases = [[] for _ in ends]
    for key in gather.arrival:
        phases[next(i for i, e in enumerate(ends) if gather.arrival[key] <= e)].append(key)
    offsets = [(z, y, x) for z in range(sizes[0]) for y in range(sizes[1]) for x in range(sizes[2])]
    back = np.array(
        [[where[c][tuple((r - o) % n for r, o, n in zip(rings[c][i], off, sizes))] for off in offsets]
         for i in range(chips) for c in range(2)], np.int32,
    )
    who = jnp.concatenate(
        [jnp.stack([chip, core]), lax.dynamic_index_in_dim(jnp.asarray(back), me, 0, keepdims=False)]
    )

    contents, bounds, caps = [], [], []
    for keys in phases:
        found = {}
        bounds.append([len(contents)])
        for key in keys:
            row = 0
            for off, first, n in gather.cells[key]:
                found[off] = found.get(off, 0) + n
                for q in range(first, first + n):
                    contents.append((offsets.index(off) << 16) + (q << 8) + row)
                    row += 1
            bounds[-1].append(len(contents))
        cap = sum(min(n * k_count, 2 * per_holder) for n in found.values())
        caps.append(-(-cap // HEAD) * HEAD)
    contents = jnp.asarray(np.array(contents, np.int32))

    state = {}
    heads = head_matrices(conv_one, conv_two, conv_three)
    tables = [jnp.zeros((chips, pairs), jnp.float32)]

    def score():
        p = len(tables) - 1
        tables.append(pair_scores(
            [gather.block(k) for k in phases[p]], videos, state["lists"][p], caps[p], heads,
            tables[-1], idx_dev, "phase_" + str(p),
        ))

    done, deep = [], []
    for i, messages in enumerate(rounds):
        behind = list(done[i - 2]) if i >= 2 else []
        if len(tables) <= len(ends) and i >= 2:
            if i == min(ends[len(tables) - 1] + LATER, total - 1) and ends[len(tables) - 1] <= i - 2:
                score()
                behind.append(tables[-1])
        done.append([])
        for together in ([m for m in messages if m[0]], [m for m in messages if not m[0]]):
            sent = [gather.block(source, behind) for _, source, _ in together]
            ties = list(behind)
            if together and together[0][0] and i >= WAITS and (i - WAITS) % gather.gap == 0:
                ties.append(deep[(i - 1) // gather.gap - 1])
            sent = lax.optimization_barrier((*sent, *ties))[:len(sent)] if sent else []
            for (axis, _, target), block in zip(together, sent):
                gather.blocks[target] = lax.ppermute(block, "shard", gather.steps[axis])
                (done[i] if axis else deep).append(gather.blocks[target])
        if i == 0:
            ids = lax.optimization_barrier((candidates, *done[0]))[0].reshape(1, pairs)
            state["ids"] = lax.all_to_all(
                jnp.broadcast_to(ids, (devices, pairs)), "shard", split_axis=0, concat_axis=0,
                tiled=True,
            )
        if i == min(LISTS, total - 1):
            later = lax.optimization_barrier((who, *done[i]))[0]
            state["lists"] = pair_lists(
                later, state["ids"], contents, bounds, caps, k_count, idx_dev
            )
    while len(tables) <= len(ends):
        score()
    table = jnp.where(jnp.arange(2)[None, :, None] == core, tables[-1][:, None], 0.0)
    scores = lax.all_to_all(
        table.reshape(devices, pairs), "shard", split_axis=0, concat_axis=0, tiled=True
    )
    return jnp.sum(scores, axis=0).reshape(q_dev, k_count)


def solution(mesh):
    places = chip_places(mesh)
    low = [min(p[a] for p in places) for a in range(3)]
    places = [tuple(c - m for c, m in zip(p, low)) for p in places]
    sizes = [max(p[a] for p in places) + 1 for a in range(3)]
    placed = (P("shard", None, None), P("shard", None, None), P("shard", None), P(), P(), P())
    return jax.shard_map(
        functools.partial(body, places, sizes), mesh=mesh, in_specs=placed,
        out_specs=P("shard", None), check_vma=False,
    )
```

```python
import functools
import math

import jax
import jax.numpy as jnp
import numpy as np
from jax import lax
from jax.experimental import pallas as pl
from jax.experimental.pallas import tpu as pltpu
from jax.sharding import PartitionSpec as P

R = 5
GROUP = 16
SHARES = (1, 7, 6, 2)
HEAD = 64
LATER = 4
LISTS = 2
WAITS = 5
LIST_FLOPS = 10**11
WEIGHT = 8


def dot(a, b):
    return jnp.dot(a, b, preferred_element_type=jnp.float32)


def iota(shape, dim):
    return lax.broadcasted_iota(jnp.int32, shape, dim)


def head_kernel(one_w, two_w, three_w, one_ref, two_ref, three_ref, one_acc, two_acc, three_acc):
    one_acc[...] = jnp.zeros_like(one_acc)
    two_acc[...] = jnp.zeros_like(two_acc)
    three_acc[...] = jnp.zeros_like(three_acc)
    c1, c2 = two_w.shape[1], two_w.shape[2]
    b1, b2 = c1.bit_length() - 1, c2.bit_length() - 1

    def tap(t, _):
        k = lax.div(t, 3) - 1
        l = lax.rem(t, 3) - 1

        n = one_acc.shape[1]
        row, col = iota((64, n), 0), iota((64, n), 1) >> b1
        y = ((col >> 2) & 3) * 2 + ((col >> 5) & 1)
        x = (col & 3) * 2 + ((col >> 4) & 1)
        hit = ((row >> 3) == y + k) & ((row & 7) == x + l)
        spread = ((iota((c1, n), 1) & (c1 - 1)) == iota((c1, n), 0)).astype(jnp.bfloat16)
        val = dot(jnp.broadcast_to(one_w[t], (16, c1)), spread)[:1]
        one_acc[...] = jnp.where(hit, val, one_acc[...])

        n = two_acc.shape[1]
        spread = ((iota((c2, n), 1) & (c2 - 1)) == iota((c2, n), 0)).astype(jnp.bfloat16)
        val = dot(two_w[t], spread)

        def cell(ij, _):
            col = iota((c1, n), 1) >> b2
            y = ((col >> 1) & 1) * 2 + ((col >> 3) & 1)
            x = (col & 1) * 2 + ((col >> 2) & 1)
            hit = (lax.div(ij, 4) == y + k) & (lax.rem(ij, 4) == x + l)
            rows = pl.ds(pl.multiple_of(ij * c1, c1), c1)
            two_acc[rows, :] = jnp.where(hit, val, two_acc[rows, :])
            return 0
        lax.fori_loop(0, 16, cell, 0)

        m, n = three_acc.shape
        pick = ((iota((m, c2), 0) & (c2 - 1)) == iota((m, c2), 1)).astype(jnp.bfloat16)
        val = lax.dot_general(
            pick, jnp.broadcast_to(three_w[t], (128, c2)), (((1,), (1,)), ((), ())),
            preferred_element_type=jnp.float32,
        )[:, :1]
        row, col = iota((m, n), 0) >> b2, iota((m, n), 1)
        y, x = col & 127, col >> 7
        hit = ((row >> 1) == y + k) & ((row & 1) == x + l) & (y < 2)
        three_acc[...] = jnp.where(hit, val, three_acc[...])
        return 0

    lax.fori_loop(0, 9, tap, 0)
    one_ref[...] = one_acc[...].astype(jnp.bfloat16)
    two_ref[...] = two_acc[...].astype(jnp.bfloat16)
    three_ref[...] = three_acc[...].astype(jnp.bfloat16)


def head_matrices(conv_one, conv_two, conv_three):
    c1, c2 = conv_two.shape[1], conv_two.shape[0]
    one_w = conv_one.transpose(2, 3, 1, 0).reshape(9, 1, c1)
    two_w = conv_two.transpose(2, 3, 1, 0).reshape(9, c1, c2)
    three_w = conv_three.transpose(2, 3, 0, 1).reshape(9, 1, c2)
    shapes = [(64, 64 * c1), (16 * c1, 16 * c2), (4 * c2, 256)]
    vmem = pl.BlockSpec(memory_space=pltpu.VMEM)
    return pl.pallas_call(
        head_kernel,
        out_shape=[jax.ShapeDtypeStruct(s, jnp.bfloat16) for s in shapes],
        in_specs=[vmem] * 3,
        out_specs=[vmem] * 3,
        scratch_shapes=[pltpu.VMEM(s, jnp.float32) for s in shapes],
        compiler_params=pltpu.CompilerParams(vmem_limit_bytes=24 * 1024 * 1024),
        cost_estimate=pl.CostEstimate(flops=10**9, bytes_accessed=3 * 10**6, transcendentals=0),
        name="head_matrices",
    )(one_w, two_w, three_w)


def list_kernel(idx_dev, k_count, pairs, bounds, who_ref, ids_ref, queries_ref, *lists):
    chip, core = who_ref[0], who_ref[1]
    bits = chip_bits(idx_dev)
    begin = chip << bits
    for p, list_ref in enumerate(lists):
        buffers = len(bounds[p]) - 1
        at = jnp.int32(buffers)
        for b in range(buffers):
            def one_of(t, n):
                packed = queries_ref[t]
                row, first = packed & 255, ((packed >> 8) & 255) * k_count
                sender = who_ref[2 + (packed >> 16)]
                base = ((sender * pairs + first) << (8 + bits)) + (row << bits)
                line = 2 * sender + core
                for k in range(k_count):
                    vid = ids_ref[line, first + k] - begin
                    list_ref[n] = base + (k << (8 + bits)) + (vid & ((1 << bits) - 1))
                    n = n + ((vid >> bits) == 0).astype(jnp.int32)
                return n
            at = lax.fori_loop(bounds[p][b], bounds[p][b + 1], one_of, at)
            list_ref[b] = at - buffers
        for i in range(GROUP):
            list_ref[at + i] = 0


def chip_bits(idx_dev):
    bits = (2 * idx_dev - 1).bit_length()
    assert 2 * idx_dev == 1 << bits
    return bits


def pair_lists(who, ids, queries, bounds, caps, k_count, idx_dev):
    smem = pl.BlockSpec(memory_space=pltpu.SMEM)
    sizes = [len(b) - 1 + cap + GROUP for b, cap in zip(bounds, caps)]
    return pl.pallas_call(
        functools.partial(list_kernel, idx_dev, k_count, ids.shape[1], bounds),
        out_shape=[jax.ShapeDtypeStruct((n,), jnp.int32) for n in sizes],
        in_specs=[smem] * 3,
        out_specs=[smem] * len(sizes),
        cost_estimate=pl.CostEstimate(flops=LIST_FLOPS, bytes_accessed=10**6, transcendentals=0),
        name="pair_lists",
    )(who, ids, queries)


def pair_kernel(frames, idx_dev, buffers, scale, list_ref, one_ref, two_ref, three_ref, before_ref,
                v_hbm, *rest):
    q_hbm, rest = rest[:buffers], rest[buffers:]
    out_ref, q_in, v_in, q_rows, v_rows, maps, scores, q_sem, v_sem = rest
    width = v_hbm.shape[2] // R
    side = GROUP * frames
    senders, pairs = out_ref.shape
    bits = chip_bits(idx_dev)
    assert senders * pairs <= 1 << (23 - bits)
    count = list_ref[buffers - 1]
    groups = (count + GROUP - 1) // GROUP

    def fetch(step, slot):
        first = step * GROUP
        for b in range(buffers):
            low = 0 if b == 0 else jnp.clip(list_ref[b - 1] - first, 0, GROUP)
            high = GROUP if b == buffers - 1 else jnp.clip(list_ref[b] - first, 0, GROUP)

            def one_query(p, _):
                pltpu.make_async_copy(
                    q_hbm[b].at[(list_ref[buffers + first + p] >> bits) & 255], q_in.at[slot, p],
                    q_sem.at[slot],
                ).start()
                return 0
            lax.fori_loop(low, high, one_query, 0)

        def one_video(p, _):
            vid = list_ref[buffers + first + p] & ((1 << bits) - 1)
            pltpu.make_async_copy(v_hbm.at[vid], v_in.at[slot, p], v_sem.at[slot]).start()
            return 0
        lax.fori_loop(0, GROUP, one_video, 0)

    maps[...] = jnp.zeros_like(maps)

    @pl.when(groups > 0)
    def _():
        fetch(0, 0)

    def step(g, _):
        slot = lax.rem(g, 2)

        @pl.when(g + 1 < groups)
        def _():
            fetch(g + 1, 1 - slot)

        pltpu.make_async_copy(q_in.at[slot], q_in.at[slot], q_sem.at[slot]).wait()
        pltpu.make_async_copy(v_in.at[slot], v_in.at[slot], v_sem.at[slot]).wait()
        for r in range(R):
            cols = pl.ds(r * width, width)
            q_rows[pl.ds(r * side, side), :] = q_in[slot, :, :, cols].reshape(side, width)
            v_rows[pl.ds(r * side, side), :] = v_in[slot, :, :, cols].reshape(side, width)

        sim = lax.dot_general(
            q_rows[...], v_rows[...], (((1,), (1,)), ((), ())), preferred_element_type=jnp.float32
        )
        best = sim[:, :side]
        for s in range(1, R):
            best = jnp.maximum(best, sim[:, s * side:(s + 1) * side])
        total = best[:side]
        for r in range(1, R):
            total = total + best[r * side:(r + 1) * side]
        cells = frames * frames
        same_pair = iota((side, side), 0) // frames == iota((side, side), 1) // frames
        lane, sub = iota((side, cells), 1), iota((side, cells), 0)
        spread = (lane % frames == sub % frames).astype(jnp.bfloat16)
        own_frame = lane // frames == sub % frames
        fold = (iota((GROUP, side), 1) // frames == iota((GROUP, side), 0)).astype(jnp.bfloat16)
        mean = jnp.where(same_pair, total * scale, 0.0).astype(jnp.bfloat16)
        wide = jnp.where(own_frame, dot(mean, spread), 0.0).astype(jnp.bfloat16)
        maps[pl.ds(pl.multiple_of(g * GROUP, GROUP), GROUP), :] = dot(fold, wide)
        return 0

    lax.fori_loop(0, groups, step, 0)

    def pooled(x):
        n = x.shape[1] // 4
        best = x[:, :n]
        for i in range(1, 4):
            best = jnp.maximum(best, x[:, i * n:(i + 1) * n])
        return jnp.maximum(best, 0.0).astype(jnp.bfloat16)

    def head(g, _):
        here = pl.ds(pl.multiple_of(g * HEAD, HEAD), HEAD)
        first = pooled(dot(maps[here, :].astype(jnp.bfloat16), one_ref[...]))
        second = pooled(dot(first, two_ref[...]))
        final = jnp.clip(dot(second, three_ref[...]), -1.0, 1.0)
        best = jnp.maximum(final[:, :128], final[:, 128:])
        scores[here, :] = jnp.broadcast_to((best[:, 0:1] + best[:, 1:2]) * 0.5, (HEAD, pairs))
        return 0

    lax.fori_loop(0, (count + HEAD - 1) // HEAD, head, 0)

    out_ref[...] = before_ref[...]

    def write(i, _):
        entry = list_ref[buffers + i] >> (8 + bits)
        at = pl.ds(lax.div(entry, pairs), 1)
        hit = iota((1, pairs), 1) == lax.rem(entry, pairs)
        out_ref[at, :] = jnp.where(hit, scores[pl.ds(i, 1), :], out_ref[at, :])
        return 0

    lax.fori_loop(0, count, write, 0)


def pair_scores(blocks, videos, pair_list, cap, heads, before, idx_dev, name):
    frames, width = videos.shape[1], videos.shape[2]
    pairs = before.shape[1]
    side = GROUP * frames
    scale = 1.0 / (math.sqrt(width // R) * R)
    smem = pl.BlockSpec(memory_space=pltpu.SMEM)
    vmem = pl.BlockSpec(memory_space=pltpu.VMEM)
    hbm = pl.BlockSpec(memory_space=pltpu.HBM)
    return pl.pallas_call(
        functools.partial(pair_kernel, frames, idx_dev, len(blocks), scale),
        out_shape=jax.ShapeDtypeStruct(before.shape, jnp.float32),
        in_specs=[smem] + [vmem] * 4 + [hbm] * (1 + len(blocks)),
        out_specs=vmem,
        scratch_shapes=[
            pltpu.VMEM((2, GROUP, frames, width), jnp.bfloat16),
            pltpu.VMEM((2, GROUP, frames, width), jnp.bfloat16),
            pltpu.VMEM((R * side, width // R), jnp.bfloat16),
            pltpu.VMEM((R * side, width // R), jnp.bfloat16),
            pltpu.VMEM((cap, frames * frames), jnp.float32),
            pltpu.VMEM((cap, pairs), jnp.float32),
            pltpu.SemaphoreType.DMA((2,)),
            pltpu.SemaphoreType.DMA((2,)),
        ],
        compiler_params=pltpu.CompilerParams(vmem_limit_bytes=58 * 1024 * 1024),
        cost_estimate=pl.CostEstimate(
            flops=WEIGHT * 2 * cap * side * R * R * frames * (width // R),
            bytes_accessed=cap * frames * width * 4, transcendentals=0,
        ),
        name=name,
    )(pair_list, *heads, before, videos, *blocks)


def chip_places(mesh):
    devices = list(mesh.devices.flat)[::2]
    places = [tuple(getattr(d, "coords", ()) or ()) for d in devices]
    if any(len(p) != 3 for p in places):
        return [(i, 0, 0) for i in range(len(devices))]
    return [tuple(reversed(p)) for p in places]


def ring_position(coordinate, size):
    if size <= 2:
        return coordinate
    order = list(range(1, size, 2)) + list(reversed(range(0, size, 2)))
    order = [0] + [c for c in order if c != 0]
    return order.index(coordinate)


class Gather:
    def __init__(self, sizes, steps, queries):
        self.steps = steps
        q_dev = queries.shape[0]
        depth, height, width = sizes
        b1, a1, a2, b2 = [q_dev * s // sum(SHARES) for s in SHARES]
        here = (0, 0, 0)
        self.blocks = {("a", 0): queries}
        self.cells = {("a", 0): [(here, 0, q_dev)]}
        self.arrival = {("a", 0): -1}
        self.pieces = {("deep",): [(("a", 0), b1, a1 + a2)]}

        def moved(cells, axis, k):
            out = []
            for off, q, n in cells:
                off = list(off)
                off[axis] = k
                out.append((tuple(off), q, n))
            return out

        def ring(axis, source, name, cells):
            out = []
            for k in range(1, sizes[axis]):
                target = name + (k,)
                self.cells[target] = moved(cells, axis, k)
                out.append((axis, source, target))
                source = target
            return out

        deep = ring(0, ("deep",), ("a",), [(here, b1, a1 + a2)])
        rounds = []
        planes = []
        for k in range(depth):
            lists, later = {1: [], 2: []}, {1: [], 2: []}
            for r, (p, q) in ((0, (2, 1)), (1, (1, 2))):
                own = ("half", k, r)
                if k == 0:
                    start, n = (0, b1 + a1) if r == 0 else (b1 + a1, a2 + b2)
                    first = start
                else:
                    start, n = (0, a1) if r == 0 else (a1, a2)
                    first = start + b1
                self.pieces[own] = [(("a", k), start, n)]
                self.cells[own] = [((k, 0, 0), first, n)]
                line = ring(p, own, ("a", k, r, "line"), self.cells[own])
                lists[p] += line
                found = [own] + [m[2] for m in line]
                for i, source in enumerate(list(found)):
                    turn = ring(q, source, ("a", k, r, "turn", i), self.cells[source])
                    later[q] += turn
                    found += [m[2] for m in turn]
                if k == 0:
                    planes += [(key, 0, b1) if r == 0 else (key, a2, b2) for key in found]
            both = [lists[axis] + later[axis] for axis in (2, 1)]
            for i in range(max(map(len, both))):
                rounds.append([l[i] for l in both if i < len(l)])
        self.pieces[("b", 0)] = planes
        cells = [(self.cells[key][0][0], self.cells[key][0][1] + at, n) for key, at, n in planes]
        deep += ring(0, ("b", 0), ("b",), cells)
        gap = max(1, len(rounds) // max(1, len(deep)))
        while len(rounds) < gap * len(deep):
            rounds.append([])
        for i, m in enumerate(deep):
            rounds[i * gap].append(m)
        self.per_plane = len(rounds) // depth
        self.rounds, self.gap = rounds, gap
        for i, messages in enumerate(rounds):
            for axis, _, target in messages:
                self.arrival[target] = i if axis else i + gap - 1

    def block(self, key, after=()):
        if key not in self.blocks:
            whole = [self.block(k) for k, _, _ in self.pieces[key]]
            whole = lax.optimization_barrier((*whole, *after))[:len(whole)]
            parts = [b[at:at + n] for b, (_, at, n) in zip(whole, self.pieces[key])]
            self.blocks[key] = parts[0] if len(parts) == 1 else jnp.concatenate(parts, axis=0)
        return self.blocks[key]


def body(places, sizes, queries, index_videos, candidates, conv_one, conv_two, conv_three):
    devices = lax.axis_size("shard")
    q_dev, frames, width = queries.shape
    k_count = candidates.shape[1]
    idx_dev = index_videos.shape[0]
    pairs = q_dev * k_count
    chips = devices // 2
    per_holder = max(2, (2 * pairs + devices - 1) // devices)
    me = lax.axis_index("shard")
    chip, core = me // 2, me % 2

    rings = [[tuple(ring_position(c, n) for c, n in zip(p, sizes)) for p in places]] * 2
    if sizes[1] == sizes[2]:
        rings[1] = [(z, x, y) for z, y, x in rings[0]]
    where = [{r: i for i, r in enumerate(rings[c])} for c in range(2)]

    def step_along(axis):
        out = []
        for i in range(chips):
            for c in range(2):
                to = list(rings[c][i])
                to[axis] = (to[axis] + 1) % sizes[axis]
                out.append((2 * i + c, 2 * where[c][tuple(to)] + c))
        return out

    videos = lax.all_gather(
        index_videos, "shard", axis=0, tiled=True,
        axis_index_groups=[[2 * c, 2 * c + 1] for c in range(chips)],
    )
    gather = Gather(sizes, [step_along(a) for a in range(3)], queries)
    rounds = gather.rounds

    total = len(rounds)
    ends = [gather.per_plane * (z + 1) - 1 for z in range(sizes[0] - 1)]
    ends = sorted({e for e in ends if 0 <= e < total - 2} | {total - 2, total - 1})
    phases = [[] for _ in ends]
    for key in gather.arrival:
        phases[next(i for i, e in enumerate(ends) if gather.arrival[key] <= e)].append(key)
    offsets = [(z, y, x) for z in range(sizes[0]) for y in range(sizes[1]) for x in range(sizes[2])]
    back = np.array(
        [[where[c][tuple((r - o) % n for r, o, n in zip(rings[c][i], off, sizes))] for off in offsets]
         for i in range(chips) for c in range(2)], np.int32,
    )
    who = jnp.concatenate(
        [jnp.stack([chip, core]), lax.dynamic_index_in_dim(jnp.asarray(back), me, 0, keepdims=False)]
    )

    contents, bounds, caps = [], [], []
    for keys in phases:
        found = {}
        bounds.append([len(contents)])
        for key in keys:
            row = 0
            for off, first, n in gather.cells[key]:
                found[off] = found.get(off, 0) + n
                for q in range(first, first + n):
                    contents.append((offsets.index(off) << 16) + (q << 8) + row)
                    row += 1
            bounds[-1].append(len(contents))
        cap = sum(min(n * k_count, 2 * per_holder) for n in found.values())
        caps.append(-(-cap // HEAD) * HEAD)
    contents = jnp.asarray(np.array(contents, np.int32))

    state = {}
    heads = head_matrices(conv_one, conv_two, conv_three)
    tables = [jnp.zeros((chips, pairs), jnp.float32)]

    def score():
        p = len(tables) - 1
        tables.append(pair_scores(
            [gather.block(k) for k in phases[p]], videos, state["lists"][p], caps[p], heads,
            tables[-1], idx_dev, "phase_" + str(p),
        ))

    done, deep = [], []
    for i, messages in enumerate(rounds):
        behind = list(done[i - 2]) if i >= 2 else []
        if len(tables) <= len(ends) and i >= 2:
            if i == min(ends[len(tables) - 1] + LATER, total - 1) and ends[len(tables) - 1] <= i - 2:
                score()
                behind.append(tables[-1])
        done.append([])
        for together in ([m for m in messages if m[0]], [m for m in messages if not m[0]]):
            sent = [gather.block(source, behind) for _, source, _ in together]
            ties = list(behind)
            if together and together[0][0] and i >= WAITS and (i - WAITS) % gather.gap == 0:
                ties.append(deep[(i - 1) // gather.gap - 1])
            sent = lax.optimization_barrier((*sent, *ties))[:len(sent)] if sent else []
            for (axis, _, target), block in zip(together, sent):
                gather.blocks[target] = lax.ppermute(block, "shard", gather.steps[axis])
                (done[i] if axis else deep).append(gather.blocks[target])
        if i == 0:
            ids = lax.optimization_barrier((candidates, *done[0]))[0].reshape(1, pairs)
            state["ids"] = lax.all_to_all(
                jnp.broadcast_to(ids, (devices, pairs)), "shard", split_axis=0, concat_axis=0,
                tiled=True,
            )
        if i == min(LISTS, total - 1):
            later = lax.optimization_barrier((who, *done[i]))[0]
            state["lists"] = pair_lists(
                later, state["ids"], contents, bounds, caps, k_count, idx_dev
            )
    while len(tables) <= len(ends):
        score()
    table = jnp.where(jnp.arange(2)[None, :, None] == core, tables[-1][:, None], 0.0)
    scores = lax.all_to_all(
        table.reshape(devices, pairs), "shard", split_axis=0, concat_axis=0, tiled=True
    )
    return jnp.sum(scores, axis=0).reshape(q_dev, k_count)


def solution(mesh):
    places = chip_places(mesh)
    low = [min(p[a] for p in places) for a in range(3)]
    places = [tuple(c - m for c, m in zip(p, low)) for p in places]
    sizes = [max(p[a] for p in places) + 1 for a in range(3)]
    placed = (P("shard", None, None), P("shard", None, None), P("shard", None), P(), P(), P())
    return jax.shard_map(
        functools.partial(body, places, sizes), mesh=mesh, in_specs=placed,
        out_specs=P("shard", None), check_vma=False,
    )
```

```python
import functools
import math

import jax
import jax.numpy as jnp
import numpy as np
from jax import lax
from jax.experimental import pallas as pl
from jax.experimental.pallas import tpu as pltpu
from jax.sharding import PartitionSpec as P

R = 5
GROUP = 16
SHARES = (1, 7, 6, 2)
HEAD = 64
LATER = 4
LISTS = 2
WAITS = 5
LIST_FLOPS = 10**11
WEIGHT = 8


def dot(a, b):
    return jnp.dot(a, b, preferred_element_type=jnp.float32)


def iota(shape, dim):
    return lax.broadcasted_iota(jnp.int32, shape, dim)


def head_kernel(one_w, two_w, three_w, one_ref, two_ref, three_ref, one_acc, two_acc, three_acc):
    one_acc[...] = jnp.zeros_like(one_acc)
    two_acc[...] = jnp.zeros_like(two_acc)
    three_acc[...] = jnp.zeros_like(three_acc)
    c1, c2 = two_w.shape[1], two_w.shape[2]
    b1, b2 = c1.bit_length() - 1, c2.bit_length() - 1

    def tap(t, _):
        k = lax.div(t, 3) - 1
        l = lax.rem(t, 3) - 1

        n = one_acc.shape[1]
        row, col = iota((64, n), 0), iota((64, n), 1) >> b1
        y = ((col >> 2) & 3) * 2 + ((col >> 5) & 1)
        x = (col & 3) * 2 + ((col >> 4) & 1)
        hit = ((row >> 3) == y + k) & ((row & 7) == x + l)
        spread = ((iota((c1, n), 1) & (c1 - 1)) == iota((c1, n), 0)).astype(jnp.bfloat16)
        val = dot(jnp.broadcast_to(one_w[t], (16, c1)), spread)[:1]
        one_acc[...] = jnp.where(hit, val, one_acc[...])

        n = two_acc.shape[1]
        spread = ((iota((c2, n), 1) & (c2 - 1)) == iota((c2, n), 0)).astype(jnp.bfloat16)
        val = dot(two_w[t], spread)

        def cell(ij, _):
            col = iota((c1, n), 1) >> b2
            y = ((col >> 1) & 1) * 2 + ((col >> 3) & 1)
            x = (col & 1) * 2 + ((col >> 2) & 1)
            hit = (lax.div(ij, 4) == y + k) & (lax.rem(ij, 4) == x + l)
            rows = pl.ds(pl.multiple_of(ij * c1, c1), c1)
            two_acc[rows, :] = jnp.where(hit, val, two_acc[rows, :])
            return 0
        lax.fori_loop(0, 16, cell, 0)

        m, n = three_acc.shape
        pick = ((iota((m, c2), 0) & (c2 - 1)) == iota((m, c2), 1)).astype(jnp.bfloat16)
        val = lax.dot_general(
            pick, jnp.broadcast_to(three_w[t], (128, c2)), (((1,), (1,)), ((), ())),
            preferred_element_type=jnp.float32,
        )[:, :1]
        row, col = iota((m, n), 0) >> b2, iota((m, n), 1)
        y, x = col & 127, col >> 7
        hit = ((row >> 1) == y + k) & ((row & 1) == x + l) & (y < 2)
        three_acc[...] = jnp.where(hit, val, three_acc[...])
        return 0

    lax.fori_loop(0, 9, tap, 0)
    one_ref[...] = one_acc[...].astype(jnp.bfloat16)
    two_ref[...] = two_acc[...].astype(jnp.bfloat16)
    three_ref[...] = three_acc[...].astype(jnp.bfloat16)


def head_matrices(conv_one, conv_two, conv_three):
    c1, c2 = conv_two.shape[1], conv_two.shape[0]
    one_w = conv_one.transpose(2, 3, 1, 0).reshape(9, 1, c1)
    two_w = conv_two.transpose(2, 3, 1, 0).reshape(9, c1, c2)
    three_w = conv_three.transpose(2, 3, 0, 1).reshape(9, 1, c2)
    shapes = [(64, 64 * c1), (16 * c1, 16 * c2), (4 * c2, 256)]
    vmem = pl.BlockSpec(memory_space=pltpu.VMEM)
    return pl.pallas_call(
        head_kernel,
        out_shape=[jax.ShapeDtypeStruct(s, jnp.bfloat16) for s in shapes],
        in_specs=[vmem] * 3,
        out_specs=[vmem] * 3,
        scratch_shapes=[pltpu.VMEM(s, jnp.float32) for s in shapes],
        compiler_params=pltpu.CompilerParams(vmem_limit_bytes=24 * 1024 * 1024),
        cost_estimate=pl.CostEstimate(flops=10**9, bytes_accessed=3 * 10**6, transcendentals=0),
        name="head_matrices",
    )(one_w, two_w, three_w)


def list_kernel(idx_dev, k_count, pairs, bounds, who_ref, ids_ref, queries_ref, *lists):
    chip, core = who_ref[0], who_ref[1]
    bits = chip_bits(idx_dev)
    begin = chip << bits
    for p, list_ref in enumerate(lists):
        buffers = len(bounds[p]) - 1
        at = jnp.int32(buffers)
        for b in range(buffers):
            def one_of(t, n):
                packed = queries_ref[t]
                row, first = packed & 255, ((packed >> 8) & 255) * k_count
                sender = who_ref[2 + (packed >> 16)]
                line = 2 * sender + core
                base = ((line * pairs + first) << (8 + bits)) + (row << bits)
                for k in range(k_count):
                    vid = ids_ref[line, first + k] - begin
                    list_ref[n] = base + (k << (8 + bits)) + (vid & ((1 << bits) - 1))
                    n = n + ((vid >> bits) == 0).astype(jnp.int32)
                return n
            at = lax.fori_loop(bounds[p][b], bounds[p][b + 1], one_of, at)
            list_ref[b] = at - buffers
        for i in range(GROUP):
            list_ref[at + i] = 0


def chip_bits(idx_dev):
    bits = (2 * idx_dev - 1).bit_length()
    assert 2 * idx_dev == 1 << bits
    return bits


def pair_lists(who, ids, queries, bounds, caps, k_count, idx_dev):
    smem = pl.BlockSpec(memory_space=pltpu.SMEM)
    sizes = [len(b) - 1 + cap + GROUP for b, cap in zip(bounds, caps)]
    return pl.pallas_call(
        functools.partial(list_kernel, idx_dev, k_count, ids.shape[1], bounds),
        out_shape=[jax.ShapeDtypeStruct((n,), jnp.int32) for n in sizes],
        in_specs=[smem] * 3,
        out_specs=[smem] * len(sizes),
        cost_estimate=pl.CostEstimate(flops=LIST_FLOPS, bytes_accessed=10**6, transcendentals=0),
        name="pair_lists",
    )(who, ids, queries)


def pair_kernel(frames, idx_dev, buffers, scale, list_ref, one_ref, two_ref, three_ref, before_ref,
                v_hbm, *rest):
    q_hbm, rest = rest[:buffers], rest[buffers:]
    out_ref, q_in, v_in, q_rows, v_rows, maps, scores, q_sem, v_sem = rest
    width = v_hbm.shape[2] // R
    side = GROUP * frames
    senders, pairs = out_ref.shape
    bits = chip_bits(idx_dev)
    assert senders * pairs <= 1 << (23 - bits)
    count = list_ref[buffers - 1]
    groups = (count + GROUP - 1) // GROUP

    def fetch(step, slot):
        first = step * GROUP
        for b in range(buffers):
            low = 0 if b == 0 else jnp.clip(list_ref[b - 1] - first, 0, GROUP)
            high = GROUP if b == buffers - 1 else jnp.clip(list_ref[b] - first, 0, GROUP)

            def one_query(p, _):
                pltpu.make_async_copy(
                    q_hbm[b].at[(list_ref[buffers + first + p] >> bits) & 255], q_in.at[slot, p],
                    q_sem.at[slot],
                ).start()
                return 0
            lax.fori_loop(low, high, one_query, 0)

        def one_video(p, _):
            vid = list_ref[buffers + first + p] & ((1 << bits) - 1)
            pltpu.make_async_copy(v_hbm.at[vid], v_in.at[slot, p], v_sem.at[slot]).start()
            return 0
        lax.fori_loop(0, GROUP, one_video, 0)

    maps[...] = jnp.zeros_like(maps)

    @pl.when(groups > 0)
    def _():
        fetch(0, 0)

    def step(g, _):
        slot = lax.rem(g, 2)

        @pl.when(g + 1 < groups)
        def _():
            fetch(g + 1, 1 - slot)

        pltpu.make_async_copy(q_in.at[slot], q_in.at[slot], q_sem.at[slot]).wait()
        pltpu.make_async_copy(v_in.at[slot], v_in.at[slot], v_sem.at[slot]).wait()
        for r in range(R):
            cols = pl.ds(r * width, width)
            q_rows[pl.ds(r * side, side), :] = q_in[slot, :, :, cols].reshape(side, width)
            v_rows[pl.ds(r * side, side), :] = v_in[slot, :, :, cols].reshape(side, width)

        sim = lax.dot_general(
            q_rows[...], v_rows[...], (((1,), (1,)), ((), ())), preferred_element_type=jnp.float32
        )
        best = sim[:, :side]
        for s in range(1, R):
            best = jnp.maximum(best, sim[:, s * side:(s + 1) * side])
        total = best[:side]
        for r in range(1, R):
            total = total + best[r * side:(r + 1) * side]
        cells = frames * frames
        same_pair = iota((side, side), 0) // frames == iota((side, side), 1) // frames
        lane, sub = iota((side, cells), 1), iota((side, cells), 0)
        spread = (lane % frames == sub % frames).astype(jnp.bfloat16)
        own_frame = lane // frames == sub % frames
        fold = (iota((GROUP, side), 1) // frames == iota((GROUP, side), 0)).astype(jnp.bfloat16)
        mean = jnp.where(same_pair, total * scale, 0.0).astype(jnp.bfloat16)
        wide = jnp.where(own_frame, dot(mean, spread), 0.0).astype(jnp.bfloat16)
        maps[pl.ds(pl.multiple_of(g * GROUP, GROUP), GROUP), :] = dot(fold, wide)
        return 0

    lax.fori_loop(0, groups, step, 0)

    def pooled(x):
        n = x.shape[1] // 4
        best = x[:, :n]
        for i in range(1, 4):
            best = jnp.maximum(best, x[:, i * n:(i + 1) * n])
        return jnp.maximum(best, 0.0).astype(jnp.bfloat16)

    def head(g, _):
        here = pl.ds(pl.multiple_of(g * HEAD, HEAD), HEAD)
        first = pooled(dot(maps[here, :].astype(jnp.bfloat16), one_ref[...]))
        second = pooled(dot(first, two_ref[...]))
        final = jnp.clip(dot(second, three_ref[...]), -1.0, 1.0)
        best = jnp.maximum(final[:, :128], final[:, 128:])
        scores[here, :] = jnp.broadcast_to((best[:, 0:1] + best[:, 1:2]) * 0.5, (HEAD, pairs))
        return 0

    lax.fori_loop(0, (count + HEAD - 1) // HEAD, head, 0)

    out_ref[...] = before_ref[...]

    def write(i, _):
        entry = list_ref[buffers + i] >> (8 + bits)
        at = pl.ds(lax.div(entry, pairs), 1)
        hit = iota((1, pairs), 1) == lax.rem(entry, pairs)
        out_ref[at, :] = jnp.where(hit, scores[pl.ds(i, 1), :], out_ref[at, :])
        return 0

    lax.fori_loop(0, count, write, 0)


def pair_scores(blocks, videos, pair_list, cap, heads, before, idx_dev, name):
    frames, width = videos.shape[1], videos.shape[2]
    pairs = before.shape[1]
    side = GROUP * frames
    scale = 1.0 / (math.sqrt(width // R) * R)
    smem = pl.BlockSpec(memory_space=pltpu.SMEM)
    vmem = pl.BlockSpec(memory_space=pltpu.VMEM)
    hbm = pl.BlockSpec(memory_space=pltpu.HBM)
    return pl.pallas_call(
        functools.partial(pair_kernel, frames, idx_dev, len(blocks), scale),
        out_shape=jax.ShapeDtypeStruct(before.shape, jnp.float32),
        in_specs=[smem] + [vmem] * 4 + [hbm] * (1 + len(blocks)),
        out_specs=vmem,
        scratch_shapes=[
            pltpu.VMEM((2, GROUP, frames, width), jnp.bfloat16),
            pltpu.VMEM((2, GROUP, frames, width), jnp.bfloat16),
            pltpu.VMEM((R * side, width // R), jnp.bfloat16),
            pltpu.VMEM((R * side, width // R), jnp.bfloat16),
            pltpu.VMEM((cap, frames * frames), jnp.float32),
            pltpu.VMEM((cap, pairs), jnp.float32),
            pltpu.SemaphoreType.DMA((2,)),
            pltpu.SemaphoreType.DMA((2,)),
        ],
        compiler_params=pltpu.CompilerParams(vmem_limit_bytes=66000000),
        cost_estimate=pl.CostEstimate(
            flops=WEIGHT * 2 * cap * side * R * R * frames * (width // R),
            bytes_accessed=cap * frames * width * 4, transcendentals=0,
        ),
        name=name,
    )(pair_list, *heads, before, videos, *blocks)


def chip_places(mesh):
    devices = list(mesh.devices.flat)[::2]
    places = [tuple(getattr(d, "coords", ()) or ()) for d in devices]
    if any(len(p) != 3 for p in places):
        return [(i, 0, 0) for i in range(len(devices))]
    return [tuple(reversed(p)) for p in places]


def ring_position(coordinate, size):
    if size <= 2:
        return coordinate
    order = list(range(1, size, 2)) + list(reversed(range(0, size, 2)))
    order = [0] + [c for c in order if c != 0]
    return order.index(coordinate)


class Gather:
    def __init__(self, sizes, steps, queries):
        self.steps = steps
        q_dev = queries.shape[0]
        depth, height, width = sizes
        b1, a1, a2, b2 = [q_dev * s // sum(SHARES) for s in SHARES]
        here = (0, 0, 0)
        self.blocks = {("a", 0): queries}
        self.cells = {("a", 0): [(here, 0, q_dev)]}
        self.arrival = {("a", 0): -1}
        self.pieces = {("deep",): [(("a", 0), b1, a1 + a2)]}

        def moved(cells, axis, k):
            out = []
            for off, q, n in cells:
                off = list(off)
                off[axis] = k
                out.append((tuple(off), q, n))
            return out

        def ring(axis, source, name, cells):
            out = []
            for k in range(1, sizes[axis]):
                target = name + (k,)
                self.cells[target] = moved(cells, axis, k)
                out.append((axis, source, target))
                source = target
            return out

        deep = ring(0, ("deep",), ("a",), [(here, b1, a1 + a2)])
        rounds = []
        planes = []
        for k in range(depth):
            lists, later = {1: [], 2: []}, {1: [], 2: []}
            for r, (p, q) in ((0, (2, 1)), (1, (1, 2))):
                own = ("half", k, r)
                if k == 0:
                    start, n = (0, b1 + a1) if r == 0 else (b1 + a1, a2 + b2)
                    first = start
                else:
                    start, n = (0, a1) if r == 0 else (a1, a2)
                    first = start + b1
                self.pieces[own] = [(("a", k), start, n)]
                self.cells[own] = [((k, 0, 0), first, n)]
                line = ring(p, own, ("a", k, r, "line"), self.cells[own])
                lists[p] += line
                found = [own] + [m[2] for m in line]
                for i, source in enumerate(list(found)):
                    turn = ring(q, source, ("a", k, r, "turn", i), self.cells[source])
                    later[q] += turn
                    found += [m[2] for m in turn]
                if k == 0:
                    planes += [(key, 0, b1) if r == 0 else (key, a2, b2) for key in found]
            both = [lists[axis] + later[axis] for axis in (2, 1)]
            for i in range(max(map(len, both))):
                rounds.append([l[i] for l in both if i < len(l)])
        self.pieces[("b", 0)] = planes
        cells = [(self.cells[key][0][0], self.cells[key][0][1] + at, n) for key, at, n in planes]
        deep += ring(0, ("b", 0), ("b",), cells)
        gap = max(1, len(rounds) // max(1, len(deep)))
        while len(rounds) < gap * len(deep):
            rounds.append([])
        for i, m in enumerate(deep):
            rounds[i * gap].append(m)
        self.per_plane = len(rounds) // depth
        self.rounds, self.gap = rounds, gap
        for i, messages in enumerate(rounds):
            for axis, _, target in messages:
                self.arrival[target] = i if axis else i + gap - 1

    def block(self, key, after=()):
        if key not in self.blocks:
            whole = [self.block(k) for k, _, _ in self.pieces[key]]
            whole = lax.optimization_barrier((*whole, *after))[:len(whole)]
            parts = [b[at:at + n] for b, (_, at, n) in zip(whole, self.pieces[key])]
            self.blocks[key] = parts[0] if len(parts) == 1 else jnp.concatenate(parts, axis=0)
        return self.blocks[key]


def body(places, sizes, queries, index_videos, candidates, conv_one, conv_two, conv_three):
    devices = lax.axis_size("shard")
    q_dev, frames, width = queries.shape
    k_count = candidates.shape[1]
    idx_dev = index_videos.shape[0]
    pairs = q_dev * k_count
    chips = devices // 2
    per_holder = max(2, (2 * pairs + devices - 1) // devices)
    me = lax.axis_index("shard")
    chip, core = me // 2, me % 2

    rings = [[tuple(ring_position(c, n) for c, n in zip(p, sizes)) for p in places]] * 2
    if sizes[1] == sizes[2]:
        rings[1] = [(z, x, y) for z, y, x in rings[0]]
    where = [{r: i for i, r in enumerate(rings[c])} for c in range(2)]

    def step_along(axis):
        out = []
        for i in range(chips):
            for c in range(2):
                to = list(rings[c][i])
                to[axis] = (to[axis] + 1) % sizes[axis]
                out.append((2 * i + c, 2 * where[c][tuple(to)] + c))
        return out

    videos = lax.all_gather(
        index_videos, "shard", axis=0, tiled=True,
        axis_index_groups=[[2 * c, 2 * c + 1] for c in range(chips)],
    )
    gather = Gather(sizes, [step_along(a) for a in range(3)], queries)
    rounds = gather.rounds

    total = len(rounds)
    ends = [gather.per_plane * (z + 1) - 1 for z in range(sizes[0] - 1)]
    ends = sorted({e for e in ends if 0 <= e < total - 2} | {total - 2, total - 1})
    phases = [[] for _ in ends]
    for key in gather.arrival:
        phases[next(i for i, e in enumerate(ends) if gather.arrival[key] <= e)].append(key)
    offsets = [(z, y, x) for z in range(sizes[0]) for y in range(sizes[1]) for x in range(sizes[2])]
    back = np.array(
        [[where[c][tuple((r - o) % n for r, o, n in zip(rings[c][i], off, sizes))] for off in offsets]
         for i in range(chips) for c in range(2)], np.int32,
    )
    who = jnp.concatenate(
        [jnp.stack([chip, core]), lax.dynamic_index_in_dim(jnp.asarray(back), me, 0, keepdims=False)]
    )

    contents, bounds, caps = [], [], []
    for keys in phases:
        found = {}
        bounds.append([len(contents)])
        for key in keys:
            row = 0
            for off, first, n in gather.cells[key]:
                found[off] = found.get(off, 0) + n
                for q in range(first, first + n):
                    contents.append((offsets.index(off) << 16) + (q << 8) + row)
                    row += 1
            bounds[-1].append(len(contents))
        cap = sum(min(n * k_count, 2 * per_holder) for n in found.values())
        caps.append(-(-cap // HEAD) * HEAD)
    contents = jnp.asarray(np.array(contents, np.int32))

    state = {}
    heads = head_matrices(conv_one, conv_two, conv_three)
    tables = [jnp.zeros((devices, pairs), jnp.float32)]

    def score():
        p = len(tables) - 1
        tables.append(pair_scores(
            [gather.block(k) for k in phases[p]], videos, state["lists"][p], caps[p], heads,
            tables[-1], idx_dev, "phase_" + str(p),
        ))

    done, deep = [], []
    for i, messages in enumerate(rounds):
        behind = list(done[i - 2]) if i >= 2 else []
        if len(tables) <= len(ends) and i >= 2:
            if i == min(ends[len(tables) - 1] + LATER, total - 1) and ends[len(tables) - 1] <= i - 2:
                score()
                behind.append(tables[-1])
        done.append([])
        for together in ([m for m in messages if m[0]], [m for m in messages if not m[0]]):
            sent = [gather.block(source, behind) for _, source, _ in together]
            ties = list(behind)
            if together and together[0][0] and i >= WAITS and (i - WAITS) % gather.gap == 0:
                ties.append(deep[(i - 1) // gather.gap - 1])
            sent = lax.optimization_barrier((*sent, *ties))[:len(sent)] if sent else []
            for (axis, _, target), block in zip(together, sent):
                gather.blocks[target] = lax.ppermute(block, "shard", gather.steps[axis])
                (done[i] if axis else deep).append(gather.blocks[target])
        if i == 0:
            ids = lax.optimization_barrier((candidates, *done[0]))[0].reshape(1, pairs)
            state["ids"] = lax.all_to_all(
                jnp.broadcast_to(ids, (devices, pairs)), "shard", split_axis=0, concat_axis=0,
                tiled=True,
            )
        if i == min(LISTS, total - 1):
            later = lax.optimization_barrier((who, *done[i]))[0]
            state["lists"] = pair_lists(
                later, state["ids"], contents, bounds, caps, k_count, idx_dev
            )
    while len(tables) <= len(ends):
        score()
    scores = lax.all_to_all(tables[-1], "shard", split_axis=0, concat_axis=0, tiled=True)
    return jnp.sum(scores, axis=0).reshape(q_dev, k_count)


def solution(mesh):
    places = chip_places(mesh)
    low = [min(p[a] for p in places) for a in range(3)]
    places = [tuple(c - m for c, m in zip(p, low)) for p in places]
    sizes = [max(p[a] for p in places) + 1 for a in range(3)]
    placed = (P("shard", None, None), P("shard", None, None), P("shard", None), P(), P(), P())
    return jax.shard_map(
        functools.partial(body, places, sizes), mesh=mesh, in_specs=placed,
        out_specs=P("shard", None), check_vma=False,
    )
```

```python
import functools
import math

import jax
import jax.numpy as jnp
import numpy as np
from jax import lax
from jax.experimental import pallas as pl
from jax.experimental.pallas import tpu as pltpu
from jax.sharding import PartitionSpec as P

R = 5
GROUP = 16
SHARES = (1, 7, 6, 2)
HEAD = 64
LATER = 4
LISTS = 2
WAITS = 5
LIST_FLOPS = 10**11
WEIGHT = 8


def dot(a, b):
    return jnp.dot(a, b, preferred_element_type=jnp.float32)


def iota(shape, dim):
    return lax.broadcasted_iota(jnp.int32, shape, dim)


def head_kernel(one_w, two_w, three_w, one_ref, two_ref, three_ref, one_acc, two_acc, three_acc):
    one_acc[...] = jnp.zeros_like(one_acc)
    two_acc[...] = jnp.zeros_like(two_acc)
    three_acc[...] = jnp.zeros_like(three_acc)
    c1, c2 = two_w.shape[1], two_w.shape[2]
    b1, b2 = c1.bit_length() - 1, c2.bit_length() - 1

    def tap(t, _):
        k = lax.div(t, 3) - 1
        l = lax.rem(t, 3) - 1

        n = one_acc.shape[1]
        row, col = iota((64, n), 0), iota((64, n), 1) >> b1
        y = ((col >> 2) & 3) * 2 + ((col >> 5) & 1)
        x = (col & 3) * 2 + ((col >> 4) & 1)
        hit = ((row >> 3) == y + k) & ((row & 7) == x + l)
        spread = ((iota((c1, n), 1) & (c1 - 1)) == iota((c1, n), 0)).astype(jnp.bfloat16)
        val = dot(jnp.broadcast_to(one_w[t], (16, c1)), spread)[:1]
        one_acc[...] = jnp.where(hit, val, one_acc[...])

        n = two_acc.shape[1]
        spread = ((iota((c2, n), 1) & (c2 - 1)) == iota((c2, n), 0)).astype(jnp.bfloat16)
        val = dot(two_w[t], spread)

        def cell(ij, _):
            col = iota((c1, n), 1) >> b2
            y = ((col >> 1) & 1) * 2 + ((col >> 3) & 1)
            x = (col & 1) * 2 + ((col >> 2) & 1)
            hit = (lax.div(ij, 4) == y + k) & (lax.rem(ij, 4) == x + l)
            rows = pl.ds(pl.multiple_of(ij * c1, c1), c1)
            two_acc[rows, :] = jnp.where(hit, val, two_acc[rows, :])
            return 0
        lax.fori_loop(0, 16, cell, 0)

        m, n = three_acc.shape
        pick = ((iota((m, c2), 0) & (c2 - 1)) == iota((m, c2), 1)).astype(jnp.bfloat16)
        val = lax.dot_general(
            pick, jnp.broadcast_to(three_w[t], (128, c2)), (((1,), (1,)), ((), ())),
            preferred_element_type=jnp.float32,
        )[:, :1]
        row, col = iota((m, n), 0) >> b2, iota((m, n), 1)
        y, x = col & 127, col >> 7
        hit = ((row >> 1) == y + k) & ((row & 1) == x + l) & (y < 2)
        three_acc[...] = jnp.where(hit, val, three_acc[...])
        return 0

    lax.fori_loop(0, 9, tap, 0)
    one_ref[...] = one_acc[...].astype(jnp.bfloat16)
    two_ref[...] = two_acc[...].astype(jnp.bfloat16)
    three_ref[...] = three_acc[...].astype(jnp.bfloat16)


def head_matrices(conv_one, conv_two, conv_three):
    c1, c2 = conv_two.shape[1], conv_two.shape[0]
    one_w = conv_one.transpose(2, 3, 1, 0).reshape(9, 1, c1)
    two_w = conv_two.transpose(2, 3, 1, 0).reshape(9, c1, c2)
    three_w = conv_three.transpose(2, 3, 0, 1).reshape(9, 1, c2)
    shapes = [(64, 64 * c1), (16 * c1, 16 * c2), (4 * c2, 256)]
    vmem = pl.BlockSpec(memory_space=pltpu.VMEM)
    return pl.pallas_call(
        head_kernel,
        out_shape=[jax.ShapeDtypeStruct(s, jnp.bfloat16) for s in shapes],
        in_specs=[vmem] * 3,
        out_specs=[vmem] * 3,
        scratch_shapes=[pltpu.VMEM(s, jnp.float32) for s in shapes],
        compiler_params=pltpu.CompilerParams(vmem_limit_bytes=24 * 1024 * 1024),
        cost_estimate=pl.CostEstimate(flops=10**9, bytes_accessed=3 * 10**6, transcendentals=0),
        name="head_matrices",
    )(one_w, two_w, three_w)


def list_kernel(idx_dev, k_count, pairs, bounds, who_ref, ids_ref, queries_ref, *lists):
    chip, core = who_ref[0], who_ref[1]
    bits = chip_bits(idx_dev)
    begin = chip << bits
    for p, list_ref in enumerate(lists):
        buffers = len(bounds[p]) - 1
        at = jnp.int32(buffers)
        for b in range(buffers):
            def one_of(t, n):
                packed = queries_ref[t]
                row, first = packed & 255, ((packed >> 8) & 255) * k_count
                sender = who_ref[2 + (packed >> 16)]
                line = 2 * sender + core
                base = ((line * pairs + first) << (8 + bits)) + (row << bits)
                for k in range(k_count):
                    vid = ids_ref[line, first + k] - begin
                    list_ref[n] = base + (k << (8 + bits)) + (vid & ((1 << bits) - 1))
                    n = n + ((vid >> bits) == 0).astype(jnp.int32)
                return n
            at = lax.fori_loop(bounds[p][b], bounds[p][b + 1], one_of, at)
            list_ref[b] = at - buffers
        for i in range(GROUP):
            list_ref[at + i] = 0


def chip_bits(idx_dev):
    bits = (2 * idx_dev - 1).bit_length()
    assert 2 * idx_dev == 1 << bits
    return bits


def pair_lists(who, ids, queries, bounds, caps, k_count, idx_dev):
    smem = pl.BlockSpec(memory_space=pltpu.SMEM)
    sizes = [len(b) - 1 + cap + GROUP for b, cap in zip(bounds, caps)]
    return pl.pallas_call(
        functools.partial(list_kernel, idx_dev, k_count, ids.shape[1], bounds),
        out_shape=[jax.ShapeDtypeStruct((n,), jnp.int32) for n in sizes],
        in_specs=[smem] * 3,
        out_specs=[smem] * len(sizes),
        cost_estimate=pl.CostEstimate(flops=LIST_FLOPS, bytes_accessed=10**6, transcendentals=0),
        name="pair_lists",
    )(who, ids, queries)


def pair_kernel(frames, idx_dev, buffers, scale, list_ref, one_ref, two_ref, three_ref, before_ref,
                v_hbm, *rest):
    q_hbm, rest = rest[:buffers], rest[buffers:]
    out_ref, q_in, v_in, q_rows, v_rows, maps, scores, q_sem, v_sem = rest
    width = v_hbm.shape[2] // R
    side = GROUP * frames
    senders, pairs = out_ref.shape
    bits = chip_bits(idx_dev)
    assert senders * pairs <= 1 << (23 - bits)
    count = list_ref[buffers - 1]
    groups = (count + GROUP - 1) // GROUP

    def fetch(step, slot):
        first = step * GROUP
        here = jnp.minimum(count - first, GROUP)
        for b in range(buffers):
            low = 0 if b == 0 else jnp.clip(list_ref[b - 1] - first, 0, GROUP)
            high = here if b == buffers - 1 else jnp.clip(list_ref[b] - first, 0, GROUP)

            def one_query(p, _):
                pltpu.make_async_copy(
                    q_hbm[b].at[(list_ref[buffers + first + p] >> bits) & 255], q_in.at[slot, p],
                    q_sem.at[slot],
                ).start()
                return 0
            lax.fori_loop(low, high, one_query, 0)

        def one_video(p, _):
            vid = list_ref[buffers + first + p] & ((1 << bits) - 1)
            pltpu.make_async_copy(v_hbm.at[vid], v_in.at[slot, p], v_sem.at[slot]).start()
            return 0
        lax.fori_loop(0, here, one_video, 0)

    maps[...] = jnp.zeros_like(maps)

    @pl.when(groups > 0)
    def _():
        fetch(0, 0)

    def step(g, _):
        slot = lax.rem(g, 2)

        @pl.when(g + 1 < groups)
        def _():
            fetch(g + 1, 1 - slot)

        here = jnp.minimum(count - g * GROUP, GROUP)

        def arrived(p, _):
            pltpu.make_async_copy(v_hbm.at[0], q_in.at[slot, p], q_sem.at[slot]).wait()
            pltpu.make_async_copy(v_hbm.at[0], v_in.at[slot, p], v_sem.at[slot]).wait()
            return 0
        lax.fori_loop(0, here, arrived, 0)
        for r in range(R):
            cols = pl.ds(r * width, width)
            q_rows[pl.ds(r * side, side), :] = q_in[slot, :, :, cols].reshape(side, width)
            v_rows[pl.ds(r * side, side), :] = v_in[slot, :, :, cols].reshape(side, width)

        sim = lax.dot_general(
            q_rows[...], v_rows[...], (((1,), (1,)), ((), ())), preferred_element_type=jnp.float32
        )
        best = sim[:, :side]
        for s in range(1, R):
            best = jnp.maximum(best, sim[:, s * side:(s + 1) * side])
        total = best[:side]
        for r in range(1, R):
            total = total + best[r * side:(r + 1) * side]
        cells = frames * frames
        row = iota((side, side), 0) // frames
        same_pair = (row == iota((side, side), 1) // frames) & (row < here)
        lane, sub = iota((side, cells), 1), iota((side, cells), 0)
        spread = (lane % frames == sub % frames).astype(jnp.bfloat16)
        own_frame = lane // frames == sub % frames
        fold = (iota((GROUP, side), 1) // frames == iota((GROUP, side), 0)).astype(jnp.bfloat16)
        mean = jnp.where(same_pair, total * scale, 0.0).astype(jnp.bfloat16)
        wide = jnp.where(own_frame, dot(mean, spread), 0.0).astype(jnp.bfloat16)
        maps[pl.ds(pl.multiple_of(g * GROUP, GROUP), GROUP), :] = dot(fold, wide)
        return 0

    lax.fori_loop(0, groups, step, 0)

    def pooled(x):
        n = x.shape[1] // 4
        best = x[:, :n]
        for i in range(1, 4):
            best = jnp.maximum(best, x[:, i * n:(i + 1) * n])
        return jnp.maximum(best, 0.0).astype(jnp.bfloat16)

    def head(g, _):
        here = pl.ds(pl.multiple_of(g * HEAD, HEAD), HEAD)
        first = pooled(dot(maps[here, :].astype(jnp.bfloat16), one_ref[...]))
        second = pooled(dot(first, two_ref[...]))
        final = jnp.clip(dot(second, three_ref[...]), -1.0, 1.0)
        best = jnp.maximum(final[:, :128], final[:, 128:])
        scores[here, :] = jnp.broadcast_to((best[:, 0:1] + best[:, 1:2]) * 0.5, (HEAD, pairs))
        return 0

    lax.fori_loop(0, (count + HEAD - 1) // HEAD, head, 0)

    out_ref[...] = before_ref[...]

    def write(i, _):
        entry = list_ref[buffers + i] >> (8 + bits)
        at = pl.ds(lax.div(entry, pairs), 1)
        hit = iota((1, pairs), 1) == lax.rem(entry, pairs)
        out_ref[at, :] = jnp.where(hit, scores[pl.ds(i, 1), :], out_ref[at, :])
        return 0

    lax.fori_loop(0, count, write, 0)


def pair_scores(blocks, videos, pair_list, cap, heads, before, idx_dev, name):
    frames, width = videos.shape[1], videos.shape[2]
    pairs = before.shape[1]
    side = GROUP * frames
    scale = 1.0 / (math.sqrt(width // R) * R)
    smem = pl.BlockSpec(memory_space=pltpu.SMEM)
    vmem = pl.BlockSpec(memory_space=pltpu.VMEM)
    hbm = pl.BlockSpec(memory_space=pltpu.HBM)
    return pl.pallas_call(
        functools.partial(pair_kernel, frames, idx_dev, len(blocks), scale),
        out_shape=jax.ShapeDtypeStruct(before.shape, jnp.float32),
        in_specs=[smem] + [vmem] * 4 + [hbm] * (1 + len(blocks)),
        out_specs=vmem,
        scratch_shapes=[
            pltpu.VMEM((2, GROUP, frames, width), jnp.bfloat16),
            pltpu.VMEM((2, GROUP, frames, width), jnp.bfloat16),
            pltpu.VMEM((R * side, width // R), jnp.bfloat16),
            pltpu.VMEM((R * side, width // R), jnp.bfloat16),
            pltpu.VMEM((cap, frames * frames), jnp.float32),
            pltpu.VMEM((cap, pairs), jnp.float32),
            pltpu.SemaphoreType.DMA((2,)),
            pltpu.SemaphoreType.DMA((2,)),
        ],
        compiler_params=pltpu.CompilerParams(vmem_limit_bytes=66000000),
        cost_estimate=pl.CostEstimate(
            flops=WEIGHT * 2 * cap * side * R * R * frames * (width // R),
            bytes_accessed=cap * frames * width * 4, transcendentals=0,
        ),
        name=name,
    )(pair_list, *heads, before, videos, *blocks)


def chip_places(mesh):
    devices = list(mesh.devices.flat)[::2]
    places = [tuple(getattr(d, "coords", ()) or ()) for d in devices]
    if any(len(p) != 3 for p in places):
        return [(i, 0, 0) for i in range(len(devices))]
    return [tuple(reversed(p)) for p in places]


def ring_position(coordinate, size):
    if size <= 2:
        return coordinate
    order = list(range(1, size, 2)) + list(reversed(range(0, size, 2)))
    order = [0] + [c for c in order if c != 0]
    return order.index(coordinate)


class Gather:
    def __init__(self, sizes, steps, queries):
        self.steps = steps
        q_dev = queries.shape[0]
        depth, height, width = sizes
        b1, a1, a2, b2 = [q_dev * s // sum(SHARES) for s in SHARES]
        here = (0, 0, 0)
        self.blocks = {("a", 0): queries}
        self.cells = {("a", 0): [(here, 0, q_dev)]}
        self.arrival = {("a", 0): -1}
        self.pieces = {("deep",): [(("a", 0), b1, a1 + a2)]}

        def moved(cells, axis, k):
            out = []
            for off, q, n in cells:
                off = list(off)
                off[axis] = k
                out.append((tuple(off), q, n))
            return out

        def ring(axis, source, name, cells):
            out = []
            for k in range(1, sizes[axis]):
                target = name + (k,)
                self.cells[target] = moved(cells, axis, k)
                out.append((axis, source, target))
                source = target
            return out

        deep = ring(0, ("deep",), ("a",), [(here, b1, a1 + a2)])
        rounds = []
        planes = []
        for k in range(depth):
            lists, later = {1: [], 2: []}, {1: [], 2: []}
            for r, (p, q) in ((0, (2, 1)), (1, (1, 2))):
                own = ("half", k, r)
                if k == 0:
                    start, n = (0, b1 + a1) if r == 0 else (b1 + a1, a2 + b2)
                    first = start
                else:
                    start, n = (0, a1) if r == 0 else (a1, a2)
                    first = start + b1
                self.pieces[own] = [(("a", k), start, n)]
                self.cells[own] = [((k, 0, 0), first, n)]
                line = ring(p, own, ("a", k, r, "line"), self.cells[own])
                lists[p] += line
                found = [own] + [m[2] for m in line]
                for i, source in enumerate(list(found)):
                    turn = ring(q, source, ("a", k, r, "turn", i), self.cells[source])
                    later[q] += turn
                    found += [m[2] for m in turn]
                if k == 0:
                    planes += [(key, 0, b1) if r == 0 else (key, a2, b2) for key in found]
            both = [lists[axis] + later[axis] for axis in (2, 1)]
            for i in range(max(map(len, both))):
                rounds.append([l[i] for l in both if i < len(l)])
        self.pieces[("b", 0)] = planes
        cells = [(self.cells[key][0][0], self.cells[key][0][1] + at, n) for key, at, n in planes]
        deep += ring(0, ("b", 0), ("b",), cells)
        gap = max(1, len(rounds) // max(1, len(deep)))
        while len(rounds) < gap * len(deep):
            rounds.append([])
        for i, m in enumerate(deep):
            rounds[i * gap].append(m)
        self.per_plane = len(rounds) // depth
        self.rounds, self.gap = rounds, gap
        for i, messages in enumerate(rounds):
            for axis, _, target in messages:
                self.arrival[target] = i if axis else i + gap - 1

    def block(self, key, after=()):
        if key not in self.blocks:
            whole = [self.block(k) for k, _, _ in self.pieces[key]]
            whole = lax.optimization_barrier((*whole, *after))[:len(whole)]
            parts = [b[at:at + n] for b, (_, at, n) in zip(whole, self.pieces[key])]
            self.blocks[key] = parts[0] if len(parts) == 1 else jnp.concatenate(parts, axis=0)
        return self.blocks[key]


def body(places, sizes, queries, index_videos, candidates, conv_one, conv_two, conv_three):
    devices = lax.axis_size("shard")
    q_dev, frames, width = queries.shape
    k_count = candidates.shape[1]
    idx_dev = index_videos.shape[0]
    pairs = q_dev * k_count
    chips = devices // 2
    per_holder = max(2, (2 * pairs + devices - 1) // devices)
    me = lax.axis_index("shard")
    chip, core = me // 2, me % 2

    rings = [[tuple(ring_position(c, n) for c, n in zip(p, sizes)) for p in places]] * 2
    if sizes[1] == sizes[2]:
        rings[1] = [(z, x, y) for z, y, x in rings[0]]
    where = [{r: i for i, r in enumerate(rings[c])} for c in range(2)]

    def step_along(axis):
        out = []
        for i in range(chips):
            for c in range(2):
                to = list(rings[c][i])
                to[axis] = (to[axis] + 1) % sizes[axis]
                out.append((2 * i + c, 2 * where[c][tuple(to)] + c))
        return out

    videos = lax.all_gather(
        index_videos, "shard", axis=0, tiled=True,
        axis_index_groups=[[2 * c, 2 * c + 1] for c in range(chips)],
    )
    gather = Gather(sizes, [step_along(a) for a in range(3)], queries)
    rounds = gather.rounds

    total = len(rounds)
    ends = [gather.per_plane * (z + 1) - 1 for z in range(sizes[0] - 1)]
    ends = sorted({e for e in ends if 0 <= e < total - 2} | {total - 2, total - 1})
    phases = [[] for _ in ends]
    for key in gather.arrival:
        phases[next(i for i, e in enumerate(ends) if gather.arrival[key] <= e)].append(key)
    offsets = [(z, y, x) for z in range(sizes[0]) for y in range(sizes[1]) for x in range(sizes[2])]
    back = np.array(
        [[where[c][tuple((r - o) % n for r, o, n in zip(rings[c][i], off, sizes))] for off in offsets]
         for i in range(chips) for c in range(2)], np.int32,
    )
    who = jnp.concatenate(
        [jnp.stack([chip, core]), lax.dynamic_index_in_dim(jnp.asarray(back), me, 0, keepdims=False)]
    )

    contents, bounds, caps = [], [], []
    for keys in phases:
        found = {}
        bounds.append([len(contents)])
        for key in keys:
            row = 0
            for off, first, n in gather.cells[key]:
                found[off] = found.get(off, 0) + n
                for q in range(first, first + n):
                    contents.append((offsets.index(off) << 16) + (q << 8) + row)
                    row += 1
            bounds[-1].append(len(contents))
        cap = sum(min(n * k_count, 2 * per_holder) for n in found.values())
        caps.append(-(-cap // HEAD) * HEAD)
    contents = jnp.asarray(np.array(contents, np.int32))

    state = {}
    heads = head_matrices(conv_one, conv_two, conv_three)
    tables = [jnp.zeros((devices, pairs), jnp.float32)]

    def score():
        p = len(tables) - 1
        tables.append(pair_scores(
            [gather.block(k) for k in phases[p]], videos, state["lists"][p], caps[p], heads,
            tables[-1], idx_dev, "phase_" + str(p),
        ))

    done, deep = [], []
    for i, messages in enumerate(rounds):
        behind = list(done[i - 2]) if i >= 2 else []
        if len(tables) <= len(ends) and i >= 2:
            if i == min(ends[len(tables) - 1] + LATER, total - 1) and ends[len(tables) - 1] <= i - 2:
                score()
                behind.append(tables[-1])
        done.append([])
        for together in ([m for m in messages if m[0]], [m for m in messages if not m[0]]):
            sent = [gather.block(source, behind) for _, source, _ in together]
            ties = list(behind)
            if together and together[0][0] and i >= WAITS and (i - WAITS) % gather.gap == 0:
                ties.append(deep[(i - 1) // gather.gap - 1])
            sent = lax.optimization_barrier((*sent, *ties))[:len(sent)] if sent else []
            for (axis, _, target), block in zip(together, sent):
                gather.blocks[target] = lax.ppermute(block, "shard", gather.steps[axis])
                (done[i] if axis else deep).append(gather.blocks[target])
        if i == 0:
            ids = lax.optimization_barrier((candidates, *done[0]))[0].reshape(1, pairs)
            state["ids"] = lax.all_to_all(
                jnp.broadcast_to(ids, (devices, pairs)), "shard", split_axis=0, concat_axis=0,
                tiled=True,
            )
        if i == min(LISTS, total - 1):
            later = lax.optimization_barrier((who, *done[i]))[0]
            state["lists"] = pair_lists(
                later, state["ids"], contents, bounds, caps, k_count, idx_dev
            )
    while len(tables) <= len(ends):
        score()
    scores = lax.all_to_all(tables[-1], "shard", split_axis=0, concat_axis=0, tiled=True)
    return jnp.sum(scores, axis=0).reshape(q_dev, k_count)


def solution(mesh):
    places = chip_places(mesh)
    low = [min(p[a] for p in places) for a in range(3)]
    places = [tuple(c - m for c, m in zip(p, low)) for p in places]
    sizes = [max(p[a] for p in places) + 1 for a in range(3)]
    placed = (P("shard", None, None), P("shard", None, None), P("shard", None), P(), P(), P())
    return jax.shard_map(
        functools.partial(body, places, sizes), mesh=mesh, in_specs=placed,
        out_specs=P("shard", None), check_vma=False,
    )
```

```python
import functools
import math

import jax
import jax.numpy as jnp
import numpy as np
from jax import lax
from jax.experimental import pallas as pl
from jax.experimental.pallas import tpu as pltpu
from jax.sharding import PartitionSpec as P

R = 5
GROUP = 16
SHARES = (1, 7, 6, 2)
HEAD = 32
LATER = 4
LISTS = 2
WAITS = 5
LIST_FLOPS = 10**11
WEIGHT = 8


def dot(a, b):
    return jnp.dot(a, b, preferred_element_type=jnp.float32)


def iota(shape, dim):
    return lax.broadcasted_iota(jnp.int32, shape, dim)


def head_kernel(one_w, two_w, three_w, one_ref, two_ref, three_ref, one_acc, two_acc, three_acc):
    one_acc[...] = jnp.zeros_like(one_acc)
    two_acc[...] = jnp.zeros_like(two_acc)
    three_acc[...] = jnp.zeros_like(three_acc)
    c1, c2 = two_w.shape[1], two_w.shape[2]
    b1, b2 = c1.bit_length() - 1, c2.bit_length() - 1

    def tap(t, _):
        k = lax.div(t, 3) - 1
        l = lax.rem(t, 3) - 1

        n = one_acc.shape[1]
        row, col = iota((64, n), 0), iota((64, n), 1) >> b1
        y = ((col >> 2) & 3) * 2 + ((col >> 5) & 1)
        x = (col & 3) * 2 + ((col >> 4) & 1)
        hit = ((row >> 3) == y + k) & ((row & 7) == x + l)
        spread = ((iota((c1, n), 1) & (c1 - 1)) == iota((c1, n), 0)).astype(jnp.bfloat16)
        val = dot(jnp.broadcast_to(one_w[t], (16, c1)), spread)[:1]
        one_acc[...] = jnp.where(hit, val, one_acc[...])

        n = two_acc.shape[1]
        spread = ((iota((c2, n), 1) & (c2 - 1)) == iota((c2, n), 0)).astype(jnp.bfloat16)
        val = dot(two_w[t], spread)

        def cell(ij, _):
            col = iota((c1, n), 1) >> b2
            y = ((col >> 1) & 1) * 2 + ((col >> 3) & 1)
            x = (col & 1) * 2 + ((col >> 2) & 1)
            hit = (lax.div(ij, 4) == y + k) & (lax.rem(ij, 4) == x + l)
            rows = pl.ds(pl.multiple_of(ij * c1, c1), c1)
            two_acc[rows, :] = jnp.where(hit, val, two_acc[rows, :])
            return 0
        lax.fori_loop(0, 16, cell, 0)

        m, n = three_acc.shape
        pick = ((iota((m, c2), 0) & (c2 - 1)) == iota((m, c2), 1)).astype(jnp.bfloat16)
        val = lax.dot_general(
            pick, jnp.broadcast_to(three_w[t], (128, c2)), (((1,), (1,)), ((), ())),
            preferred_element_type=jnp.float32,
        )[:, :1]
        row, col = iota((m, n), 0) >> b2, iota((m, n), 1)
        y, x = col & 127, col >> 7
        hit = ((row >> 1) == y + k) & ((row & 1) == x + l) & (y < 2)
        three_acc[...] = jnp.where(hit, val, three_acc[...])
        return 0

    lax.fori_loop(0, 9, tap, 0)
    one_ref[...] = one_acc[...].astype(jnp.bfloat16)
    two_ref[...] = two_acc[...].astype(jnp.bfloat16)
    three_ref[...] = three_acc[...].astype(jnp.bfloat16)


def head_matrices(conv_one, conv_two, conv_three):
    c1, c2 = conv_two.shape[1], conv_two.shape[0]
    one_w = conv_one.transpose(2, 3, 1, 0).reshape(9, 1, c1)
    two_w = conv_two.transpose(2, 3, 1, 0).reshape(9, c1, c2)
    three_w = conv_three.transpose(2, 3, 0, 1).reshape(9, 1, c2)
    shapes = [(64, 64 * c1), (16 * c1, 16 * c2), (4 * c2, 256)]
    vmem = pl.BlockSpec(memory_space=pltpu.VMEM)
    return pl.pallas_call(
        head_kernel,
        out_shape=[jax.ShapeDtypeStruct(s, jnp.bfloat16) for s in shapes],
        in_specs=[vmem] * 3,
        out_specs=[vmem] * 3,
        scratch_shapes=[pltpu.VMEM(s, jnp.float32) for s in shapes],
        compiler_params=pltpu.CompilerParams(vmem_limit_bytes=24 * 1024 * 1024),
        cost_estimate=pl.CostEstimate(flops=10**9, bytes_accessed=3 * 10**6, transcendentals=0),
        name="head_matrices",
    )(one_w, two_w, three_w)


def list_kernel(idx_dev, k_count, pairs, bounds, who_ref, ids_ref, queries_ref, *lists):
    chip, core = who_ref[0], who_ref[1]
    bits = chip_bits(idx_dev)
    begin = chip << bits
    for p, list_ref in enumerate(lists):
        buffers = len(bounds[p]) - 1
        at = jnp.int32(buffers)
        for b in range(buffers):
            def one_of(t, n):
                packed = queries_ref[t]
                row, first = packed & 255, ((packed >> 8) & 255) * k_count
                sender = who_ref[2 + (packed >> 16)]
                line = 2 * sender + core
                base = ((line * pairs + first) << (8 + bits)) + (row << bits)
                for k in range(k_count):
                    vid = ids_ref[line, first + k] - begin
                    list_ref[n] = base + (k << (8 + bits)) + (vid & ((1 << bits) - 1))
                    n = n + ((vid >> bits) == 0).astype(jnp.int32)
                return n
            at = lax.fori_loop(bounds[p][b], bounds[p][b + 1], one_of, at)
            list_ref[b] = at - buffers
        for i in range(GROUP):
            list_ref[at + i] = 0


def chip_bits(idx_dev):
    bits = (2 * idx_dev - 1).bit_length()
    assert 2 * idx_dev == 1 << bits
    return bits


def pair_lists(who, ids, queries, bounds, caps, k_count, idx_dev):
    smem = pl.BlockSpec(memory_space=pltpu.SMEM)
    sizes = [len(b) - 1 + cap + GROUP for b, cap in zip(bounds, caps)]
    return pl.pallas_call(
        functools.partial(list_kernel, idx_dev, k_count, ids.shape[1], bounds),
        out_shape=[jax.ShapeDtypeStruct((n,), jnp.int32) for n in sizes],
        in_specs=[smem] * 3,
        out_specs=[smem] * len(sizes),
        cost_estimate=pl.CostEstimate(flops=LIST_FLOPS, bytes_accessed=10**6, transcendentals=0),
        name="pair_lists",
    )(who, ids, queries)


def pair_kernel(frames, idx_dev, buffers, scale, list_ref, one_ref, two_ref, three_ref, before_ref,
                v_hbm, *rest):
    q_hbm, rest = rest[:buffers], rest[buffers:]
    out_ref, q_in, v_in, q_rows, v_rows, maps, scores, q_sem, v_sem = rest
    width = v_hbm.shape[2] // R
    side = GROUP * frames
    senders, pairs = out_ref.shape
    bits = chip_bits(idx_dev)
    assert senders * pairs <= 1 << (23 - bits)
    count = list_ref[buffers - 1]
    groups = (count + GROUP - 1) // GROUP

    def fetch(step, slot):
        first = step * GROUP
        here = jnp.minimum(count - first, GROUP)
        for b in range(buffers):
            low = 0 if b == 0 else jnp.clip(list_ref[b - 1] - first, 0, GROUP)
            high = here if b == buffers - 1 else jnp.clip(list_ref[b] - first, 0, GROUP)

            def one_query(p, _):
                pltpu.make_async_copy(
                    q_hbm[b].at[(list_ref[buffers + first + p] >> bits) & 255], q_in.at[slot, p],
                    q_sem.at[slot],
                ).start()
                return 0
            lax.fori_loop(low, high, one_query, 0)

        def one_video(p, _):
            vid = list_ref[buffers + first + p] & ((1 << bits) - 1)
            pltpu.make_async_copy(v_hbm.at[vid], v_in.at[slot, p], v_sem.at[slot]).start()
            return 0
        lax.fori_loop(0, here, one_video, 0)

    maps[...] = jnp.zeros_like(maps)

    @pl.when(groups > 0)
    def _():
        fetch(0, 0)

    def step(g, _):
        slot = lax.rem(g, 2)

        @pl.when(g + 1 < groups)
        def _():
            fetch(g + 1, 1 - slot)

        here = jnp.minimum(count - g * GROUP, GROUP)

        def arrived(p, _):
            pltpu.make_async_copy(v_hbm.at[0], q_in.at[slot, p], q_sem.at[slot]).wait()
            pltpu.make_async_copy(v_hbm.at[0], v_in.at[slot, p], v_sem.at[slot]).wait()
            return 0
        lax.fori_loop(0, here, arrived, 0)
        for r in range(R):
            cols = pl.ds(r * width, width)
            q_rows[pl.ds(r * side, side), :] = q_in[slot, :, :, cols].reshape(side, width)
            v_rows[pl.ds(r * side, side), :] = v_in[slot, :, :, cols].reshape(side, width)

        sim = lax.dot_general(
            q_rows[...], v_rows[...], (((1,), (1,)), ((), ())), preferred_element_type=jnp.float32
        )
        best = sim[:, :side]
        for s in range(1, R):
            best = jnp.maximum(best, sim[:, s * side:(s + 1) * side])
        total = best[:side]
        for r in range(1, R):
            total = total + best[r * side:(r + 1) * side]
        cells = frames * frames
        row = iota((side, side), 0) // frames
        same_pair = (row == iota((side, side), 1) // frames) & (row < here)
        lane, sub = iota((side, cells), 1), iota((side, cells), 0)
        spread = (lane % frames == sub % frames).astype(jnp.bfloat16)
        own_frame = lane // frames == sub % frames
        fold = (iota((GROUP, side), 1) // frames == iota((GROUP, side), 0)).astype(jnp.bfloat16)
        mean = jnp.where(same_pair, total * scale, 0.0).astype(jnp.bfloat16)
        wide = jnp.where(own_frame, dot(mean, spread), 0.0).astype(jnp.bfloat16)
        maps[pl.ds(pl.multiple_of(g * GROUP, GROUP), GROUP), :] = dot(fold, wide)
        return 0

    lax.fori_loop(0, groups, step, 0)

    def pooled(x):
        n = x.shape[1] // 4
        best = x[:, :n]
        for i in range(1, 4):
            best = jnp.maximum(best, x[:, i * n:(i + 1) * n])
        return jnp.maximum(best, 0.0).astype(jnp.bfloat16)

    def head(g, _):
        here = pl.ds(pl.multiple_of(g * HEAD, HEAD), HEAD)
        first = pooled(dot(maps[here, :].astype(jnp.bfloat16), one_ref[...]))
        second = pooled(dot(first, two_ref[...]))
        final = jnp.clip(dot(second, three_ref[...]), -1.0, 1.0)
        best = jnp.maximum(final[:, :128], final[:, 128:])
        scores[here, :] = jnp.broadcast_to((best[:, 0:1] + best[:, 1:2]) * 0.5, (HEAD, pairs))
        return 0

    lax.fori_loop(0, (count + HEAD - 1) // HEAD, head, 0)

    out_ref[...] = before_ref[...]

    def write(i, _):
        entry = list_ref[buffers + i] >> (8 + bits)
        at = pl.ds(lax.div(entry, pairs), 1)
        hit = iota((1, pairs), 1) == lax.rem(entry, pairs)
        out_ref[at, :] = jnp.where(hit, scores[pl.ds(i, 1), :], out_ref[at, :])
        return 0

    lax.fori_loop(0, count, write, 0)


def pair_scores(blocks, videos, pair_list, cap, heads, before, idx_dev, name):
    frames, width = videos.shape[1], videos.shape[2]
    pairs = before.shape[1]
    side = GROUP * frames
    scale = 1.0 / (math.sqrt(width // R) * R)
    smem = pl.BlockSpec(memory_space=pltpu.SMEM)
    vmem = pl.BlockSpec(memory_space=pltpu.VMEM)
    hbm = pl.BlockSpec(memory_space=pltpu.HBM)
    return pl.pallas_call(
        functools.partial(pair_kernel, frames, idx_dev, len(blocks), scale),
        out_shape=jax.ShapeDtypeStruct(before.shape, jnp.float32),
        in_specs=[smem] + [vmem] * 4 + [hbm] * (1 + len(blocks)),
        out_specs=vmem,
        scratch_shapes=[
            pltpu.VMEM((2, GROUP, frames, width), jnp.bfloat16),
            pltpu.VMEM((2, GROUP, frames, width), jnp.bfloat16),
            pltpu.VMEM((R * side, width // R), jnp.bfloat16),
            pltpu.VMEM((R * side, width // R), jnp.bfloat16),
            pltpu.VMEM((cap, frames * frames), jnp.float32),
            pltpu.VMEM((cap, pairs), jnp.float32),
            pltpu.SemaphoreType.DMA((2,)),
            pltpu.SemaphoreType.DMA((2,)),
        ],
        compiler_params=pltpu.CompilerParams(vmem_limit_bytes=66000000),
        cost_estimate=pl.CostEstimate(
            flops=WEIGHT * 2 * cap * side * R * R * frames * (width // R),
            bytes_accessed=cap * frames * width * 4, transcendentals=0,
        ),
        name=name,
    )(pair_list, *heads, before, videos, *blocks)


def chip_places(mesh):
    devices = list(mesh.devices.flat)[::2]
    places = [tuple(getattr(d, "coords", ()) or ()) for d in devices]
    if any(len(p) != 3 for p in places):
        return [(i, 0, 0) for i in range(len(devices))]
    return [tuple(reversed(p)) for p in places]


def ring_position(coordinate, size):
    if size <= 2:
        return coordinate
    order = list(range(1, size, 2)) + list(reversed(range(0, size, 2)))
    order = [0] + [c for c in order if c != 0]
    return order.index(coordinate)


class Gather:
    def __init__(self, sizes, steps, queries):
        self.steps = steps
        q_dev = queries.shape[0]
        depth, height, width = sizes
        b1, a1, a2, b2 = [q_dev * s // sum(SHARES) for s in SHARES]
        here = (0, 0, 0)
        self.blocks = {("a", 0): queries}
        self.cells = {("a", 0): [(here, 0, q_dev)]}
        self.arrival = {("a", 0): -1}
        self.pieces = {("deep",): [(("a", 0), b1, a1 + a2)]}

        def moved(cells, axis, k):
            out = []
            for off, q, n in cells:
                off = list(off)
                off[axis] = k
                out.append((tuple(off), q, n))
            return out

        def ring(axis, source, name, cells):
            out = []
            for k in range(1, sizes[axis]):
                target = name + (k,)
                self.cells[target] = moved(cells, axis, k)
                out.append((axis, source, target))
                source = target
            return out

        deep = ring(0, ("deep",), ("a",), [(here, b1, a1 + a2)])
        rounds = []
        planes = []
        for k in range(depth):
            lists, later = {1: [], 2: []}, {1: [], 2: []}
            for r, (p, q) in ((0, (2, 1)), (1, (1, 2))):
                own = ("half", k, r)
                if k == 0:
                    start, n = (0, b1 + a1) if r == 0 else (b1 + a1, a2 + b2)
                    first = start
                else:
                    start, n = (0, a1) if r == 0 else (a1, a2)
                    first = start + b1
                self.pieces[own] = [(("a", k), start, n)]
                self.cells[own] = [((k, 0, 0), first, n)]
                line = ring(p, own, ("a", k, r, "line"), self.cells[own])
                lists[p] += line
                found = [own] + [m[2] for m in line]
                for i, source in enumerate(list(found)):
                    turn = ring(q, source, ("a", k, r, "turn", i), self.cells[source])
                    later[q] += turn
                    found += [m[2] for m in turn]
                if k == 0:
                    planes += [(key, 0, b1) if r == 0 else (key, a2, b2) for key in found]
            both = [lists[axis] + later[axis] for axis in (2, 1)]
            for i in range(max(map(len, both))):
                rounds.append([l[i] for l in both if i < len(l)])
        self.pieces[("b", 0)] = planes
        cells = [(self.cells[key][0][0], self.cells[key][0][1] + at, n) for key, at, n in planes]
        deep += ring(0, ("b", 0), ("b",), cells)
        gap = max(1, len(rounds) // max(1, len(deep)))
        while len(rounds) < gap * len(deep):
            rounds.append([])
        for i, m in enumerate(deep):
            rounds[i * gap].append(m)
        self.per_plane = len(rounds) // depth
        self.rounds, self.gap = rounds, gap
        for i, messages in enumerate(rounds):
            for axis, _, target in messages:
                self.arrival[target] = i if axis else i + gap - 1

    def block(self, key, after=()):
        if key not in self.blocks:
            whole = [self.block(k) for k, _, _ in self.pieces[key]]
            whole = lax.optimization_barrier((*whole, *after))[:len(whole)]
            parts = [b[at:at + n] for b, (_, at, n) in zip(whole, self.pieces[key])]
            self.blocks[key] = parts[0] if len(parts) == 1 else jnp.concatenate(parts, axis=0)
        return self.blocks[key]


def body(places, sizes, queries, index_videos, candidates, conv_one, conv_two, conv_three):
    devices = lax.axis_size("shard")
    q_dev, frames, width = queries.shape
    k_count = candidates.shape[1]
    idx_dev = index_videos.shape[0]
    pairs = q_dev * k_count
    chips = devices // 2
    per_holder = max(2, (2 * pairs + devices - 1) // devices)
    me = lax.axis_index("shard")
    chip, core = me // 2, me % 2

    rings = [[tuple(ring_position(c, n) for c, n in zip(p, sizes)) for p in places]] * 2
    if sizes[1] == sizes[2]:
        rings[1] = [(z, x, y) for z, y, x in rings[0]]
    where = [{r: i for i, r in enumerate(rings[c])} for c in range(2)]

    def step_along(axis):
        out = []
        for i in range(chips):
            for c in range(2):
                to = list(rings[c][i])
                to[axis] = (to[axis] + 1) % sizes[axis]
                out.append((2 * i + c, 2 * where[c][tuple(to)] + c))
        return out

    videos = lax.all_gather(
        index_videos, "shard", axis=0, tiled=True,
        axis_index_groups=[[2 * c, 2 * c + 1] for c in range(chips)],
    )
    gather = Gather(sizes, [step_along(a) for a in range(3)], queries)
    rounds = gather.rounds

    total = len(rounds)
    ends = [gather.per_plane * (z + 1) - 1 for z in range(sizes[0] - 1)]
    ends = sorted({e for e in ends if 0 <= e < total - 2} | {total - 2, total - 1})
    phases = [[] for _ in ends]
    for key in gather.arrival:
        phases[next(i for i, e in enumerate(ends) if gather.arrival[key] <= e)].append(key)
    offsets = [(z, y, x) for z in range(sizes[0]) for y in range(sizes[1]) for x in range(sizes[2])]
    back = np.array(
        [[where[c][tuple((r - o) % n for r, o, n in zip(rings[c][i], off, sizes))] for off in offsets]
         for i in range(chips) for c in range(2)], np.int32,
    )
    who = jnp.concatenate(
        [jnp.stack([chip, core]), lax.dynamic_index_in_dim(jnp.asarray(back), me, 0, keepdims=False)]
    )

    contents, bounds, caps = [], [], []
    for keys in phases:
        found = {}
        bounds.append([len(contents)])
        for key in keys:
            row = 0
            for off, first, n in gather.cells[key]:
                found[off] = found.get(off, 0) + n
                for q in range(first, first + n):
                    contents.append((offsets.index(off) << 16) + (q << 8) + row)
                    row += 1
            bounds[-1].append(len(contents))
        cap = sum(min(n * k_count, 2 * per_holder) for n in found.values())
        caps.append(-(-cap // HEAD) * HEAD)
    contents = jnp.asarray(np.array(contents, np.int32))

    state = {}
    heads = head_matrices(conv_one, conv_two, conv_three)
    tables = [jnp.zeros((devices, pairs), jnp.float32)]

    def score():
        p = len(tables) - 1
        tables.append(pair_scores(
            [gather.block(k) for k in phases[p]], videos, state["lists"][p], caps[p], heads,
            tables[-1], idx_dev, "phase_" + str(p),
        ))

    done, deep = [], []
    for i, messages in enumerate(rounds):
        behind = list(done[i - 2]) if i >= 2 else []
        if len(tables) <= len(ends) and i >= 2:
            if i == min(ends[len(tables) - 1] + LATER, total - 1) and ends[len(tables) - 1] <= i - 2:
                score()
                behind.append(tables[-1])
        done.append([])
        for together in ([m for m in messages if m[0]], [m for m in messages if not m[0]]):
            sent = [gather.block(source, behind) for _, source, _ in together]
            ties = list(behind)
            if together and together[0][0] and i >= WAITS and (i - WAITS) % gather.gap == 0:
                ties.append(deep[(i - 1) // gather.gap - 1])
            sent = lax.optimization_barrier((*sent, *ties))[:len(sent)] if sent else []
            for (axis, _, target), block in zip(together, sent):
                gather.blocks[target] = lax.ppermute(block, "shard", gather.steps[axis])
                (done[i] if axis else deep).append(gather.blocks[target])
        if i == 0:
            ids = lax.optimization_barrier((candidates, *done[0]))[0].reshape(1, pairs)
            state["ids"] = lax.all_to_all(
                jnp.broadcast_to(ids, (devices, pairs)), "shard", split_axis=0, concat_axis=0,
                tiled=True,
            )
        if i == min(LISTS, total - 1):
            later = lax.optimization_barrier((who, *done[i]))[0]
            state["lists"] = pair_lists(
                later, state["ids"], contents, bounds, caps, k_count, idx_dev
            )
    while len(tables) <= len(ends):
        score()
    scores = lax.all_to_all(tables[-1], "shard", split_axis=0, concat_axis=0, tiled=True)
    return jnp.sum(scores, axis=0).reshape(q_dev, k_count)


def solution(mesh):
    places = chip_places(mesh)
    low = [min(p[a] for p in places) for a in range(3)]
    places = [tuple(c - m for c, m in zip(p, low)) for p in places]
    sizes = [max(p[a] for p in places) + 1 for a in range(3)]
    placed = (P("shard", None, None), P("shard", None, None), P("shard", None), P(), P(), P())
    return jax.shard_map(
        functools.partial(body, places, sizes), mesh=mesh, in_specs=placed,
        out_specs=P("shard", None), check_vma=False,
    )
```
